32 devices in a mesh: parts: 2 (over y), strip: 4 (over z), col: 2 (over x), probe: 2 (over core).
Axes of the slice: x: 2, y: 2, z: 4, core: 2. Of those that a mesh axis runs over, the one named last changes fastest.
Arguments:
- signs: int32 [16, 256, 1024], P(('parts', 'probe'), 'strip', 'col'), parts along dimension 0, may hold values from -1 to 1, as said below
- onsite: float32 [512, 1024], P(('parts', 'strip'), 'col'), parts along dimension 0, may hold values from -1 to 1
- hop_right: float32 [512, 1024], P(('parts', 'strip'), 'col'), parts along dimension 0, may hold values from -1.5 to -0.5
- hop_down: float32 [512, 1024], P(('parts', 'strip'), 'col'), parts along dimension 0, may hold values from -1.5 to -0.5
- moment_weights: float32 [3], replicated, may hold values from 0.5 to 1.5
- forward_now: float32 [16, 256, 1024], P(('parts', 'probe'), 'strip', 'col'), parts along dimension 0, may hold values from -6 to 6
- forward_next: float32 [16, 256, 1024], P(('parts', 'probe'), 'strip', 'col'), parts along dimension 0, may hold values from -6 to 6
- adjoint_now: float32 [16, 256, 1024], P(('parts', 'probe'), 'strip', 'col'), parts along dimension 0, may hold values from -6 to 6
- adjoint_next: float32 [16, 256, 1024], P(('parts', 'probe'), 'strip', 'col'), parts along dimension 0, may hold values from -6 to 6
Outputs:
- right_force: float32 [512, 1024], P(('parts', 'strip'), 'col'), parts along dimension 0
- down_force: float32 [512, 1024], P(('parts', 'strip'), 'col'), parts along dimension 0
- site_force: float32 [512, 1024], P(('parts', 'strip'), 'col'), parts along dimension 0
- forward_out: float32 [16, 256, 1024], P(('parts', 'probe'), 'strip', 'col'), parts along dimension 0
- adjoint_out: float32 [16, 256, 1024], P(('parts', 'probe'), 'strip', 'col'), parts along dimension 0
The draws below stay inside these ranges and needn't reach their ends.
There are 2 independent parts, one for each index of `parts`. The reference program is written for one: setup_inputs(seed, part) draws one part's arguments, and reference() takes and returns one part's arrays. A program takes and returns all parts, laid end to end along the dimension named above; an argument that names none is the same for every part. Nothing has to cross between parts.
Inputs may be any that keep to these rules, and one draw needn't show every extreme that they name: `signs`: each entry is -1 or 1.
All inputs are finite; a program needn't handle non-finite values.
Results may differ from the reference program's by a relative error of at most 0.0001.
Values sent between devices are 32-bit elements; how exact they have to be, the bound alone decides.
No kernel may reach another device: no remote copies, remote signals or barrier semaphores. Data moves between devices by JAX's collectives and lax.ppermute only.
A program may use at most 64 MiB of HBM per device.

```python
import jax
import jax.numpy as jnp

STEPS = 3
NR = 256
NC = 1024
PROBES = 8


def draw_signs(key, part):
    key = jax.random.fold_in(key, 7)
    picks = jax.random.randint(key, (PROBES, NR, NC), 0, 2)
    return (2 * picks - 1).astype(jnp.int32)


def steps_of(key, extent, split, low, high):
    def one(axis_at, parts):
        heights = jax.random.uniform(jax.random.fold_in(jax.random.fold_in(key, 6), axis_at), (parts,), jnp.float32, low / len(split), high / len(split))
        return jnp.repeat(jnp.exp(heights), extent[axis_at] // parts).reshape((-1,) + (1,) * (len(extent) - axis_at - 1))

    factor_of = one(*split[0])
    for cut in split[1:]:
        factor_of = factor_of * one(*cut)
    return factor_of


def gaussian(own_key, shape, deviation, bound, split=(), held_as=jnp.bfloat16):
    entries = jax.random.normal(own_key, shape, jnp.float32) * deviation
    if len(split) > 0:
        entries = steps_of(own_key, shape, split, -0.22, 0.18) * entries
    return jnp.clip(entries, min=-bound, max=bound).astype(held_as)


def setup_inputs(seed: int = 0, part: int = 0) -> dict:
    key_list = jax.random.split(jax.random.key(seed), 10)
    own_keys = jax.random.split(jax.random.fold_in(key_list[9], part), 10)
    signs = draw_signs(jax.random.fold_in(jax.random.fold_in(key_list[9], part), 71), part)
    onsite = jnp.clip(jax.random.uniform(own_keys[1], (NR, NC), jnp.float32, -1.0, 1.0) * steps_of(own_keys[1], (NR, NC), ((0, 4), (1, 2)), -0.4, 0.0), -1.0, 1.0)
    hop_right = jnp.clip(-1.5 + 1.0 * jax.random.uniform(own_keys[2], (NR, NC), jnp.float32) ** steps_of(own_keys[2], (NR, NC), ((0, 4), (1, 2)), -0.2, 0.2), -1.5, -0.5)
    hop_down = jnp.clip(-1.5 + 1.0 * jax.random.uniform(own_keys[3], (NR, NC), jnp.float32) ** steps_of(own_keys[3], (NR, NC), ((0, 4), (1, 2)), -0.2, 0.2), -1.5, -0.5)
    moment_weights = jnp.clip(jax.random.uniform(key_list[4], (STEPS,), jnp.float32, 0.5, 1.5), 0.5, 1.5)
    forward_now = gaussian(own_keys[5], (PROBES, NR, NC), 1.0, 6.0, ((0, 2), (1, 4), (2, 2)), jnp.float32)
    forward_next = gaussian(own_keys[6], (PROBES, NR, NC), 1.0, 6.0, ((0, 2), (1, 4), (2, 2)), jnp.float32)
    adjoint_now = gaussian(own_keys[7], (PROBES, NR, NC), 1.0, 6.0, ((0, 2), (1, 4), (2, 2)), jnp.float32)
    adjoint_next = gaussian(own_keys[8], (PROBES, NR, NC), 1.0, 6.0, ((0, 2), (1, 4), (2, 2)), jnp.float32)
    return dict(signs=signs, onsite=onsite, hop_right=hop_right, hop_down=hop_down, moment_weights=moment_weights, forward_now=forward_now, forward_next=forward_next, adjoint_now=adjoint_now, adjoint_next=adjoint_next)


spectral_half = 7.5


def apply_scaled(field, onsite, hop_right, hop_down):
    total = onsite * field
    total = total + hop_right * jnp.roll(field, -1, axis=2)
    total = total + jnp.roll(hop_right, 1, axis=1) * jnp.roll(field, 1, axis=2)
    total = total + hop_down * jnp.roll(field, -1, axis=1)
    total = total + jnp.roll(hop_down, 1, axis=0) * jnp.roll(field, 1, axis=1)
    return total / spectral_half


def reference(signs, onsite, hop_right, hop_down, moment_weights, forward_now, forward_next, adjoint_now, adjoint_next):
    sign_field = signs.astype(jnp.float32)
    right_acc = jnp.zeros(onsite.shape, jnp.float32)
    down_acc = jnp.zeros(onsite.shape, jnp.float32)
    site_acc = jnp.zeros(onsite.shape, jnp.float32)
    current, previous = forward_now, forward_next
    adjoint, adjoint_prev = adjoint_now, adjoint_next
    for moment in range(STEPS):
        right_acc = right_acc + jnp.sum(adjoint * jnp.roll(current, -1, axis=2) + jnp.roll(adjoint, -1, axis=2) * current, axis=0)
        down_acc = down_acc + jnp.sum(adjoint * jnp.roll(current, -1, axis=1) + jnp.roll(adjoint, -1, axis=1) * current, axis=0)
        site_acc = site_acc + jnp.sum(adjoint * current, axis=0)
        adjoint_new = moment_weights[moment] * sign_field + 2.0 * apply_scaled(adjoint, onsite, hop_right, hop_down) - adjoint_prev
        current_new = 2.0 * apply_scaled(current, onsite, hop_right, hop_down) - previous
        previous, current = current, current_new
        adjoint_prev, adjoint = adjoint, adjoint_new
    factor = 2.0 / spectral_half
    return right_acc * factor, down_acc * factor, site_acc * factor, current, adjoint
```

```python
import jax
import jax.numpy as jnp
from jax import lax
from jax.experimental import pallas as pl
from jax.experimental.pallas import tpu as pltpu
from jax.sharding import PartitionSpec as P

STEPS = 3
LANES = 128
TILE = 8
spectral_half = 7.5
SCALE = 2.0 / spectral_half

WIDE = 2 * STEPS
VMEM_LIMIT = 48 * 1024 * 1024


def shifted(x, axis, by):
    size = lax.axis_size(axis)
    return lax.ppermute(x, axis, [(i, (i + by) % size) for i in range(size)])


def lane_of(shape):
    return lax.broadcasted_iota(jnp.int32, shape, len(shape) - 1)


def turned(x, by):
    return pltpu.roll(x, by % x.shape[1], 1)


def edge_kernel(weights, *refs):
    *sources, out = refs
    lows, highs = sources[0::2], sources[1::2]
    probes = lows[0].shape[0]
    span = WIDE * 2 * probes
    lane = lane_of(out.shape)

    def joined(at, probe=None):
        if probe is None:
            return jnp.where(lane < LANES // 2, lows[at][...], highs[at][...])
        return jnp.where(lane < LANES // 2, lows[at][probe], highs[at][probe])

    packed = jnp.zeros(out.shape, jnp.float32)

    def put(packed, x, start):
        return jnp.where((lane >= start) & (lane < start + WIDE), turned(x, start + STEPS), packed)

    first, last = LANES - STEPS, STEPS - 1
    for probe in range(probes):
        group = WIDE * probe
        sign = joined(4, probe).astype(jnp.float32)
        base = weights[0] * sign - joined(2, probe)
        base = jnp.where(lane == first, turned(sign, -2), jnp.where(lane == last, turned(sign, 2), base))
        packed = put(packed, joined(0, probe), group)
        packed = put(packed, base, span + group)
        group = WIDE * (probes + probe)
        base = jnp.where((lane == first) | (lane == last), 0.0, -joined(3, probe))
        packed = put(packed, joined(1, probe), group)
        packed = put(packed, base, span + group)
    for at in range(3):
        packed = put(packed, joined(5 + at), 2 * span + WIDE * at)
    out[...] = packed


def strips(own, left, right, span):
    lane = lane_of(own.shape)
    inner = lax.rem(lane, WIDE) < STEPS
    low = jnp.where(inner, left, own)
    high = jnp.where(inner, own, right)
    below = lane < span
    field = jnp.where(below, low, turned(high, span))
    base = jnp.where(below, turned(low, -span), high)
    coefficients = []
    for at in range(3):
        start = 2 * span + WIDE * at
        x = jnp.where(
            lane < WIDE,
            turned(low, -start),
            jnp.where((lane >= span) & (lane < span + WIDE), turned(high, span - start), 0.0),
        )
        reach = WIDE
        while reach < span:
            x = x + turned(x, reach)
            reach *= 2
        coefficients.append(x * SCALE)
    return field, base, coefficients


def column_of(row, groups, at):
    shape = (groups, LANES)
    wanted = WIDE * lax.broadcasted_iota(jnp.int32, shape, 0) + at
    return jnp.sum(jnp.where(lane_of(shape) == wanted, row, 0.0), axis=1, keepdims=True)


def sideways(x, hop, strip_row, hop_row, span):
    groups, cols = x.shape
    lane = lane_of(x.shape)
    before = jnp.where(lane == 0, column_of(strip_row, groups, STEPS - 1), turned(x, 1))
    after = jnp.where(lane == cols - 1, column_of(strip_row, groups, span + STEPS), turned(x, -1))
    hop = jnp.broadcast_to(hop, x.shape)
    hop_before = jnp.where(lane == 0, hop_row[:, STEPS - 1 : STEPS], turned(hop, 1))
    return hop * after + hop_before * before


def edge_rows(weights, refs, rows, out):
    adj, fwd, adj_next, fwd_next, signs, onsite, hop_right, hop_down, own, left, right = refs
    edge, second, third = rows
    probes = adj.shape[0]
    groups = 2 * probes
    span = WIDE * groups

    def pair(top, bottom, at):
        return jnp.concatenate([top[:, at, :], bottom[:, at, :]], axis=0)

    def sign_pair(weight, at):
        sign = weight * signs[:, at, :].astype(jnp.float32)
        return jnp.concatenate([sign, jnp.zeros_like(sign)], axis=0)

    def bond(at, other):
        return min(at, other)

    def scaled(ref, at):
        return ref[at : at + 1, :] * SCALE

    field, base, (s_on, s_right, s_down) = strips(own[...], left[...], right[...], span)
    x_edge, x_second, x_third = (pair(adj, fwd, at) for at in rows)
    one = (
        sign_pair(weights[0], second)
        - pair(adj_next, fwd_next, second)
        + scaled(onsite, second) * x_second
        + sideways(
            x_second,
            scaled(hop_right, second),
            field[second : second + 1, :],
            s_right[second : second + 1, :],
            span,
        )
        + scaled(hop_down, bond(edge, second)) * x_edge
        + scaled(hop_down, bond(second, third)) * x_third
    )
    part_one = (
        sign_pair(weights[0], edge)
        - pair(adj_next, fwd_next, edge)
        + scaled(onsite, edge) * x_edge
        + sideways(
            x_edge, scaled(hop_right, edge), field[edge : edge + 1, :], s_right[edge : edge + 1, :], span
        )
        + scaled(hop_down, bond(edge, second)) * x_second
    )
    part_two = sign_pair(weights[1], edge) - x_edge + scaled(hop_down, bond(edge, second)) * one
    level = (
        base
        + s_on * field
        + s_right * turned(field, -1)
        + turned(s_right, 1) * turned(field, 1)
    )
    down = bond(edge, second)
    strip_one = level[edge : edge + 1, :] + s_down[down : down + 1, :] * field[second : second + 1, :]
    strip_row = jnp.concatenate(
        [field[edge : edge + 1, :], strip_one, s_down[edge : edge + 1, :], s_right[edge : edge + 1, :]], axis=1
    )
    out[0:groups, :] = x_edge
    out[groups : 2 * groups, :] = part_one
    out[2 * groups : 3 * groups, :] = part_two
    at = 3 * groups
    out[at : at + 1, :] = scaled(onsite, edge)
    out[at + 1 : at + 2, :] = scaled(hop_right, edge)
    out[at + 2 : at + 3, :] = scaled(hop_down, edge)
    out[at + 3 : at + 4, 0 : 4 * LANES] = strip_row
    out[at + 4 : at + TILE, :] = jnp.zeros((TILE - 4, out.shape[1]), jnp.float32)


def rows_kernel(weights, *refs):
    *sources, first_out, last_out = refs
    edge_rows(weights, sources[0::2], (0, 1, 2), first_out)
    edge_rows(weights, sources[1::2], (TILE - 1, TILE - 2, TILE - 3), last_out)


def main_kernel(
    weights,
    adj,
    fwd,
    adj_next,
    fwd_next,
    signs,
    onsite,
    hop_right,
    hop_down,
    own,
    left,
    right,
    above,
    below,
    forces,
    fwd_out,
    adj_out,
    x,
    strip,
    strip_base,
    strip_hops,
    hops,
    halo,
):
    probes, rows, cols = adj.shape
    groups = 2 * probes
    span = WIDE * groups
    tiles = cols // LANES
    tall = rows + 2 * TILE
    top, bottom = TILE, TILE + rows
    lane = lane_of((TILE, LANES))
    misc = 3 * groups

    def lanes(c):
        return pl.ds(c * LANES, LANES)

    def fields_at(step, c, row):
        return (step, pl.ds(c * tall + row, groups, stride=tiles * tall), slice(None))

    field, base, (s_on, s_right, s_down) = strips(own[...], left[...], right[...], span)
    below_span = lane_of(base.shape) < span
    sign_strip = jnp.where(below_span, turned(base, 2), turned(base, -2))
    corner_above = above[misc + 3 : misc + 4, 0 : 4 * LANES]
    corner_below = below[misc + 3 : misc + 4, 0 : 4 * LANES]
    strip[0, top:bottom, :] = field
    strip[0, top - 1 : top, :] = corner_above[:, :LANES]
    strip[0, bottom : bottom + 1, :] = corner_below[:, :LANES]
    strip_base[0] = base
    strip_base[1] = weights[1] * sign_strip - field
    strip_hops[0, top:bottom, :] = s_on
    strip_hops[1, top:bottom, :] = s_right
    strip_hops[2, top:bottom, :] = s_down
    strip_hops[2, top - 1 : top, :] = corner_above[:, 2 * LANES : 3 * LANES]
    edge_above = corner_above[:, 2 * LANES : 3 * LANES]
    edge_below = s_down[rows - 1 : rows, :]
    one_above = corner_above[:, LANES : 2 * LANES] + edge_above * field[0:1, :]
    one_below = corner_below[:, LANES : 2 * LANES] + edge_below * field[rows - 1 : rows, :]
    strip[1, top - 1 : top, :] = one_above
    strip[1, bottom : bottom + 1, :] = one_below

    hop_before = turned(s_right, -(STEPS - 1))
    wide_lane = lane_of((rows, LANES))
    for c in range(tiles):
        hop = hop_right[:, lanes(c)] * SCALE
        hop_turned = turned(hop, 1)
        hops[0, c, top:bottom, :] = onsite[:, lanes(c)] * SCALE
        hops[1, c, top:bottom, :] = hop
        hops[2, c, top:bottom, :] = jnp.where(wide_lane == 0, hop_before, hop_turned)
        hops[3, c, top:bottom, :] = hop_down[:, lanes(c)] * SCALE
        hops[3, c, top - 1 : top, :] = above[misc + 2 : misc + 3, lanes(c)]
        hop_before = hop_turned

    for g in range(groups):
        source = adj if g < probes else fwd
        for c in range(tiles):
            x[0, pl.ds((g * tiles + c) * tall + top, rows), :] = source[g % probes, :, lanes(c)]
    for c in range(tiles):
        x[fields_at(0, c, top - 1)] = above[0:groups, lanes(c)]
        x[fields_at(0, c, bottom)] = below[0:groups, lanes(c)]

    def set_halo(step):
        now = strip[step, top:bottom, :]
        wide = lane_of(now.shape)
        picked = (lax.rem(wide, WIDE) == STEPS - 1) & (wide < span)
        halo[...] = jnp.where(picked, now, turned(now, -(span + 2)))

    def strip_step(step):
        now = strip[step, top:bottom, :]
        s_right = strip_hops[1, top:bottom, :]
        strip[step + 1, top:bottom, :] = (
            strip_base[step]
            + strip_hops[0, top:bottom, :] * now
            + s_right * turned(now, -1)
            + turned(s_right, 1) * turned(now, 1)
            + strip_hops[2, top:bottom, :] * strip[step, top + 1 : bottom + 1, :]
            + strip_hops[2, top - 1 : bottom - 1, :] * strip[step, top - 1 : bottom - 1, :]
        )

    def gathered(step, row):
        return jnp.concatenate([x[fields_at(step, c, row)] for c in range(tiles)], axis=1)

    def scattered(step, row, value):
        for c in range(tiles):
            x[fields_at(step, c, row)] = value[:, c * LANES : (c + 1) * LANES]

    hop_above = above[misc + 2 : misc + 3, :]
    hop_below = hop_down[rows - 1 : rows, :] * SCALE

    def beyond_one():
        scattered(1, top - 1, above[groups : 2 * groups, :] + hop_above * gathered(0, top))
        scattered(1, bottom, below[groups : 2 * groups, :] + hop_below * gathered(0, bottom - 1))

    def beyond_two():
        for source, hop, corner, strip_row, edge, inside in (
            (above, hop_above, corner_above, one_above, top - 1, top),
            (below, hop_below, corner_below, one_below, bottom, bottom - 1),
        ):
            now = gathered(1, edge)
            value = (
                source[2 * groups : 3 * groups, :]
                + source[misc : misc + 1, :] * now
                + sideways(now, source[misc + 1 : misc + 2, :], strip_row, corner[:, 3 * LANES :], span)
                + hop * gathered(1, inside)
            )
            scattered(2, edge, value)

    def step_of(step):
        def body(t, carry):
            row = pl.multiple_of(t * TILE, TILE)

            def load(at, g, c, by):
                return x[at, pl.ds((g * tiles + c) * tall + top + by + row, TILE), :]

            def hop(kind, c, by=0):
                return hops[kind, c, pl.ds(top + by + row, TILE), :]

            beside = halo[pl.ds(row, TILE), :]
            right_sum = [None] * tiles
            down_sum = [None] * tiles
            site_sum = [None] * tiles
            for p in range(probes):
                kept = []
                for f in range(2):
                    g = f * probes + p
                    outer = turned(beside, -(WIDE * g + STEPS - 1))
                    centre = [load(step, g, c, 0) for c in range(tiles)]
                    low = [turned(v, 1) for v in centre]
                    high = [turned(v, -1) for v in centre]
                    before = [jnp.where(lane == 0, (low[c - 1] if c else outer), low[c]) for c in range(tiles)]
                    after = [
                        jnp.where(lane == LANES - 1, (high[c + 1] if c < tiles - 1 else outer), high[c])
                        for c in range(tiles)
                    ]
                    under = [load(step, g, c, 1) for c in range(tiles)]
                    for c in range(tiles):
                        if step > 0:
                            previous = load(step - 1, g, c, 0)
                        else:
                            previous = (fwd_next if f else adj_next)[p, pl.ds(row, TILE), lanes(c)]
                        total = hop(0, c) * centre[c] - previous
                        total = total + hop(1, c) * after[c]
                        total = total + hop(2, c) * before[c]
                        total = total + hop(3, c) * under[c]
                        total = total + hop(3, c, -1) * load(step, g, c, -1)
                        if f == 0:
                            sign = signs[p, pl.ds(row, TILE), lanes(c)].astype(jnp.float32)
                            total = total + weights[step] * sign
                        if step < STEPS - 1:
                            x[step + 1, pl.ds((g * tiles + c) * tall + top + row, TILE), :] = total
                        else:
                            (fwd_out if f else adj_out)[p, pl.ds(row, TILE), lanes(c)] = total
                    kept.append((centre, after, under))
                (a_centre, a_after, a_under), (q_centre, q_after, q_under) = kept
                for c in range(tiles):
                    r_term = a_centre[c] * q_after[c] + a_after[c] * q_centre[c]
                    d_term = a_centre[c] * q_under[c] + a_under[c] * q_centre[c]
                    s_term = a_centre[c] * q_centre[c]
                    right_sum[c] = r_term if p == 0 else right_sum[c] + r_term
                    down_sum[c] = d_term if p == 0 else down_sum[c] + d_term
                    site_sum[c] = s_term if p == 0 else site_sum[c] + s_term
            for c in range(tiles):
                for kind, term in enumerate((right_sum[c], down_sum[c], site_sum[c])):
                    spot = (kind, pl.ds(row, TILE), lanes(c))
                    forces[spot] = term if step == 0 else forces[spot] + term
            return carry

        lax.fori_loop(0, rows // TILE, body, 0)

    set_halo(0)
    step_of(0)
    strip_step(0)
    beyond_one()
    set_halo(1)
    step_of(1)
    strip_step(1)
    beyond_two()
    set_halo(2)
    step_of(2)


def sum_kernel(mine, other, right_out, down_out, site_out):
    for at, out in enumerate((right_out, down_out, site_out)):
        out[...] = (mine[at] + other[at]) * SCALE


def local(
    signs,
    onsite,
    hop_right,
    hop_down,
    moment_weights,
    forward_now,
    forward_next,
    adjoint_now,
    adjoint_next,
):
    probes, rows, cols = forward_now.shape
    groups = 2 * probes
    f32 = jnp.float32
    fields = (adjoint_now, forward_now, adjoint_next, forward_next, signs)
    lattice = (onsite, hop_right, hop_down)
    in_smem = pl.BlockSpec(memory_space=pltpu.SMEM)
    params = pltpu.CompilerParams(vmem_limit_bytes=VMEM_LIMIT)

    last = cols // LANES - 1
    field_specs = [pl.BlockSpec((probes, rows, LANES), lambda i, c=c: (0, 0, c)) for c in (0, last)]
    lattice_specs = [pl.BlockSpec((rows, LANES), lambda i, c=c: (0, c)) for c in (0, last)]
    packed = pl.pallas_call(
        edge_kernel,
        grid=(1,),
        out_shape=jax.ShapeDtypeStruct((rows, LANES), f32),
        in_specs=[in_smem] + field_specs * len(fields) + lattice_specs * len(lattice),
        out_specs=pl.BlockSpec((rows, LANES), lambda i: (0, 0)),
        compiler_params=params,
        name="edge_columns",
    )(moment_weights, *(v for v in fields + lattice for _ in range(2)))
    left = shifted(packed, "col", 1)
    right = left if lax.axis_size("col") == 2 else shifted(packed, "col", -1)

    last = rows // TILE - 1
    field_specs = [pl.BlockSpec((probes, TILE, cols), lambda i, r=r: (0, r, 0)) for r in (0, last)]
    lattice_specs = [pl.BlockSpec((TILE, cols), lambda i, r=r: (r, 0)) for r in (0, last)]
    strip_specs = [pl.BlockSpec((TILE, LANES), lambda i, r=r: (r, 0)) for r in (0, last)]
    message = jax.ShapeDtypeStruct((3 * groups + TILE, cols), f32)
    whole = pl.BlockSpec(message.shape, lambda i: (0, 0))
    first_rows, last_rows = pl.pallas_call(
        rows_kernel,
        grid=(1,),
        out_shape=(message, message),
        in_specs=[in_smem] + field_specs * len(fields) + lattice_specs * len(lattice) + strip_specs * 3,
        out_specs=(whole, whole),
        compiler_params=params,
        name="edge_rows",
    )(moment_weights, *(v for v in fields + lattice + (packed, left, right) for _ in range(2)))
    above = shifted(last_rows, "strip", 1)
    below = shifted(first_rows, "strip", -1)

    tiles = cols // LANES
    tall = rows + 2 * TILE
    in_vmem = pl.BlockSpec(memory_space=pltpu.VMEM)
    forces, forward_out, adjoint_out = pl.pallas_call(
        main_kernel,
        out_shape=(
            jax.ShapeDtypeStruct((3, rows, cols), f32),
            jax.ShapeDtypeStruct(forward_now.shape, f32),
            jax.ShapeDtypeStruct(forward_now.shape, f32),
        ),
        in_specs=[in_smem] + [in_vmem] * 13,
        out_specs=(in_vmem,) * 3,
        scratch_shapes=[
            pltpu.VMEM((STEPS, groups * tiles * tall, LANES), f32),
            pltpu.VMEM((STEPS, tall, LANES), f32),
            pltpu.VMEM((2, rows, LANES), f32),
            pltpu.VMEM((3, tall, LANES), f32),
            pltpu.VMEM((4, tiles, tall, LANES), f32),
            pltpu.VMEM((rows, LANES), f32),
        ],
        compiler_params=params,
        name="steps",
    )(moment_weights, *fields, *lattice, packed, left, right, above, below)

    other = shifted(forces, "probe", 1)
    right_force, down_force, site_force = pl.pallas_call(
        sum_kernel,
        out_shape=(jax.ShapeDtypeStruct((rows, cols), f32),) * 3,
        in_specs=[in_vmem] * 2,
        out_specs=(in_vmem,) * 3,
        compiler_params=params,
        name="force_sums",
    )(forces, other)
    return right_force, down_force, site_force, forward_out, adjoint_out


def solution(mesh):
    placed = (
        P(("parts", "probe"), "strip", "col"),
        P(("parts", "strip"), "col"),
        P(("parts", "strip"), "col"),
        P(("parts", "strip"), "col"),
        P(),
        P(("parts", "probe"), "strip", "col"),
        P(("parts", "probe"), "strip", "col"),
        P(("parts", "probe"), "strip", "col"),
        P(("parts", "probe"), "strip", "col"),
    )
    return jax.shard_map(
        local,
        mesh=mesh,
        in_specs=placed,
        out_specs=(
            P(("parts", "strip"), "col"),
            P(("parts", "strip"), "col"),
            P(("parts", "strip"), "col"),
            P(("parts", "probe"), "strip", "col"),
            P(("parts", "probe"), "strip", "col"),
        ),
        check_vma=False,
    )
```

```python
import jax
import jax.numpy as jnp
from jax import lax
from jax.experimental import pallas as pl
from jax.experimental.pallas import tpu as pltpu
from jax.sharding import PartitionSpec as P

STEPS = 3
LANES = 128
TILE = 8
spectral_half = 7.5
SCALE = 2.0 / spectral_half

WIDE = 2 * STEPS
VMEM_LIMIT = 16 * 1024 * 1024
COST = 4_000_000


def shifted(x, axis, by):
    size = lax.axis_size(axis)
    return lax.ppermute(x, axis, [(i, (i + by) % size) for i in range(size)])


def lane_of(shape):
    return lax.broadcasted_iota(jnp.int32, shape, len(shape) - 1)


def turned(x, by):
    return pltpu.roll(x, by % x.shape[1], 1)


def pair_swap(x, axis, odd):
    size = lax.axis_size(axis)
    pairs = []
    for i in range(odd, size, 2):
        pairs += [(i, (i + 1) % size), ((i + 1) % size, i)]
    return lax.ppermute(x, axis, pairs)


def load_kernel(
    weights_in,
    adj_in,
    fwd_in,
    adj_next_in,
    fwd_next_in,
    signs_in,
    onsite_in,
    hop_right_in,
    hop_down_in,
    x0,
    adj_next,
    fwd_next,
    signs,
    onsite,
    hop_right,
    hop_down,
    weights,
    out,
    done,
):
    probes, rows, cols = adj_in.shape
    tiles = cols // LANES
    span = WIDE * 2 * probes
    lane = lane_of(out.shape)
    copies = []

    def copy(source, target):
        copies.append(pltpu.make_async_copy(source, target, done.at[len(copies)]))
        copies[-1].start()

    def copy_tile(c):
        for f, source in enumerate((adj_in, fwd_in)):
            copy(
                source.at[:, :, pl.ds(c * LANES, LANES)],
                x0.at[pl.ds(f * probes, probes), c, pl.ds(TILE, rows), :],
            )

    copy(weights_in, weights)
    copy_tile(0)
    copy_tile(tiles - 1)
    copy(signs_in, signs)
    copy(adj_next_in, adj_next)
    copy(fwd_next_in, fwd_next)
    copy(onsite_in, onsite)
    copy(hop_right_in, hop_right)
    copy(hop_down_in, hop_down)
    needed = len(copies)
    for c in range(1, tiles - 1):
        copy_tile(c)
    for at in range(needed):
        copies[at].wait()

    first_lanes, last_lanes = pl.ds(0, LANES), pl.ds(cols - LANES, LANES)

    def joined(low, high):
        return jnp.where(lane < LANES // 2, low, high)

    def joined_field(ref, probe):
        return joined(ref[probe, :, first_lanes], ref[probe, :, last_lanes])

    def joined_now(g):
        return joined(x0[g, 0, pl.ds(TILE, rows), :], x0[g, tiles - 1, pl.ds(TILE, rows), :])

    packed = jnp.zeros(out.shape, jnp.float32)

    def put(packed, x, start):
        return jnp.where((lane >= start) & (lane < start + WIDE), turned(x, start + STEPS), packed)

    first, last = LANES - STEPS, STEPS - 1
    weight = weights[0:1, 0:1]
    for probe in range(probes):
        group = WIDE * probe
        sign = joined_field(signs, probe).astype(jnp.float32)
        base = weight * sign - joined_field(adj_next, probe)
        base = jnp.where(lane == first, turned(sign, -2), jnp.where(lane == last, turned(sign, 2), base))
        packed = put(packed, joined_now(probe), group)
        packed = put(packed, base, span + group)
        group = WIDE * (probes + probe)
        base = jnp.where((lane == first) | (lane == last), 0.0, -joined_field(fwd_next, probe))
        packed = put(packed, joined_now(probes + probe), group)
        packed = put(packed, base, span + group)
    for at, ref in enumerate((onsite, hop_right, hop_down)):
        packed = put(packed, joined(ref[:, first_lanes], ref[:, last_lanes]), 2 * span + WIDE * at)
    out[...] = packed
    for at in range(needed, len(copies)):
        copies[at].wait()


def strips(own, left, right, span):
    lane = lane_of(own.shape)
    inner = lax.rem(lane, WIDE) < STEPS
    low = jnp.where(inner, left, own)
    high = jnp.where(inner, own, right)
    below = lane < span
    field = jnp.where(below, low, turned(high, span))
    base = jnp.where(below, turned(low, -span), high)
    coefficients = []
    for at in range(3):
        start = 2 * span + WIDE * at
        x = jnp.where(
            lane < WIDE,
            turned(low, -start),
            jnp.where((lane >= span) & (lane < span + WIDE), turned(high, span - start), 0.0),
        )
        reach = WIDE
        while reach < span:
            x = x + turned(x, reach)
            reach *= 2
        coefficients.append(x * SCALE)
    return field, base, coefficients


def column_of(row, groups, at):
    shape = (groups, LANES)
    wanted = WIDE * lax.broadcasted_iota(jnp.int32, shape, 0) + at
    return jnp.sum(jnp.where(lane_of(shape) == wanted, row, 0.0), axis=1, keepdims=True)


def sideways(x, hop, strip_row, hop_row, span):
    groups, cols = x.shape
    lane = lane_of(x.shape)
    before = jnp.where(lane == 0, column_of(strip_row, groups, STEPS - 1), turned(x, 1))
    after = jnp.where(lane == cols - 1, column_of(strip_row, groups, span + STEPS), turned(x, -1))
    hop = jnp.broadcast_to(hop, x.shape)
    hop_before = jnp.where(lane == 0, hop_row[:, STEPS - 1 : STEPS], turned(hop, 1))
    return hop * after + hop_before * before


class Block:
    def __init__(self, probes, rows, cols):
        self.probes, self.rows, self.cols = probes, rows, cols
        self.groups = 2 * probes
        self.span = WIDE * self.groups
        self.tiles = cols // LANES
        self.tall = rows + 2 * TILE
        self.field_shape = (self.groups * self.tiles * self.tall, LANES)

    def at(self, g, c, row, count=TILE):
        return (pl.ds((g * self.tiles + c) * self.tall + TILE + row, count), slice(None))

    def across(self, c, row):
        return (pl.ds(c * self.tall + TILE + row, self.groups, stride=self.tiles * self.tall), slice(None))

    def gathered(self, ref, row):
        return jnp.concatenate([ref[self.across(c, row)] for c in range(self.tiles)], axis=1)

    def scattered(self, ref, row, value):
        for c in range(self.tiles):
            ref[self.across(c, row)] = value[:, c * LANES : (c + 1) * LANES]

    def hop_row(self, hops, kind, row):
        at = TILE + row
        return jnp.concatenate([hops[kind, c, at : at + 1, :] for c in range(self.tiles)], axis=1)


def lanes(c):
    return pl.ds(c * LANES, LANES)


def beside(block, strip_tile):
    lane = lane_of(strip_tile.shape)
    picked = (lax.rem(lane, WIDE) == STEPS - 1) & (lane < block.span)
    both = jnp.where(picked, strip_tile, turned(strip_tile, -(block.span + 2)))
    return [turned(both, -(WIDE * g + STEPS - 1)) for g in range(block.groups)]


def tile_step(block, row, now, hops, sides, previous, sign, store, add):
    lane = lane_of((TILE, LANES))
    tiles = block.tiles
    for c in range(tiles):
        at = pl.ds(TILE + row, TILE)
        hop_site, hop_after, hop_before, hop_under = (hops[kind, c, at, :] for kind in range(4))
        hop_over = hops[3, c, pl.ds(TILE + row - 1, TILE), :]
        sums = None
        for p in range(block.probes):
            kept = []
            for f in range(2):
                g = f * block.probes + p
                side = 0.0 if sides is None else sides[g]
                centre = now[block.at(g, c, row)]
                if c > 0:
                    before = turned(jnp.where(lane == LANES - 1, now[block.at(g, c - 1, row)], centre), 1)
                else:
                    before = jnp.where(lane == 0, side, turned(centre, 1))
                if c < tiles - 1:
                    after = turned(jnp.where(lane == 0, now[block.at(g, c + 1, row)], centre), -1)
                else:
                    after = jnp.where(lane == LANES - 1, side, turned(centre, -1))
                under = now[block.at(g, c, row + 1)]
                over = now[block.at(g, c, row - 1)]
                total = hop_site * centre - previous(f, p, c)
                total = total + (hop_after * after + hop_before * before)
                total = total + (hop_under * under + hop_over * over)
                if f == 0:
                    total = total + sign(p, c)
                store(f, p, c, total)
                kept.append((centre, after, under))
            if add is not None:
                (a_centre, a_after, a_under), (q_centre, q_after, q_under) = kept
                terms = (
                    a_centre * q_after + a_after * q_centre,
                    a_centre * q_under + a_under * q_centre,
                    a_centre * q_centre,
                )
                sums = terms if p == 0 else tuple(x + y for x, y in zip(sums, terms))
        if add is not None:
            add(c, *sums)


def force_adder(forces, row, first):
    def add(c, *sums):
        for kind, term in enumerate(sums):
            spot = (kind, pl.ds(row, TILE), lanes(c))
            forces[spot] = term if first else forces[spot] + term

    return add


def sign_reader(signs, weights, step, row):
    weight = jnp.broadcast_to(weights[0:1, step : step + 1], (TILE, LANES))
    return lambda p, c: weight * signs[p, pl.ds(row, TILE), lanes(c)].astype(jnp.float32)


def field_storer(block, target, row):
    def store(f, p, c, tile):
        target[block.at(f * block.probes + p, c, row)] = tile

    return store


def field_reader(block, source, row):
    return lambda f, p, c: source[block.at(f * block.probes + p, c, row)]


def block_reader(adj, fwd, row):
    return lambda f, p, c: (fwd if f else adj)[p, pl.ds(row, TILE), lanes(c)]


def block_storer(adj, fwd, row):
    def store(f, p, c, tile):
        (fwd if f else adj)[p, pl.ds(row, TILE), lanes(c)] = tile

    return store


def first_kernel(weights, x0, adj_next, fwd_next, signs, onsite, hop_right, hop_down, x1, hops, forces):
    block = Block(*signs.shape)
    rows = block.rows
    wide_lane = lane_of((rows, LANES))
    inside = pl.ds(TILE, rows)
    hop_before = 0.0
    for c in range(block.tiles):
        hop = hop_right[:, lanes(c)] * SCALE
        hop_turned = turned(hop, 1)
        hops[0, c, inside, :] = onsite[:, lanes(c)] * SCALE
        hops[1, c, inside, :] = hop
        hops[2, c, inside, :] = jnp.where(wide_lane == 0, hop_before, hop_turned)
        hops[3, c, inside, :] = hop_down[:, lanes(c)] * SCALE
        hop_before = hop_turned
    for row in range(0, rows, TILE):
        inner = 0 < row < rows - TILE
        tile_step(
            block,
            row,
            x0,
            hops,
            None,
            block_reader(adj_next, fwd_next, row),
            sign_reader(signs, weights, 0, row),
            field_storer(block, x1, row),
            force_adder(forces, row, True) if inner else None,
        )


def edge_rows(block, weights, x0, adj_next, fwd_next, signs, hops, strip_tile, rows, at, out):
    edge, second, third = rows
    groups, span = block.groups, block.span
    field, base, (s_on, s_right, s_down) = strip_tile

    def line(x, i):
        return x[i : i + 1, :]

    def next_rows(row):
        return jnp.concatenate([adj_next[:, row, :], fwd_next[:, row, :]], axis=0)

    def sign_rows(step, row):
        sign = weights[0:1, step : step + 1] * signs[:, row, :].astype(jnp.float32)
        return jnp.concatenate([sign, jnp.zeros_like(sign)], axis=0)

    x_edge, x_second, x_third = (block.gathered(x0, row) for row in rows)
    down = block.hop_row(hops, 3, min(edge, second))

    def across(x, row, i):
        return block.hop_row(hops, 0, row) * x + sideways(
            x, block.hop_row(hops, 1, row), line(field, i), line(s_right, i), span
        )

    one = (
        sign_rows(0, second)
        - next_rows(second)
        + across(x_second, second, at[1])
        + down * x_edge
        + block.hop_row(hops, 3, min(second, third)) * x_third
    )
    part_one = sign_rows(0, edge) - next_rows(edge) + across(x_edge, edge, at[0]) + down * x_second
    part_two = sign_rows(1, edge) - x_edge + down * one
    level = base + s_on * field + s_right * turned(field, -1) + turned(s_right, 1) * turned(field, 1)
    strip_one = line(level, at[0]) + line(s_down, min(at[0], at[1])) * line(field, at[1])
    out[0:groups, :] = x_edge
    out[groups : 2 * groups, :] = part_one
    out[2 * groups : 3 * groups, :] = part_two
    misc = 3 * groups
    out[misc : misc + 1, :] = block.hop_row(hops, 0, edge)
    out[misc + 1 : misc + 2, :] = block.hop_row(hops, 1, edge)
    out[misc + 2 : misc + 3, :] = block.hop_row(hops, 3, edge)
    out[misc + 3 : misc + 4, 0 : 4 * LANES] = jnp.concatenate(
        [line(field, at[0]), strip_one, line(s_down, at[0]), line(s_right, at[0])], axis=1
    )
    out[misc + 4 : misc + TILE, :] = jnp.zeros((TILE - 4, out.shape[1]), jnp.float32)


def rows_kernel(weights, x0, adj_next, fwd_next, signs, hops, own, left, right, out_odd, out_even, message):
    block = Block(*signs.shape)
    rows = block.rows
    for side, (lines, at, start) in enumerate(
        (((0, 1, 2), (0, 1, 2), 0), ((rows - 1, rows - 2, rows - 3), (TILE - 1, TILE - 2, TILE - 3), rows - TILE))
    ):
        part = pl.ds(start, TILE)
        strip_tile = strips(own[part, :], left[part, :], right[part, :], block.span)
        edge_rows(
            block, weights, x0, adj_next, fwd_next, signs, hops, strip_tile, lines, at, message.at[side]
        )
    odd = lax.rem(lax.axis_index("strip"), 2) == 1
    out_odd[...] = jnp.where(odd, message[1], message[0])
    out_even[...] = jnp.where(odd, message[0], message[1])


def strip_rows(block, strip, strip_base, strip_hops, step, row, count):
    here = pl.ds(TILE + row, count)
    now = strip[step, here, :]
    s_right = strip_hops[1, here, :]
    strip[step + 1, here, :] = (
        strip_base[step, pl.ds(row, count), :]
        + strip_hops[0, here, :] * now
        + s_right * turned(now, -1)
        + turned(s_right, 1) * turned(now, 1)
        + strip_hops[2, here, :] * strip[step, pl.ds(TILE + row + 1, count), :]
        + strip_hops[2, pl.ds(TILE + row - 1, count), :] * strip[step, pl.ds(TILE + row - 1, count), :]
    )


def inner_kernel(
    weights,
    x0,
    signs,
    own,
    left,
    right,
    sent,
    x1_in,
    hops_in,
    forces_in,
    x1,
    hops,
    forces,
    x2,
    adj_out,
    fwd_out,
    strip,
    strip_base,
    strip_hops,
):
    del sent, x1_in, hops_in, forces_in
    block = Block(*signs.shape)
    rows, tiles, probes = block.rows, block.tiles, block.probes
    inside = pl.ds(TILE, rows)
    lane = lane_of((TILE, LANES))
    field, base, (s_on, s_right, s_down) = strips(own[...], left[...], right[...], block.span)
    sign_strip = jnp.where(lane_of(base.shape) < block.span, turned(base, 2), turned(base, -2))
    strip[0, inside, :] = field
    strip_base[0] = base
    strip_base[1] = weights[0:1, 1:2] * sign_strip - field
    strip_hops[0, inside, :] = s_on
    strip_hops[1, inside, :] = s_right
    strip_hops[2, inside, :] = s_down

    last = tiles - 1
    for row in range(0, rows, TILE):
        at = pl.ds(TILE + row, TILE)
        sides = beside(block, strip[0, at, :])
        hop_first = turned(strip_hops[1, at, :], -(STEPS - 1))
        hops[2, 0, at, :] = jnp.where(lane == 0, hop_first, hops[2, 0, at, :])
        hop_last = hops[1, last, at, :]
        for g in range(block.groups):
            spot = block.at(g, 0, row)
            x1[spot] = x1[spot] + jnp.where(lane == 0, hop_first * sides[g], 0.0)
            spot = block.at(g, last, row)
            x1[spot] = x1[spot] + jnp.where(lane == LANES - 1, hop_last * sides[g], 0.0)
        if 0 < row < rows - TILE:
            total = None
            for p in range(probes):
                q = probes + p
                term = x0[block.at(p, last, row)] * sides[q] + sides[p] * x0[block.at(q, last, row)]
                total = term if total is None else total + term
            spot = (0, pl.ds(row, TILE), lanes(last))
            forces[spot] = forces[spot] + jnp.where(lane == LANES - 1, total, 0.0)

    for step in (1, 2):
        strip_rows(block, strip, strip_base, strip_hops, step - 1, 0, rows)
        for row in range(0, rows, TILE):
            inner = 0 < row < rows - TILE
            if step == 2 and not inner:
                continue
            now, before = (x1, x0) if step == 1 else (x2, x1)
            tile_step(
                block,
                row,
                now,
                hops,
                beside(block, strip[step, pl.ds(TILE + row, TILE), :]),
                field_reader(block, before, row),
                sign_reader(signs, weights, step, row),
                field_storer(block, x2, row) if step == 1 else block_storer(adj_out, fwd_out, row),
                force_adder(forces, row, False) if inner else None,
            )


def outer_kernel(
    weights, adj_next, fwd_next, signs, strip_base, received_odd, received_even, *refs
):
    x0, x1, x2, hops, forces, adj_out, fwd_out, strip, strip_hops, message = refs[9:]
    block = Block(*signs.shape)
    rows, groups, span = block.rows, block.groups, block.span
    odd = lax.rem(lax.axis_index("strip"), 2) == 1
    message[0] = jnp.where(odd, received_even[...], received_odd[...])
    message[1] = jnp.where(odd, received_odd[...], received_even[...])
    above, below = message.at[0], message.at[1]
    misc = 3 * groups
    corner_above = above[misc + 3 : misc + 4, 0 : 4 * LANES]
    corner_below = below[misc + 3 : misc + 4, 0 : 4 * LANES]
    over, under = TILE - 1, TILE + rows
    strip[0, over : over + 1, :] = corner_above[:, :LANES]
    strip[0, under : under + 1, :] = corner_below[:, :LANES]
    s_over = corner_above[:, 2 * LANES : 3 * LANES]
    s_under = strip_hops[2, under - 1 : under, :]
    strip_hops[2, over : over + 1, :] = s_over
    one_above = corner_above[:, LANES : 2 * LANES] + s_over * strip[0, TILE : TILE + 1, :]
    one_below = corner_below[:, LANES : 2 * LANES] + s_under * strip[0, under - 1 : under, :]
    strip[1, over : over + 1, :] = one_above
    strip[1, under : under + 1, :] = one_below
    for c in range(block.tiles):
        hops[3, c, over : over + 1, :] = above[misc + 2 : misc + 3, c * LANES : (c + 1) * LANES]
    block.scattered(x0, -1, above[0:groups, :])
    block.scattered(x0, rows, below[0:groups, :])

    edges = (0, rows - TILE)
    hop_above = block.hop_row(hops, 3, -1)
    hop_below = block.hop_row(hops, 3, rows - 1)
    for step in range(STEPS):
        now = (x0, x1, x2)[step]
        for row in edges:
            previous = (
                block_reader(adj_next, fwd_next, row) if step == 0 else field_reader(block, (x0, x1)[step - 1], row)
            )
            store = (
                block_storer(adj_out, fwd_out, row)
                if step == STEPS - 1
                else field_storer(block, (x1, x2)[step], row)
            )
            tile_step(
                block,
                row,
                now,
                hops,
                beside(block, strip[step, pl.ds(TILE + row, TILE), :]),
                previous,
                sign_reader(signs, weights, step, row),
                store,
                force_adder(forces, row, step == 0),
            )
        if step == STEPS - 1:
            break
        for row in edges:
            strip_rows(block, strip, strip_base, strip_hops, step, row, TILE)
        if step == 0:
            block.scattered(x1, -1, above[groups : 2 * groups, :] + hop_above * block.gathered(x0, 0))
            block.scattered(x1, rows, below[groups : 2 * groups, :] + hop_below * block.gathered(x0, rows - 1))
        else:
            for source, hop, corner, strip_row, edge, inside in (
                (above, hop_above, corner_above, one_above, -1, 0),
                (below, hop_below, corner_below, one_below, rows, rows - 1),
            ):
                line = block.gathered(x1, edge)
                value = (
                    source[2 * groups : 3 * groups, :]
                    + source[misc : misc + 1, :] * line
                    + sideways(line, source[misc + 1 : misc + 2, :], strip_row, corner[:, 3 * LANES :], span)
                    + hop * block.gathered(x1, inside)
                )
                block.scattered(x2, edge, value)


def sum_kernel(mine, other, right_out, down_out, site_out):
    for at, out in enumerate((right_out, down_out, site_out)):
        out[...] = (mine[at] + other[at]) * SCALE


def in_vmem(*arrays):
    return tuple(pltpu.with_memory_space_constraint(v, pltpu.VMEM) for v in arrays)


def local(
    signs,
    onsite,
    hop_right,
    hop_down,
    moment_weights,
    forward_now,
    forward_next,
    adjoint_now,
    adjoint_next,
):
    probes, rows, cols = forward_now.shape
    block = Block(probes, rows, cols)
    groups, tiles, tall = block.groups, block.tiles, block.tall
    f32 = jnp.float32
    vmem = pl.BlockSpec(memory_space=pltpu.VMEM)
    hbm = pl.BlockSpec(memory_space=pltpu.HBM)
    params = pltpu.CompilerParams(vmem_limit_bytes=VMEM_LIMIT)

    def call(kernel, name, inputs, outs, scratch=(), aliases=None, flops=0, in_spec=vmem):
        return pl.pallas_call(
            kernel,
            out_shape=outs,
            in_specs=[in_spec] * len(inputs),
            out_specs=(vmem,) * len(outs),
            scratch_shapes=list(scratch),
            input_output_aliases=aliases or {},
            compiler_params=params,
            cost_estimate=pl.CostEstimate(flops=flops, bytes_accessed=flops, transcendentals=0),
            name=name,
        )(*inputs)

    def like(v, dtype=f32):
        return pltpu.VMEM(v.shape, dtype)

    sources = (
        moment_weights.reshape(1, STEPS),
        adjoint_now,
        forward_now,
        adjoint_next,
        forward_next,
        signs,
        onsite,
        hop_right,
        hop_down,
    )
    sources = tuple(pltpu.with_memory_space_constraint(v, pltpu.HBM) for v in sources)
    x0, adj_next, fwd_next, sign, on, hr, hd, weights, packed = call(
        load_kernel,
        "load",
        sources,
        (
            pltpu.VMEM((groups, tiles, tall, LANES), f32),
            like(adjoint_next),
            like(forward_next),
            like(signs, jnp.int32),
            like(onsite),
            like(hop_right),
            like(hop_down),
            pltpu.VMEM((1, STEPS), f32),
            pltpu.VMEM((rows, LANES), f32),
        ),
        [pltpu.SemaphoreType.DMA((7 + 2 * tiles,))],
        in_spec=hbm,
    )
    x0 = x0.reshape(block.field_shape)
    left = shifted(packed, "col", 1)
    right = left if lax.axis_size("col") == 2 else shifted(packed, "col", -1)

    x0, adj_next, fwd_next, sign, on, hr, hd, weights = in_vmem(
        x0, adj_next, fwd_next, sign, on, hr, hd, weights
    )
    field = pltpu.VMEM(block.field_shape, f32)
    hops_shape = pltpu.VMEM((4, tiles, tall, LANES), f32)
    forces_shape = pltpu.VMEM((3, rows, cols), f32)
    x1, hops, forces = call(
        first_kernel,
        "first_step",
        (weights, x0, adj_next, fwd_next, sign, on, hr, hd),
        (field, hops_shape, forces_shape),
        flops=COST,
    )

    x1, hops, forces, own, left, right = in_vmem(x1, hops, forces, packed, left, right)
    message = pltpu.VMEM((3 * groups + TILE, cols), f32)
    to_odd, to_even = call(
        rows_kernel,
        "edge_rows",
        (weights, x0, adj_next, fwd_next, sign, hops, own, left, right),
        (message, message),
        [pltpu.VMEM((2, 3 * groups + TILE, cols), f32)],
    )
    received_odd = pair_swap(to_odd, "strip", 1)
    received_even = pair_swap(to_even, "strip", 0)

    (sent,) = in_vmem(to_even)
    x1, hops, forces, x2, adj_out, fwd_out, strip, strip_base, strip_hops = call(
        inner_kernel,
        "inner_steps",
        (weights, x0, sign, own, left, right, sent, x1, hops, forces),
        (
            field,
            hops_shape,
            forces_shape,
            field,
            like(adjoint_now),
            like(forward_now),
            pltpu.VMEM((STEPS, tall, LANES), f32),
            pltpu.VMEM((2, rows, LANES), f32),
            pltpu.VMEM((3, tall, LANES), f32),
        ),
        aliases={7: 0, 8: 1, 9: 2},
        flops=COST,
    )

    kept = in_vmem(x0, x1, x2, hops, forces, adj_out, fwd_out, strip, strip_hops)
    read = (weights, adj_next, fwd_next, sign) + in_vmem(strip_base, received_odd, received_even)
    outs = call(
        outer_kernel,
        "outer_rows",
        read + kept,
        tuple(like(v) for v in kept),
        [pltpu.VMEM((2, 3 * groups + TILE, cols), f32)],
        aliases={len(read) + i: i for i in range(len(kept))},
        flops=COST,
    )
    forces, adjoint_out, forward_out = outs[4:7]

    other = shifted(forces, "probe", 1)
    plain = jax.ShapeDtypeStruct((rows, cols), f32)
    right_force, down_force, site_force = call(
        sum_kernel, "force_sums", in_vmem(forces, other), (plain, plain, plain)
    )
    return right_force, down_force, site_force, forward_out, adjoint_out


def solution(mesh):
    placed = (
        P(("parts", "probe"), "strip", "col"),
        P(("parts", "strip"), "col"),
        P(("parts", "strip"), "col"),
        P(("parts", "strip"), "col"),
        P(),
        P(("parts", "probe"), "strip", "col"),
        P(("parts", "probe"), "strip", "col"),
        P(("parts", "probe"), "strip", "col"),
        P(("parts", "probe"), "strip", "col"),
    )
    return jax.shard_map(
        local,
        mesh=mesh,
        in_specs=placed,
        out_specs=(
            P(("parts", "strip"), "col"),
            P(("parts", "strip"), "col"),
            P(("parts", "strip"), "col"),
            P(("parts", "probe"), "strip", "col"),
            P(("parts", "probe"), "strip", "col"),
        ),
        check_vma=False,
    )
```

```python
import jax
import jax.numpy as jnp
from jax import lax
from jax.experimental import pallas as pl
from jax.experimental.pallas import tpu as pltpu
from jax.sharding import PartitionSpec as P

STEPS = 3
LANES = 128
TILE = 8
spectral_half = 7.5
SCALE = 2.0 / spectral_half

WIDE = 2 * STEPS
VMEM_LIMIT = 16 * 1024 * 1024
COST = 4_000_000


def shifted(x, axis, by):
    size = lax.axis_size(axis)
    return lax.ppermute(x, axis, [(i, (i + by) % size) for i in range(size)])


def lane_of(shape):
    return lax.broadcasted_iota(jnp.int32, shape, len(shape) - 1)


def turned(x, by):
    return pltpu.roll(x, by % x.shape[1], 1)


def pair_swap(x, axis, odd):
    size = lax.axis_size(axis)
    pairs = []
    for i in range(odd, size, 2):
        pairs += [(i, (i + 1) % size), ((i + 1) % size, i)]
    return lax.ppermute(x, axis, pairs)


def pack(shape, now, following, signs, lattice, weight):
    groups = len(now)
    span = WIDE * groups
    lane = lane_of(shape)

    def joined(pair):
        return jnp.where(lane < LANES // 2, pair[0], pair[1])

    packed = jnp.zeros(shape, jnp.float32)

    def put(packed, x, start):
        return jnp.where((lane >= start) & (lane < start + WIDE), turned(x, start + STEPS), packed)

    first, last = LANES - STEPS, STEPS - 1
    for g in range(groups):
        if g < len(signs):
            sign = joined(signs[g]).astype(jnp.float32)
            base = weight * sign - joined(following[g])
            base = jnp.where(lane == first, turned(sign, -2), jnp.where(lane == last, turned(sign, 2), base))
        else:
            base = jnp.where((lane == first) | (lane == last), 0.0, -joined(following[g]))
        packed = put(packed, joined(now[g]), WIDE * g)
        packed = put(packed, base, span + WIDE * g)
    for at, pair in enumerate(lattice):
        packed = put(packed, joined(pair), 2 * span + WIDE * at)
    return packed


def ends(ref, *at):
    cols = ref.shape[-1]
    return tuple(ref[(*at, slice(None), pl.ds(start, LANES))] for start in (0, cols - LANES))


def load_kernel(
    weights_in,
    adj_in,
    fwd_in,
    adj_next_in,
    fwd_next_in,
    signs_in,
    onsite_in,
    hop_right_in,
    hop_down_in,
    x0,
    adj_next,
    fwd_next,
    signs,
    onsite,
    hop_right,
    hop_down,
    weights,
    packed,
    done,
):
    probes, rows, cols = adj_in.shape
    groups = 2 * probes
    tiles = cols // LANES
    inside = pl.ds(TILE, rows)
    copies = []

    def copy(source, target):
        copies.append(pltpu.make_async_copy(source, target, done.at[len(copies)]))
        copies[-1].start()

    def copy_tile(c):
        for f, source in enumerate((adj_in, fwd_in)):
            copy(source.at[:, :, lanes(c)], x0.at[pl.ds(f * probes, probes), c, inside, :])

    def copy_lanes(start, count):
        part = pl.ds(start, count)
        for source, target in ((adj_next_in, adj_next), (fwd_next_in, fwd_next), (signs_in, signs)):
            copy(source.at[:, :, part], target.at[:, :, part])

    copy(weights_in, weights)
    for c in (0, tiles - 1):
        copy_tile(c)
        copy_lanes(c * LANES, LANES)
    copy(onsite_in, onsite)
    copy(hop_right_in, hop_right)
    copy(hop_down_in, hop_down)
    needed = len(copies)
    for c in range(1, tiles - 1):
        copy_tile(c)
    copy_lanes(LANES, cols - 2 * LANES)
    for at in range(needed):
        copies[at].wait()
    packed[...] = pack(
        packed.shape,
        [(x0[g, 0, inside, :], x0[g, tiles - 1, inside, :]) for g in range(groups)],
        [ends(ref, p) for ref in (adj_next, fwd_next) for p in range(probes)],
        [ends(signs, p) for p in range(probes)],
        [ends(ref) for ref in (onsite, hop_right, hop_down)],
        weights[0:1, 0:1],
    )
    for at in range(needed, len(copies)):
        copies[at].wait()


def edge_rows(block, weights, x0, adj_next, fwd_next, signs, lattice, lines, out):
    edge, second, third = lines
    groups, cols = block.groups, block.cols
    lane = lane_of((groups, cols))

    def next_rows(row):
        return jnp.concatenate([adj_next[:, row, :], fwd_next[:, row, :]], axis=0)

    def sign_rows(step, row):
        sign = weights[0:1, step : step + 1] * signs[:, row, :].astype(jnp.float32)
        return jnp.concatenate([sign, jnp.zeros_like(sign)], axis=0)

    def hop(kind, row):
        return lattice[kind][row : row + 1, :] * SCALE

    def across(x, row):
        right = jnp.broadcast_to(hop(1, row), x.shape)
        after = jnp.where(lane == cols - 1, 0.0, right * turned(x, -1))
        return hop(0, row) * x + after + jnp.where(lane == 0, 0.0, turned(right * x, 1))

    x_edge, x_second, x_third = (block.gathered(x0, row) for row in lines)
    down = hop(2, min(edge, second))
    one = (
        sign_rows(0, second)
        - next_rows(second)
        + across(x_second, second)
        + down * x_edge
        + hop(2, min(second, third)) * x_third
    )
    out[0:groups, :] = x_edge
    out[groups : 2 * groups, :] = (
        sign_rows(0, edge) - next_rows(edge) + across(x_edge, edge) + down * x_second
    )
    out[2 * groups : 3 * groups, :] = sign_rows(1, edge) - x_edge + down * one
    misc = 3 * groups
    for kind in range(3):
        out[misc + kind : misc + kind + 1, :] = hop(kind, edge)
    out[misc + 3 : misc + TILE, :] = jnp.zeros((TILE - 3, cols), jnp.float32)


def strips(own, left, right, span):
    lane = lane_of(own.shape)
    inner = lax.rem(lane, WIDE) < STEPS
    low = jnp.where(inner, left, own)
    high = jnp.where(inner, own, right)
    below = lane < span
    field = jnp.where(below, low, turned(high, span))
    base = jnp.where(below, turned(low, -span), high)
    coefficients = []
    for at in range(3):
        start = 2 * span + WIDE * at
        x = jnp.where(
            lane < WIDE,
            turned(low, -start),
            jnp.where((lane >= span) & (lane < span + WIDE), turned(high, span - start), 0.0),
        )
        reach = WIDE
        while reach < span:
            x = x + turned(x, reach)
            reach *= 2
        coefficients.append(x * SCALE)
    return field, base, coefficients


def column_of(row, groups, at):
    shape = (groups, LANES)
    wanted = WIDE * lax.broadcasted_iota(jnp.int32, shape, 0) + at
    return jnp.sum(jnp.where(lane_of(shape) == wanted, row, 0.0), axis=1, keepdims=True)


def sideways(x, hop, strip_row, hop_row, span):
    groups, cols = x.shape
    lane = lane_of(x.shape)
    before = jnp.where(lane == 0, column_of(strip_row, groups, STEPS - 1), turned(x, 1))
    after = jnp.where(lane == cols - 1, column_of(strip_row, groups, span + STEPS), turned(x, -1))
    hop = jnp.broadcast_to(hop, x.shape)
    hop_before = jnp.where(lane == 0, hop_row[:, STEPS - 1 : STEPS], turned(hop, 1))
    return hop * after + hop_before * before


class Block:
    def __init__(self, probes, rows, cols):
        self.probes, self.rows, self.cols = probes, rows, cols
        self.groups = 2 * probes
        self.span = WIDE * self.groups
        self.tiles = cols // LANES
        self.tall = rows + 2 * TILE
        self.field_shape = (self.groups * self.tiles * self.tall, LANES)

    def at(self, g, c, row, count=TILE):
        return (pl.ds((g * self.tiles + c) * self.tall + TILE + row, count), slice(None))

    def across(self, c, row):
        return (pl.ds(c * self.tall + TILE + row, self.groups, stride=self.tiles * self.tall), slice(None))

    def gathered(self, ref, row):
        return jnp.concatenate([ref[self.across(c, row)] for c in range(self.tiles)], axis=1)

    def scattered(self, ref, row, value):
        for c in range(self.tiles):
            ref[self.across(c, row)] = value[:, c * LANES : (c + 1) * LANES]

    def hop_row(self, hops, kind, row):
        at = TILE + row
        return jnp.concatenate([hops[kind, c, at : at + 1, :] for c in range(self.tiles)], axis=1)


def lanes(c):
    return pl.ds(c * LANES, LANES)


def beside(block, strip_tile):
    lane = lane_of(strip_tile.shape)
    picked = (lax.rem(lane, WIDE) == STEPS - 1) & (lane < block.span)
    both = jnp.where(picked, strip_tile, turned(strip_tile, -(block.span + 2)))
    return [turned(both, -(WIDE * g + STEPS - 1)) for g in range(block.groups)]


def tile_step(block, row, now, hops, sides, previous, sign, store, add, columns=None):
    lane = lane_of((TILE, LANES))
    tiles = block.tiles
    for c in range(tiles) if columns is None else columns:
        at = pl.ds(TILE + row, TILE)
        hop_site, hop_after, hop_before, hop_under = (hops[kind, c, at, :] for kind in range(4))
        hop_over = hops[3, c, pl.ds(TILE + row - 1, TILE), :]
        sums = None
        for p in range(block.probes):
            kept = []
            for f in range(2):
                g = f * block.probes + p
                side = 0.0 if sides is None else sides[g]
                centre = now[block.at(g, c, row)]
                if c > 0:
                    before = turned(jnp.where(lane == LANES - 1, now[block.at(g, c - 1, row)], centre), 1)
                else:
                    before = jnp.where(lane == 0, side, turned(centre, 1))
                if c < tiles - 1:
                    after = turned(jnp.where(lane == 0, now[block.at(g, c + 1, row)], centre), -1)
                else:
                    after = jnp.where(lane == LANES - 1, side, turned(centre, -1))
                under = now[block.at(g, c, row + 1)]
                over = now[block.at(g, c, row - 1)]
                total = hop_site * centre - previous(f, p, c)
                total = total + (hop_after * after + hop_before * before)
                total = total + (hop_under * under + hop_over * over)
                if f == 0:
                    total = total + sign(p, c)
                store(f, p, c, total)
                kept.append((centre, after, under))
            if add is not None:
                (a_centre, a_after, a_under), (q_centre, q_after, q_under) = kept
                terms = (
                    a_centre * q_after + a_after * q_centre,
                    a_centre * q_under + a_under * q_centre,
                    a_centre * q_centre,
                )
                sums = terms if p == 0 else tuple(x + y for x, y in zip(sums, terms))
        if add is not None:
            add(c, *sums)


def force_adder(forces, row, first):
    def add(c, *sums):
        for kind, term in enumerate(sums):
            spot = (kind, pl.ds(row, TILE), lanes(c))
            forces[spot] = term if first else forces[spot] + term

    return add


def sign_reader(signs, weights, step, row):
    weight = jnp.broadcast_to(weights[0:1, step : step + 1], (TILE, LANES))
    return lambda p, c: weight * signs[p, pl.ds(row, TILE), lanes(c)].astype(jnp.float32)


def field_storer(block, target, row):
    def store(f, p, c, tile):
        target[block.at(f * block.probes + p, c, row)] = tile

    return store


def field_reader(block, source, row):
    return lambda f, p, c: source[block.at(f * block.probes + p, c, row)]


def block_reader(adj, fwd, row):
    return lambda f, p, c: (fwd if f else adj)[p, pl.ds(row, TILE), lanes(c)]


def block_storer(adj, fwd, row):
    def store(f, p, c, tile):
        (fwd if f else adj)[p, pl.ds(row, TILE), lanes(c)] = tile

    return store


def first_kernel(
    weights, x0, adj_next, fwd_next, signs, onsite, hop_right, hop_down, x0_out, x1, hops, forces, messages
):
    block = Block(*signs.shape)
    rows = block.rows
    nothing = jnp.zeros((block.groups, block.cols), jnp.float32)
    for row in (-1, rows):
        block.scattered(x0_out, row, nothing)
        block.scattered(x1, row, nothing)
    for side, lines in enumerate(((0, 1, 2), (rows - 1, rows - 2, rows - 3))):
        edge_rows(
            block,
            weights,
            x0,
            adj_next,
            fwd_next,
            signs,
            (onsite, hop_right, hop_down),
            lines,
            messages.at[side],
        )
    wide_lane = lane_of((rows, LANES))
    inside = pl.ds(TILE, rows)
    hop_before = 0.0
    for c in range(block.tiles):
        hop = hop_right[:, lanes(c)] * SCALE
        hop_turned = turned(hop, 1)
        hops[0, c, inside, :] = onsite[:, lanes(c)] * SCALE
        hops[1, c, inside, :] = hop
        hops[2, c, inside, :] = jnp.where(wide_lane == 0, hop_before, hop_turned)
        hops[3, c, inside, :] = hop_down[:, lanes(c)] * SCALE
        hops[3, c, pl.ds(TILE - 1, 1), :] = jnp.zeros((1, LANES), jnp.float32)
        hop_before = hop_turned
    for row in range(0, rows, TILE):
        tile_step(
            block,
            row,
            x0_out,
            hops,
            None,
            block_reader(adj_next, fwd_next, row),
            sign_reader(signs, weights, 0, row),
            field_storer(block, x1, row),
            force_adder(forces, row, True),
        )


def at_ends(block, row):
    return column_of(row, block.groups, STEPS - 1), column_of(row, block.groups, block.span + STEPS)


def send_kernel(own, left, right, messages, to_odd, to_even, message):
    rows, cols = own.shape[0], to_odd.shape[1]
    groups = (to_odd.shape[0] - TILE) // 3
    span = WIDE * groups
    misc = 3 * groups
    lane = lane_of((groups, LANES))
    left_part = lane_of((TILE, LANES)) < span
    message[...] = messages[...]
    for side, (edge, second) in enumerate(((0, 1), (TILE - 1, TILE - 2))):
        part = pl.ds(side * (rows - TILE), TILE)
        field, base, (s_on, s_right, s_down) = strips(own[part, :], left[part, :], right[part, :], span)
        before = turned(s_right, 1)
        level = base + s_on * field + s_right * turned(field, -1) + before * turned(field, 1)
        inward = jnp.where(left_part, s_right, before) * field
        down_inward = jnp.where(left_part, turned(s_down, -1), turned(s_down, 1))
        bond = min(edge, second)
        one = inward[edge : edge + 1, :]
        two = down_inward[bond : bond + 1, :] * inward[second : second + 1, :]
        for at, row in ((groups, one), (2 * groups, two)):
            for start, value, spot in (
                (0, column_of(row, groups, STEPS - 1), 0),
                (cols - LANES, column_of(row, groups, span + STEPS), LANES - 1),
            ):
                where = (side, pl.ds(at, groups), pl.ds(start, LANES))
                message[where] = message[where] + jnp.where(lane == spot, value, 0.0)
        message[side, misc + 3 : misc + 4, 0 : 4 * LANES] = jnp.concatenate(
            [
                field[edge : edge + 1, :],
                level[edge : edge + 1, :] + s_down[bond : bond + 1, :] * field[second : second + 1, :],
                s_down[edge : edge + 1, :],
                s_right[edge : edge + 1, :],
            ],
            axis=1,
        )
    odd = lax.rem(lax.axis_index("strip"), 2) == 1
    to_odd[...] = jnp.where(odd, message[1], message[0])
    to_even[...] = jnp.where(odd, message[0], message[1])


def strip_rows(block, strip, strip_base, strip_hops, step, row, count):
    here = pl.ds(TILE + row, count)
    now = strip[step, here, :]
    s_right = strip_hops[1, here, :]
    strip[step + 1, here, :] = (
        strip_base[step, pl.ds(row, count), :]
        + strip_hops[0, here, :] * now
        + s_right * turned(now, -1)
        + turned(s_right, 1) * turned(now, 1)
        + strip_hops[2, here, :] * strip[step, pl.ds(TILE + row + 1, count), :]
        + strip_hops[2, pl.ds(TILE + row - 1, count), :] * strip[step, pl.ds(TILE + row - 1, count), :]
    )


def inner_kernel(
    weights,
    x0,
    signs,
    own,
    left,
    right,
    sent,
    x1_in,
    hops_in,
    forces_in,
    x1,
    hops,
    forces,
    x2,
    adj_out,
    fwd_out,
    strip,
    strip_base,
    strip_hops,
):
    del sent, x1_in, hops_in, forces_in
    block = Block(*signs.shape)
    rows, tiles, probes = block.rows, block.tiles, block.probes
    inside = pl.ds(TILE, rows)
    lane = lane_of((TILE, LANES))
    nothing = jnp.zeros((block.groups, block.cols), jnp.float32)
    for row in (-1, rows):
        block.scattered(x2, row, nothing)
    for row in (TILE - 1, TILE + rows):
        strip_hops[2, row : row + 1, :] = jnp.zeros((1, LANES), jnp.float32)
        for step in range(2):
            strip[step, row : row + 1, :] = jnp.zeros((1, LANES), jnp.float32)
    field, base, (s_on, s_right, s_down) = strips(own[...], left[...], right[...], block.span)
    sign_strip = jnp.where(lane_of(base.shape) < block.span, turned(base, 2), turned(base, -2))
    strip[0, inside, :] = field
    strip_base[0] = base
    strip_base[1] = weights[0:1, 1:2] * sign_strip - field
    strip_hops[0, inside, :] = s_on
    strip_hops[1, inside, :] = s_right
    strip_hops[2, inside, :] = s_down

    last = tiles - 1
    for row in range(0, rows, TILE):
        at = pl.ds(TILE + row, TILE)
        sides = beside(block, strip[0, at, :])
        hop_first = turned(strip_hops[1, at, :], -(STEPS - 1))
        hops[2, 0, at, :] = jnp.where(lane == 0, hop_first, hops[2, 0, at, :])
        hop_last = hops[1, last, at, :]
        for g in range(block.groups):
            spot = block.at(g, 0, row)
            x1[spot] = x1[spot] + jnp.where(lane == 0, hop_first * sides[g], 0.0)
            spot = block.at(g, last, row)
            x1[spot] = x1[spot] + jnp.where(lane == LANES - 1, hop_last * sides[g], 0.0)
        total = None
        for p in range(probes):
            q = probes + p
            term = x0[block.at(p, last, row)] * sides[q] + sides[p] * x0[block.at(q, last, row)]
            total = term if total is None else total + term
        spot = (0, pl.ds(row, TILE), lanes(last))
        forces[spot] = forces[spot] + jnp.where(lane == LANES - 1, total, 0.0)

    for step in (1, 2):
        strip_rows(block, strip, strip_base, strip_hops, step - 1, 0, rows)
        now, before = (x1, x0) if step == 1 else (x2, x1)
        for row in range(0, rows, TILE):
            tile_step(
                block,
                row,
                now,
                hops,
                beside(block, strip[step, pl.ds(TILE + row, TILE), :]),
                field_reader(block, before, row),
                sign_reader(signs, weights, step, row),
                field_storer(block, x2, row) if step == 1 else block_storer(adj_out, fwd_out, row),
                force_adder(forces, row, False),
            )


def sorted_messages(received_odd, received_even, message):
    odd = lax.rem(lax.axis_index("strip"), 2) == 1
    message[0] = jnp.where(odd, received_even[...], received_odd[...])
    message[1] = jnp.where(odd, received_odd[...], received_even[...])
    return message.at[0], message.at[1]


def other_field(x):
    return pltpu.roll(x, x.shape[0] // 2, 0)


def outer_kernel(
    x0, x1, x2, hops, strip, strip_hops, received_odd, received_even, forces_in, adj_in, fwd_in, *refs
):
    del forces_in, adj_in, fwd_in
    forces, adj_out, fwd_out, message = refs
    probes, rows, cols = adj_out.shape
    block = Block(probes, rows, cols)
    groups, span = block.groups, block.span
    misc = 3 * groups
    lane = lane_of((groups, cols))
    messages = sorted_messages(received_odd, received_even, message)

    def s_line(ref, at, row):
        return ref[at, TILE + row : TILE + row + 1, :]

    def neighbours(x, strip_row):
        first, last = at_ends(block, strip_row)
        before = jnp.where(lane == 0, first, turned(x, 1))
        return before, jnp.where(lane == cols - 1, last, turned(x, -1))

    for side, source in enumerate(messages):
        edge, second, third = (0, 1, 2) if side == 0 else (rows - 1, rows - 2, rows - 3)
        bond, next_bond = (edge, second) if side == 0 else (second, third)
        corner = source[misc + 3 : misc + 4, 0 : 4 * LANES]
        c_field, c_one, c_down, c_right = (corner[:, k * LANES : (k + 1) * LANES] for k in range(4))
        hop_out = source[misc + 2 : misc + 3, :] if side == 0 else block.hop_row(hops, 3, edge)
        s_out = c_down if side == 0 else s_line(strip_hops, 2, edge)
        hop_in, hop_next = block.hop_row(hops, 3, bond), block.hop_row(hops, 3, next_bond)

        def across(x, pair, row):
            before, after = pair
            return (
                block.hop_row(hops, 0, row) * x
                + block.hop_row(hops, 1, row) * after
                + block.hop_row(hops, 2, row) * before
            )

        s_right = s_line(strip_hops, 1, edge)
        s_one_beyond = c_one + s_out * s_line(strip, 0, edge)
        s_one = s_out * c_field
        s_two = (
            s_line(strip_hops, 0, edge) * s_one
            + s_right * turned(s_one, -1)
            + turned(s_right, 1) * turned(s_one, 1)
            + s_out * s_one_beyond
        )
        s_two_second = s_line(strip_hops, 2, bond) * s_one

        x0_edge, x1_edge, x2_edge = (block.gathered(x, edge) for x in (x0, x1, x2))
        x1_second, x2_second = (block.gathered(x, second) for x in (x1, x2))
        x2_third = block.gathered(x2, third)
        x0_beyond = source[0:groups, :]
        one = hop_out * x0_beyond
        one_pair = neighbours(one, s_one)
        x1_beyond = source[groups : 2 * groups, :] + hop_out * x0_edge
        two = across(one, one_pair, edge) + hop_out * x1_beyond
        two_pair = neighbours(two, s_two)
        two_second = hop_in * one
        two_second_pair = neighbours(two_second, s_two_second)
        x1_new = x1_edge + one
        x2_beyond = (
            source[2 * groups : 3 * groups, :]
            + source[misc : misc + 1, :] * x1_beyond
            + sideways(x1_beyond, source[misc + 1 : misc + 2, :], s_one_beyond, c_right, span)
            + hop_out * x1_new
        )
        x2_new, x2_second_new = x2_edge + two, x2_second + two_second
        changes = (
            (edge, across(two, two_pair, edge) + hop_in * two_second + hop_out * x2_beyond - one),
            (second, across(two_second, two_second_pair, second) + hop_in * two),
            (third, hop_next * two_second),
        )
        for row, change in changes:
            adj_out[:, row, :] = adj_out[:, row, :] + change[:probes]
            fwd_out[:, row, :] = fwd_out[:, row, :] + change[probes:]

        def changed(x, change, new, other, other_change):
            return change * other_field(other) + x * other_field(other_change)

        def right_of(x, strip_row):
            return jnp.where(lane == cols - 1, column_of(strip_row, groups, span + STEPS), turned(x, -1))

        one_right = right_of(x1_new, s_line(strip, 1, edge) + s_one)
        two_right = right_of(x2_new, s_line(strip, 2, edge) + s_two)
        second_right = right_of(x2_second_new, s_line(strip, 2, second) + s_two_second)
        terms = [
            (
                0,
                edge,
                changed(x1_edge, one, x1_new, one_right, one_pair[1])
                + changed(x2_edge, two, x2_new, two_right, two_pair[1]),
            ),
            (0, second, changed(x2_second, two_second, x2_second_new, second_right, two_second_pair[1])),
            (1, bond, changed(x2_edge, two, x2_new, x2_second_new, two_second) + one * other_field(x1_second)),
            (1, next_bond, two_second * other_field(x2_third)),
            (2, edge, 0.5 * (changed(x1_edge, one, x1_new, x1_new, one) + changed(x2_edge, two, x2_new, x2_new, two))),
            (2, second, 0.5 * changed(x2_second, two_second, x2_second_new, x2_second_new, two_second)),
        ]
        if side == 1:
            outward = (
                x0_edge * other_field(x0_beyond)
                + x1_new * other_field(x1_beyond)
                + x2_new * other_field(x2_beyond)
            )
            terms.append((1, edge, outward))
        for kind, row, term in terms:
            spot = (kind, pl.ds(row, 1), slice(None))
            forces[spot] = forces[spot] + jnp.sum(term, axis=0, keepdims=True)


def sum_kernel(mine, other, right_out, down_out, site_out):
    for at, out in enumerate((right_out, down_out, site_out)):
        out[...] = (mine[at] + other[at]) * SCALE


def both_sides(x):
    left = shifted(x, "col", 1)
    return left, left if lax.axis_size("col") == 2 else shifted(x, "col", -1)


def in_vmem(*arrays):
    return tuple(pltpu.with_memory_space_constraint(v, pltpu.VMEM) for v in arrays)


def local(
    signs,
    onsite,
    hop_right,
    hop_down,
    moment_weights,
    forward_now,
    forward_next,
    adjoint_now,
    adjoint_next,
):
    probes, rows, cols = forward_now.shape
    block = Block(probes, rows, cols)
    groups, tiles, tall = block.groups, block.tiles, block.tall
    f32 = jnp.float32
    vmem = pl.BlockSpec(memory_space=pltpu.VMEM)
    hbm = pl.BlockSpec(memory_space=pltpu.HBM)
    params = pltpu.CompilerParams(vmem_limit_bytes=VMEM_LIMIT)

    def call(kernel, name, inputs, outs, scratch=(), aliases=None, flops=0, in_spec=vmem):
        return pl.pallas_call(
            kernel,
            out_shape=outs,
            in_specs=[in_spec] * len(inputs),
            out_specs=(vmem,) * len(outs),
            scratch_shapes=list(scratch),
            input_output_aliases=aliases or {},
            compiler_params=params,
            cost_estimate=pl.CostEstimate(flops=flops, bytes_accessed=flops, transcendentals=0),
            name=name,
        )(*inputs)

    def like(v, dtype=f32):
        return pltpu.VMEM(v.shape, dtype)

    sources = (
        moment_weights.reshape(1, STEPS),
        adjoint_now,
        forward_now,
        adjoint_next,
        forward_next,
        signs,
        onsite,
        hop_right,
        hop_down,
    )
    sources = tuple(pltpu.with_memory_space_constraint(v, pltpu.HBM) for v in sources)
    strip_tile = pltpu.VMEM((rows, LANES), f32)
    x0, adj_next, fwd_next, sign, on, hr, hd, weights, packed = call(
        load_kernel,
        "load",
        sources,
        (
            pltpu.VMEM((groups, tiles, tall, LANES), f32),
            like(adjoint_next),
            like(forward_next),
            like(signs, jnp.int32),
            like(onsite),
            like(hop_right),
            like(hop_down),
            pltpu.VMEM((1, STEPS), f32),
            strip_tile,
        ),
        [pltpu.SemaphoreType.DMA((13 + 2 * tiles,))],
        in_spec=hbm,
    )
    x0 = x0.reshape(block.field_shape)
    left, right = both_sides(packed)

    x0, adj_next, fwd_next, sign, on, hr, hd, weights, packed = in_vmem(
        x0, adj_next, fwd_next, sign, on, hr, hd, weights, packed
    )
    message = pltpu.VMEM((3 * groups + TILE, cols), f32)
    both_messages = pltpu.VMEM((2, 3 * groups + TILE, cols), f32)
    field = pltpu.VMEM(block.field_shape, f32)
    hops_shape = pltpu.VMEM((4, tiles, tall, LANES), f32)
    forces_shape = pltpu.VMEM((3, rows, cols), f32)
    x0, x1, hops, forces, messages = call(
        first_kernel,
        "step_0",
        (weights, x0, adj_next, fwd_next, sign, on, hr, hd),
        (field, field, hops_shape, forces_shape, both_messages),
        aliases={1: 0},
        flops=COST,
    )

    x0, x1, hops, forces, messages, left, right = in_vmem(x0, x1, hops, forces, messages, left, right)
    to_odd, to_even = call(
        send_kernel, "edge_rows", (packed, left, right, messages), (message, message), [both_messages]
    )
    received_odd = pair_swap(to_odd, "strip", 1)
    received_even = pair_swap(to_even, "strip", 0)

    (sent,) = in_vmem(to_even)
    x1, hops, forces, x2, adj_out, fwd_out, strip, strip_base, strip_hops = call(
        inner_kernel,
        "inner_steps",
        (weights, x0, sign, packed, left, right, sent, x1, hops, forces),
        (
            field,
            hops_shape,
            forces_shape,
            field,
            like(adjoint_now),
            like(forward_now),
            pltpu.VMEM((STEPS, tall, LANES), f32),
            pltpu.VMEM((2, rows, LANES), f32),
            pltpu.VMEM((3, tall, LANES), f32),
        ),
        aliases={7: 0, 8: 1, 9: 2},
        flops=COST,
    )

    kept = in_vmem(forces, adj_out, fwd_out)
    read = (x0,) + in_vmem(x1, x2, hops, strip, strip_hops, received_odd, received_even)
    forces, adjoint_out, forward_out = call(
        outer_kernel,
        "outer_rows",
        read + kept,
        tuple(like(v) for v in kept),
        [both_messages],
        aliases={len(read) + i: i for i in range(len(kept))},
        flops=COST,
    )

    other = shifted(forces, "probe", 1)
    plain = jax.ShapeDtypeStruct((rows, cols), f32)
    right_force, down_force, site_force = call(
        sum_kernel, "force_sums", in_vmem(forces, other), (plain, plain, plain)
    )
    return right_force, down_force, site_force, forward_out, adjoint_out


def solution(mesh):
    placed = (
        P(("parts", "probe"), "strip", "col"),
        P(("parts", "strip"), "col"),
        P(("parts", "strip"), "col"),
        P(("parts", "strip"), "col"),
        P(),
        P(("parts", "probe"), "strip", "col"),
        P(("parts", "probe"), "strip", "col"),
        P(("parts", "probe"), "strip", "col"),
        P(("parts", "probe"), "strip", "col"),
    )
    return jax.shard_map(
        local,
        mesh=mesh,
        in_specs=placed,
        out_specs=(
            P(("parts", "strip"), "col"),
            P(("parts", "strip"), "col"),
            P(("parts", "strip"), "col"),
            P(("parts", "probe"), "strip", "col"),
            P(("parts", "probe"), "strip", "col"),
        ),
        check_vma=False,
    )
```

```python
import jax
import jax.numpy as jnp
from jax import lax
from jax.experimental import pallas as pl
from jax.experimental.pallas import tpu as pltpu
from jax.sharding import PartitionSpec as P

STEPS = 3
LANES = 128
TILE = 8
spectral_half = 7.5
SCALE = 2.0 / spectral_half

WIDE = 2 * STEPS
VMEM_LIMIT = 16 * 1024 * 1024
COST = 4_000_000


def shifted(x, axis, by):
    size = lax.axis_size(axis)
    return lax.ppermute(x, axis, [(i, (i + by) % size) for i in range(size)])


def lane_of(shape):
    return lax.broadcasted_iota(jnp.int32, shape, len(shape) - 1)


def lanes_from(x, source):
    return jnp.take_along_axis(x, source, axis=1, mode="promise_in_bounds")


def turned(x, by):
    return pltpu.roll(x, by % x.shape[1], 1)


def pair_swap(x, axis, odd):
    size = lax.axis_size(axis)
    pairs = []
    for i in range(odd, size, 2):
        pairs += [(i, (i + 1) % size), ((i + 1) % size, i)]
    return lax.ppermute(x, axis, pairs)


def pack(shape, now, following, signs, lattice, weight):
    groups = len(now)
    span = WIDE * groups
    lane = lane_of(shape)

    def joined(pair):
        return jnp.where(lane < LANES // 2, pair[0], pair[1])

    packed = jnp.zeros(shape, jnp.float32)

    def put(packed, x, start):
        return jnp.where((lane >= start) & (lane < start + WIDE), turned(x, start + STEPS), packed)

    first, last = LANES - STEPS, STEPS - 1
    for g in range(groups):
        if g < len(signs):
            sign = joined(signs[g]).astype(jnp.float32)
            base = weight * sign - joined(following[g])
            base = jnp.where(lane == first, turned(sign, -2), jnp.where(lane == last, turned(sign, 2), base))
        else:
            base = jnp.where((lane == first) | (lane == last), 0.0, -joined(following[g]))
        packed = put(packed, joined(now[g]), WIDE * g)
        packed = put(packed, base, span + WIDE * g)
    for at, pair in enumerate(lattice):
        packed = put(packed, joined(pair), 2 * span + WIDE * at)
    return packed


def ends(ref, *at):
    cols = ref.shape[-1]
    return tuple(ref[(*at, slice(None), pl.ds(start, LANES))] for start in (0, cols - LANES))


def load_kernel(
    weights_in,
    adj_in,
    fwd_in,
    adj_next_in,
    fwd_next_in,
    signs_in,
    onsite_in,
    hop_right_in,
    hop_down_in,
    x0,
    adj_next,
    fwd_next,
    signs,
    onsite,
    hop_right,
    hop_down,
    weights,
    packed,
    done,
):
    probes, rows, cols = adj_in.shape
    groups = 2 * probes
    tiles = cols // LANES
    inside = pl.ds(TILE, rows)
    copies = []

    def copy(source, target):
        copies.append(pltpu.make_async_copy(source, target, done.at[len(copies)]))
        copies[-1].start()

    def copy_tile(c):
        for f, source in enumerate((adj_in, fwd_in)):
            copy(source.at[:, :, lanes(c)], x0.at[pl.ds(f * probes, probes), c, inside, :])

    def copy_lanes(start, count):
        part = pl.ds(start, count)
        for source, target in ((adj_next_in, adj_next), (fwd_next_in, fwd_next), (signs_in, signs)):
            copy(source.at[:, :, part], target.at[:, :, part])

    copy(weights_in, weights)
    for c in (0, tiles - 1):
        copy_tile(c)
        copy_lanes(c * LANES, LANES)
    copy(onsite_in, onsite)
    copy(hop_right_in, hop_right)
    copy(hop_down_in, hop_down)
    needed = len(copies)
    for c in range(1, tiles - 1):
        copy_tile(c)
    copy_lanes(LANES, cols - 2 * LANES)
    for at in range(needed):
        copies[at].wait()
    packed[...] = pack(
        packed.shape,
        [(x0[g, 0, inside, :], x0[g, tiles - 1, inside, :]) for g in range(groups)],
        [ends(ref, p) for ref in (adj_next, fwd_next) for p in range(probes)],
        [ends(signs, p) for p in range(probes)],
        [ends(ref) for ref in (onsite, hop_right, hop_down)],
        weights[0:1, 0:1],
    )
    for at in range(needed, len(copies)):
        copies[at].wait()


def edge_rows(block, weights, x0, adj_next, fwd_next, signs, lattice, lines, out):
    edge, second, third = lines
    groups, cols = block.groups, block.cols
    lane = lane_of((groups, cols))

    def next_rows(row):
        return jnp.concatenate([adj_next[:, row, :], fwd_next[:, row, :]], axis=0)

    def sign_rows(step, row):
        sign = weights[0:1, step : step + 1] * signs[:, row, :].astype(jnp.float32)
        return jnp.concatenate([sign, jnp.zeros_like(sign)], axis=0)

    def hop(kind, row):
        return lattice[kind][row : row + 1, :] * SCALE

    def across(x, row):
        right = jnp.broadcast_to(hop(1, row), x.shape)
        after = jnp.where(lane == cols - 1, 0.0, right * turned(x, -1))
        return hop(0, row) * x + after + jnp.where(lane == 0, 0.0, turned(right * x, 1))

    x_edge, x_second, x_third = (block.gathered(x0, row) for row in lines)
    down = hop(2, min(edge, second))
    one = (
        sign_rows(0, second)
        - next_rows(second)
        + across(x_second, second)
        + down * x_edge
        + hop(2, min(second, third)) * x_third
    )
    out[0:groups, :] = x_edge
    out[groups : 2 * groups, :] = (
        sign_rows(0, edge) - next_rows(edge) + across(x_edge, edge) + down * x_second
    )
    out[2 * groups : 3 * groups, :] = sign_rows(1, edge) - x_edge + down * one
    misc = 3 * groups
    for kind in range(3):
        out[misc + kind : misc + kind + 1, :] = hop(kind, edge)
    out[misc + 3 : misc + TILE, :] = jnp.zeros((TILE - 3, cols), jnp.float32)


def strips(own, left, right, span):
    lane = lane_of(own.shape)
    inner = lax.rem(lane, WIDE) < STEPS
    low = jnp.where(inner, left, own)
    high = jnp.where(inner, own, right)
    below = lane < span
    field = jnp.where(below, low, turned(high, span))
    base = jnp.where(below, turned(low, -span), high)
    coefficients = []
    for at in range(3):
        source = 2 * span + WIDE * at + lax.rem(lane, WIDE)
        coefficients.append(jnp.where(below, lanes_from(low, source), lanes_from(high, source)) * SCALE)
    return field, base, coefficients


def column_of(row, groups, at, cols=LANES):
    shape = (groups, LANES)
    source = WIDE * lax.broadcasted_iota(jnp.int32, shape, 0) + at
    value = lanes_from(jnp.broadcast_to(row, shape), source)
    return jnp.concatenate([value] * (cols // LANES), axis=1)


def sideways(x, hop, strip_row, hop_row, span):
    groups, cols = x.shape
    lane = lane_of(x.shape)
    before = jnp.where(lane == 0, column_of(strip_row, groups, STEPS - 1, cols), turned(x, 1))
    after = jnp.where(lane == cols - 1, column_of(strip_row, groups, span + STEPS, cols), turned(x, -1))
    hop = jnp.broadcast_to(hop, x.shape)
    hop_before = jnp.where(lane == 0, hop_row[:, STEPS - 1 : STEPS], turned(hop, 1))
    return hop * after + hop_before * before


class Block:
    def __init__(self, probes, rows, cols):
        self.probes, self.rows, self.cols = probes, rows, cols
        self.groups = 2 * probes
        self.span = WIDE * self.groups
        self.tiles = cols // LANES
        self.tall = rows + 2 * TILE
        self.field_shape = (self.groups * self.tiles * self.tall, LANES)

    def at(self, g, c, row, count=TILE):
        return (pl.ds((g * self.tiles + c) * self.tall + TILE + row, count), slice(None))

    def across(self, c, row):
        return (pl.ds(c * self.tall + TILE + row, self.groups, stride=self.tiles * self.tall), slice(None))

    def gathered(self, ref, row):
        return jnp.concatenate([ref[self.across(c, row)] for c in range(self.tiles)], axis=1)

    def scattered(self, ref, row, value):
        for c in range(self.tiles):
            ref[self.across(c, row)] = value[:, c * LANES : (c + 1) * LANES]

    def hop_row(self, hops, kind, row):
        at = TILE + row
        return jnp.concatenate([hops[kind, c, at : at + 1, :] for c in range(self.tiles)], axis=1)


def lanes(c):
    return pl.ds(c * LANES, LANES)


def beside(block, strip_tile):
    lane = lane_of(strip_tile.shape)
    picked = (lax.rem(lane, WIDE) == STEPS - 1) & (lane < block.span)
    both = jnp.where(picked, strip_tile, turned(strip_tile, -(block.span + 2)))
    return [turned(both, -(WIDE * g + STEPS - 1)) for g in range(block.groups)]


def tile_step(block, row, now, hops, sides, previous, sign, store, add, columns=None):
    lane = lane_of((TILE, LANES))
    tiles = block.tiles
    for c in range(tiles) if columns is None else columns:
        at = pl.ds(TILE + row, TILE)
        hop_site, hop_after, hop_before, hop_under = (hops[kind, c, at, :] for kind in range(4))
        hop_over = hops[3, c, pl.ds(TILE + row - 1, TILE), :]
        sums = None
        for p in range(block.probes):
            kept = []
            for f in range(2):
                g = f * block.probes + p
                side = 0.0 if sides is None else sides[g]
                centre = now[block.at(g, c, row)]
                if c > 0:
                    before = turned(jnp.where(lane == LANES - 1, now[block.at(g, c - 1, row)], centre), 1)
                else:
                    before = jnp.where(lane == 0, side, turned(centre, 1))
                if c < tiles - 1:
                    after = turned(jnp.where(lane == 0, now[block.at(g, c + 1, row)], centre), -1)
                else:
                    after = jnp.where(lane == LANES - 1, side, turned(centre, -1))
                under = now[block.at(g, c, row + 1)]
                over = now[block.at(g, c, row - 1)]
                total = hop_site * centre - previous(f, p, c)
                total = total + (hop_after * after + hop_before * before)
                total = total + (hop_under * under + hop_over * over)
                if f == 0:
                    total = total + sign(p, c)
                store(f, p, c, total)
                kept.append((centre, after, under))
            if add is not None:
                (a_centre, a_after, a_under), (q_centre, q_after, q_under) = kept
                terms = (
                    a_centre * q_after + a_after * q_centre,
                    a_centre * q_under + a_under * q_centre,
                    a_centre * q_centre,
                )
                sums = terms if p == 0 else tuple(x + y for x, y in zip(sums, terms))
        if add is not None:
            add(c, *sums)


def force_adder(forces, row, first):
    def add(c, *sums):
        for kind, term in enumerate(sums):
            spot = (kind, pl.ds(row, TILE), lanes(c))
            forces[spot] = term if first else forces[spot] + term

    return add


def sign_reader(signs, weights, step, row):
    weight = jnp.broadcast_to(weights[0:1, step : step + 1], (TILE, LANES))
    return lambda p, c: weight * signs[p, pl.ds(row, TILE), lanes(c)].astype(jnp.float32)


def field_storer(block, target, row):
    def store(f, p, c, tile):
        target[block.at(f * block.probes + p, c, row)] = tile

    return store


def field_reader(block, source, row):
    return lambda f, p, c: source[block.at(f * block.probes + p, c, row)]


def block_reader(adj, fwd, row):
    return lambda f, p, c: (fwd if f else adj)[p, pl.ds(row, TILE), lanes(c)]


def block_storer(adj, fwd, row):
    def store(f, p, c, tile):
        (fwd if f else adj)[p, pl.ds(row, TILE), lanes(c)] = tile

    return store


def first_kernel(
    weights, x0, adj_next, fwd_next, signs, onsite, hop_right, hop_down, x0_out, x1, x2, hops, forces, messages
):
    block = Block(*signs.shape)
    rows = block.rows
    nothing = jnp.zeros((block.groups, block.cols), jnp.float32)
    for row in (-1, rows):
        for x in (x0_out, x1, x2):
            block.scattered(x, row, nothing)
    for side, lines in enumerate(((0, 1, 2), (rows - 1, rows - 2, rows - 3))):
        edge_rows(
            block,
            weights,
            x0,
            adj_next,
            fwd_next,
            signs,
            (onsite, hop_right, hop_down),
            lines,
            messages.at[side],
        )
    wide_lane = lane_of((rows, LANES))
    inside = pl.ds(TILE, rows)
    hop_before = 0.0
    for c in range(block.tiles):
        hop = hop_right[:, lanes(c)] * SCALE
        hop_turned = turned(hop, 1)
        hops[0, c, inside, :] = onsite[:, lanes(c)] * SCALE
        hops[1, c, inside, :] = hop
        hops[2, c, inside, :] = jnp.where(wide_lane == 0, hop_before, hop_turned)
        hops[3, c, inside, :] = hop_down[:, lanes(c)] * SCALE
        hops[3, c, pl.ds(TILE - 1, 1), :] = jnp.zeros((1, LANES), jnp.float32)
        hop_before = hop_turned
    for row in range(0, rows, TILE):
        tile_step(
            block,
            row,
            x0_out,
            hops,
            None,
            block_reader(adj_next, fwd_next, row),
            sign_reader(signs, weights, 0, row),
            field_storer(block, x1, row),
            force_adder(forces, row, True),
        )
    for row in range(0, rows, TILE):
        tile_step(
            block,
            row,
            x1,
            hops,
            None,
            field_reader(block, x0_out, row),
            sign_reader(signs, weights, 1, row),
            field_storer(block, x2, row),
            force_adder(forces, row, False),
            range(1, block.tiles - 1),
        )


def at_ends(block, row):
    return (
        column_of(row, block.groups, STEPS - 1, block.cols),
        column_of(row, block.groups, block.span + STEPS, block.cols),
    )


def send_kernel(own, left, right, messages, to_odd, to_even, message):
    rows, cols = own.shape[0], to_odd.shape[1]
    groups = (to_odd.shape[0] - TILE) // 3
    span = WIDE * groups
    misc = 3 * groups
    lane = lane_of((groups, LANES))
    left_part = lane_of((TILE, LANES)) < span
    message[...] = messages[...]
    for side, (edge, second) in enumerate(((0, 1), (TILE - 1, TILE - 2))):
        part = pl.ds(side * (rows - TILE), TILE)
        field, base, (s_on, s_right, s_down) = strips(own[part, :], left[part, :], right[part, :], span)
        before = turned(s_right, 1)
        level = base + s_on * field + s_right * turned(field, -1) + before * turned(field, 1)
        inward = jnp.where(left_part, s_right, before) * field
        down_inward = jnp.where(left_part, turned(s_down, -1), turned(s_down, 1))
        bond = min(edge, second)
        one = inward[edge : edge + 1, :]
        two = down_inward[bond : bond + 1, :] * inward[second : second + 1, :]
        for at, row in ((groups, one), (2 * groups, two)):
            for start, value, spot in (
                (0, column_of(row, groups, STEPS - 1), 0),
                (cols - LANES, column_of(row, groups, span + STEPS), LANES - 1),
            ):
                where = (side, pl.ds(at, groups), pl.ds(start, LANES))
                message[where] = message[where] + jnp.where(lane == spot, value, 0.0)
        message[side, misc + 3 : misc + 4, 0 : 4 * LANES] = jnp.concatenate(
            [
                field[edge : edge + 1, :],
                level[edge : edge + 1, :] + s_down[bond : bond + 1, :] * field[second : second + 1, :],
                s_down[edge : edge + 1, :],
                s_right[edge : edge + 1, :],
            ],
            axis=1,
        )
    odd = lax.rem(lax.axis_index("strip"), 2) == 1
    to_odd[...] = jnp.where(odd, message[1], message[0])
    to_even[...] = jnp.where(odd, message[0], message[1])


def strip_rows(block, strip, strip_base, strip_hops, step, row, count):
    here = pl.ds(TILE + row, count)
    now = strip[step, here, :]
    s_right = strip_hops[1, here, :]
    strip[step + 1, here, :] = (
        strip_base[step, pl.ds(row, count), :]
        + strip_hops[0, here, :] * now
        + s_right * turned(now, -1)
        + turned(s_right, 1) * turned(now, 1)
        + strip_hops[2, here, :] * strip[step, pl.ds(TILE + row + 1, count), :]
        + strip_hops[2, pl.ds(TILE + row - 1, count), :] * strip[step, pl.ds(TILE + row - 1, count), :]
    )


def inner_kernel(
    weights,
    x0,
    signs,
    own,
    left,
    right,
    sent,
    x1_in,
    x2_in,
    hops_in,
    forces_in,
    x1,
    x2,
    hops,
    forces,
    adj_out,
    fwd_out,
    strip,
    strip_base,
    strip_hops,
):
    del sent, x1_in, x2_in, hops_in, forces_in
    block = Block(*signs.shape)
    rows, tiles, probes = block.rows, block.tiles, block.probes
    inside = pl.ds(TILE, rows)
    lane = lane_of((TILE, LANES))
    for row in (TILE - 1, TILE + rows):
        strip_hops[2, row : row + 1, :] = jnp.zeros((1, LANES), jnp.float32)
        for step in range(2):
            strip[step, row : row + 1, :] = jnp.zeros((1, LANES), jnp.float32)
    field, base, (s_on, s_right, s_down) = strips(own[...], left[...], right[...], block.span)
    sign_strip = jnp.where(lane_of(base.shape) < block.span, turned(base, 2), turned(base, -2))
    strip[0, inside, :] = field
    strip_base[0] = base
    strip_base[1] = weights[0:1, 1:2] * sign_strip - field
    strip_hops[0, inside, :] = s_on
    strip_hops[1, inside, :] = s_right
    strip_hops[2, inside, :] = s_down

    last = tiles - 1
    for row in range(0, rows, TILE):
        at = pl.ds(TILE + row, TILE)
        sides = beside(block, strip[0, at, :])
        hop_first = turned(strip_hops[1, at, :], -(STEPS - 1))
        hops[2, 0, at, :] = jnp.where(lane == 0, hop_first, hops[2, 0, at, :])
        hop_last = hops[1, last, at, :]
        for g in range(block.groups):
            spot = block.at(g, 0, row)
            x1[spot] = x1[spot] + jnp.where(lane == 0, hop_first * sides[g], 0.0)
            spot = block.at(g, last, row)
            x1[spot] = x1[spot] + jnp.where(lane == LANES - 1, hop_last * sides[g], 0.0)
        total = None
        for p in range(probes):
            q = probes + p
            term = x0[block.at(p, last, row)] * sides[q] + sides[p] * x0[block.at(q, last, row)]
            total = term if total is None else total + term
        spot = (0, pl.ds(row, TILE), lanes(last))
        forces[spot] = forces[spot] + jnp.where(lane == LANES - 1, total, 0.0)

    for step in (1, 2):
        strip_rows(block, strip, strip_base, strip_hops, step - 1, 0, rows)
        now, before = (x1, x0) if step == 1 else (x2, x1)
        for row in range(0, rows, TILE):
            tile_step(
                block,
                row,
                now,
                hops,
                beside(block, strip[step, pl.ds(TILE + row, TILE), :]),
                field_reader(block, before, row),
                sign_reader(signs, weights, step, row),
                field_storer(block, x2, row) if step == 1 else block_storer(adj_out, fwd_out, row),
                force_adder(forces, row, False),
                sorted({0, last}) if step == 1 else None,
            )


def sorted_messages(received_odd, received_even, message):
    odd = lax.rem(lax.axis_index("strip"), 2) == 1
    message[0] = jnp.where(odd, received_even[...], received_odd[...])
    message[1] = jnp.where(odd, received_odd[...], received_even[...])
    return message.at[0], message.at[1]


def other_field(x):
    return pltpu.roll(x, x.shape[0] // 2, 0)


def outer_kernel(
    x0, x1, x2, hops, strip, strip_hops, received_odd, received_even, forces_in, adj_in, fwd_in, *refs
):
    del forces_in, adj_in, fwd_in
    forces, adj_out, fwd_out, message = refs
    probes, rows, cols = adj_out.shape
    block = Block(probes, rows, cols)
    groups, span = block.groups, block.span
    misc = 3 * groups
    lane = lane_of((groups, cols))
    messages = sorted_messages(received_odd, received_even, message)

    def s_line(ref, at, row):
        return ref[at, TILE + row : TILE + row + 1, :]

    def neighbours(x, strip_row):
        first, last = at_ends(block, strip_row)
        before = jnp.where(lane == 0, first, turned(x, 1))
        return before, jnp.where(lane == cols - 1, last, turned(x, -1))

    for side, source in enumerate(messages):
        edge, second, third = (0, 1, 2) if side == 0 else (rows - 1, rows - 2, rows - 3)
        bond, next_bond = (edge, second) if side == 0 else (second, third)
        corner = source[misc + 3 : misc + 4, 0 : 4 * LANES]
        c_field, c_one, c_down, c_right = (corner[:, k * LANES : (k + 1) * LANES] for k in range(4))
        hop_out = source[misc + 2 : misc + 3, :] if side == 0 else block.hop_row(hops, 3, edge)
        s_out = c_down if side == 0 else s_line(strip_hops, 2, edge)
        hop_in, hop_next = block.hop_row(hops, 3, bond), block.hop_row(hops, 3, next_bond)

        def across(x, pair, row):
            before, after = pair
            return (
                block.hop_row(hops, 0, row) * x
                + block.hop_row(hops, 1, row) * after
                + block.hop_row(hops, 2, row) * before
            )

        s_right = s_line(strip_hops, 1, edge)
        s_one_beyond = c_one + s_out * s_line(strip, 0, edge)
        s_one = s_out * c_field
        s_two = (
            s_line(strip_hops, 0, edge) * s_one
            + s_right * turned(s_one, -1)
            + turned(s_right, 1) * turned(s_one, 1)
            + s_out * s_one_beyond
        )
        s_two_second = s_line(strip_hops, 2, bond) * s_one

        x0_edge, x1_edge, x2_edge = (block.gathered(x, edge) for x in (x0, x1, x2))
        x1_second, x2_second = (block.gathered(x, second) for x in (x1, x2))
        x2_third = block.gathered(x2, third)
        x0_beyond = source[0:groups, :]
        one = hop_out * x0_beyond
        one_pair = neighbours(one, s_one)
        x1_beyond = source[groups : 2 * groups, :] + hop_out * x0_edge
        two = across(one, one_pair, edge) + hop_out * x1_beyond
        two_pair = neighbours(two, s_two)
        two_second = hop_in * one
        two_second_pair = neighbours(two_second, s_two_second)
        x1_new = x1_edge + one
        x2_beyond = (
            source[2 * groups : 3 * groups, :]
            + source[misc : misc + 1, :] * x1_beyond
            + sideways(x1_beyond, source[misc + 1 : misc + 2, :], s_one_beyond, c_right, span)
            + hop_out * x1_new
        )
        x2_new, x2_second_new = x2_edge + two, x2_second + two_second
        changes = (
            (edge, across(two, two_pair, edge) + hop_in * two_second + hop_out * x2_beyond - one),
            (second, across(two_second, two_second_pair, second) + hop_in * two),
            (third, hop_next * two_second),
        )
        for row, change in changes:
            adj_out[:, row, :] = adj_out[:, row, :] + change[:probes]
            fwd_out[:, row, :] = fwd_out[:, row, :] + change[probes:]

        def changed(x, change, new, other, other_change):
            return change * other_field(other) + x * other_field(other_change)

        def right_of(x, strip_row):
            return jnp.where(lane == cols - 1, column_of(strip_row, groups, span + STEPS, cols), turned(x, -1))

        one_right = right_of(x1_new, s_line(strip, 1, edge) + s_one)
        two_right = right_of(x2_new, s_line(strip, 2, edge) + s_two)
        second_right = right_of(x2_second_new, s_line(strip, 2, second) + s_two_second)
        terms = [
            (
                0,
                edge,
                changed(x1_edge, one, x1_new, one_right, one_pair[1])
                + changed(x2_edge, two, x2_new, two_right, two_pair[1]),
            ),
            (0, second, changed(x2_second, two_second, x2_second_new, second_right, two_second_pair[1])),
            (1, bond, changed(x2_edge, two, x2_new, x2_second_new, two_second) + one * other_field(x1_second)),
            (1, next_bond, two_second * other_field(x2_third)),
            (2, edge, 0.5 * (changed(x1_edge, one, x1_new, x1_new, one) + changed(x2_edge, two, x2_new, x2_new, two))),
            (2, second, 0.5 * changed(x2_second, two_second, x2_second_new, x2_second_new, two_second)),
        ]
        if side == 1:
            outward = (
                x0_edge * other_field(x0_beyond)
                + x1_new * other_field(x1_beyond)
                + x2_new * other_field(x2_beyond)
            )
            terms.append((1, edge, outward))
        for kind, row, term in terms:
            spot = (kind, pl.ds(row, 1), slice(None))
            forces[spot] = forces[spot] + jnp.sum(term, axis=0, keepdims=True)


def store_kernel(adj, fwd, adj_out, fwd_out, done):
    copies = []
    for source, target in ((adj, adj_out), (fwd, fwd_out)):
        for p in range(source.shape[0]):
            copies.append(pltpu.make_async_copy(source.at[p], target.at[p], done.at[len(copies)]))
            copies[-1].start()
    for each in copies:
        each.wait()


def sum_kernel(mine, other, right_out, down_out, site_out):
    for at, out in enumerate((right_out, down_out, site_out)):
        out[...] = (mine[at] + other[at]) * SCALE


def both_sides(x):
    left = shifted(x, "col", 1)
    return left, left if lax.axis_size("col") == 2 else shifted(x, "col", -1)


def in_vmem(*arrays):
    return tuple(pltpu.with_memory_space_constraint(v, pltpu.VMEM) for v in arrays)


def local(
    signs,
    onsite,
    hop_right,
    hop_down,
    moment_weights,
    forward_now,
    forward_next,
    adjoint_now,
    adjoint_next,
):
    probes, rows, cols = forward_now.shape
    block = Block(probes, rows, cols)
    groups, tiles, tall = block.groups, block.tiles, block.tall
    f32 = jnp.float32
    vmem = pl.BlockSpec(memory_space=pltpu.VMEM)
    hbm = pl.BlockSpec(memory_space=pltpu.HBM)
    params = pltpu.CompilerParams(vmem_limit_bytes=VMEM_LIMIT)

    def call(kernel, name, inputs, outs, scratch=(), aliases=None, flops=0, in_spec=vmem, out_spec=vmem):
        return pl.pallas_call(
            kernel,
            out_shape=outs,
            in_specs=[in_spec] * len(inputs),
            out_specs=(out_spec,) * len(outs),
            scratch_shapes=list(scratch),
            input_output_aliases=aliases or {},
            compiler_params=params,
            cost_estimate=pl.CostEstimate(flops=flops, bytes_accessed=flops, transcendentals=0),
            name=name,
        )(*inputs)

    def like(v, dtype=f32):
        return pltpu.VMEM(v.shape, dtype)

    sources = (
        moment_weights.reshape(1, STEPS),
        adjoint_now,
        forward_now,
        adjoint_next,
        forward_next,
        signs,
        onsite,
        hop_right,
        hop_down,
    )
    sources = tuple(pltpu.with_memory_space_constraint(v, pltpu.HBM) for v in sources)
    strip_tile = pltpu.VMEM((rows, LANES), f32)
    x0, adj_next, fwd_next, sign, on, hr, hd, weights, packed = call(
        load_kernel,
        "load",
        sources,
        (
            pltpu.VMEM((groups, tiles, tall, LANES), f32),
            like(adjoint_next),
            like(forward_next),
            like(signs, jnp.int32),
            like(onsite),
            like(hop_right),
            like(hop_down),
            pltpu.VMEM((1, STEPS), f32),
            strip_tile,
        ),
        [pltpu.SemaphoreType.DMA((13 + 2 * tiles,))],
        in_spec=hbm,
    )
    x0 = x0.reshape(block.field_shape)
    left, right = both_sides(packed)

    x0, adj_next, fwd_next, sign, on, hr, hd, weights, packed = in_vmem(
        x0, adj_next, fwd_next, sign, on, hr, hd, weights, packed
    )
    message = pltpu.VMEM((3 * groups + TILE, cols), f32)
    both_messages = pltpu.VMEM((2, 3 * groups + TILE, cols), f32)
    field = pltpu.VMEM(block.field_shape, f32)
    hops_shape = pltpu.VMEM((4, tiles, tall, LANES), f32)
    forces_shape = pltpu.VMEM((3, rows, cols), f32)
    x0, x1, x2, hops, forces, messages = call(
        first_kernel,
        "step_0",
        (weights, x0, adj_next, fwd_next, sign, on, hr, hd),
        (field, field, field, hops_shape, forces_shape, both_messages),
        aliases={1: 0},
        flops=COST,
    )

    x0, x1, x2, hops, forces = in_vmem(x0, x1, x2, hops, forces)
    messages, left, right = in_vmem(messages, left, right)
    to_odd, to_even = call(
        send_kernel, "edge_rows", (packed, left, right, messages), (message, message), [both_messages]
    )
    received_odd = pair_swap(to_odd, "strip", 1)
    received_even = pair_swap(to_even, "strip", 0)

    (sent,) = in_vmem(to_even)
    x1, x2, hops, forces, adj_out, fwd_out, strip, strip_base, strip_hops = call(
        inner_kernel,
        "inner_steps",
        (weights, x0, sign, packed, left, right, sent, x1, x2, hops, forces),
        (
            field,
            field,
            hops_shape,
            forces_shape,
            like(adjoint_now),
            like(forward_now),
            pltpu.VMEM((STEPS, tall, LANES), f32),
            pltpu.VMEM((2, rows, LANES), f32),
            pltpu.VMEM((3, tall, LANES), f32),
        ),
        aliases={7: 0, 8: 1, 9: 2, 10: 3},
        flops=COST,
    )

    kept = in_vmem(forces, adj_out, fwd_out)
    read = (x0,) + in_vmem(x1, x2, hops, strip, strip_hops, received_odd, received_even)
    forces, adjoint_out, forward_out = call(
        outer_kernel,
        "outer_rows",
        read + kept,
        tuple(like(v) for v in kept),
        [both_messages],
        aliases={len(read) + i: i for i in range(len(kept))},
        flops=COST,
    )

    other = shifted(forces, "probe", 1)
    whole = jax.ShapeDtypeStruct(adjoint_now.shape, f32)
    adjoint_out, forward_out = call(
        store_kernel,
        "store",
        in_vmem(adjoint_out, forward_out),
        (whole, whole),
        [pltpu.SemaphoreType.DMA((2 * probes,))],
        flops=COST,
        out_spec=hbm,
    )
    plain = jax.ShapeDtypeStruct((rows, cols), f32)
    right_force, down_force, site_force = call(
        sum_kernel, "force_sums", in_vmem(forces, other), (plain, plain, plain)
    )
    return right_force, down_force, site_force, forward_out, adjoint_out


def solution(mesh):
    placed = (
        P(("parts", "probe"), "strip", "col"),
        P(("parts", "strip"), "col"),
        P(("parts", "strip"), "col"),
        P(("parts", "strip"), "col"),
        P(),
        P(("parts", "probe"), "strip", "col"),
        P(("parts", "probe"), "strip", "col"),
        P(("parts", "probe"), "strip", "col"),
        P(("parts", "probe"), "strip", "col"),
    )
    return jax.shard_map(
        local,
        mesh=mesh,
        in_specs=placed,
        out_specs=(
            P(("parts", "strip"), "col"),
            P(("parts", "strip"), "col"),
            P(("parts", "strip"), "col"),
            P(("parts", "probe"), "strip", "col"),
            P(("parts", "probe"), "strip", "col"),
        ),
        check_vma=False,
    )
```

```python
import jax
import jax.numpy as jnp
from jax import lax
from jax.experimental import pallas as pl
from jax.experimental.pallas import tpu as pltpu
from jax.sharding import PartitionSpec as P

STEPS = 3
LANES = 128
TILE = 8
spectral_half = 7.5
SCALE = 2.0 / spectral_half

WIDE = 2 * STEPS
VMEM_LIMIT = 16 * 1024 * 1024
COST = 4_000_000


def shifted(x, axis, by):
    size = lax.axis_size(axis)
    return lax.ppermute(x, axis, [(i, (i + by) % size) for i in range(size)])


def lane_of(shape):
    return lax.broadcasted_iota(jnp.int32, shape, len(shape) - 1)


def lanes_from(x, source):
    return jnp.take_along_axis(x, source, axis=1, mode="promise_in_bounds")


def turned(x, by):
    return pltpu.roll(x, by % x.shape[1], 1)


def pack(shape, now, following, signs, lattice, weight):
    groups = len(now)
    span = WIDE * groups
    lane = lane_of(shape)

    def joined(pair):
        return jnp.where(lane < LANES // 2, pair[0], pair[1])

    packed = jnp.zeros(shape, jnp.float32)

    def put(packed, x, start):
        return jnp.where((lane >= start) & (lane < start + WIDE), turned(x, start + STEPS), packed)

    first, last = LANES - STEPS, STEPS - 1
    for g in range(groups):
        if g < len(signs):
            sign = joined(signs[g]).astype(jnp.float32)
            base = weight * sign - joined(following[g])
            base = jnp.where(lane == first, turned(sign, -2), jnp.where(lane == last, turned(sign, 2), base))
        else:
            base = jnp.where((lane == first) | (lane == last), 0.0, -joined(following[g]))
        packed = put(packed, joined(now[g]), WIDE * g)
        packed = put(packed, base, span + WIDE * g)
    for at, pair in enumerate(lattice):
        packed = put(packed, joined(pair), 2 * span + WIDE * at)
    return packed


def ends(ref, *at):
    cols = ref.shape[-1]
    return tuple(ref[(*at, slice(None), pl.ds(start, LANES))] for start in (0, cols - LANES))


def load_kernel(
    weights_in,
    adj_in,
    fwd_in,
    adj_next_in,
    fwd_next_in,
    signs_in,
    onsite_in,
    hop_right_in,
    hop_down_in,
    x0,
    adj_next,
    fwd_next,
    signs,
    onsite,
    hop_right,
    hop_down,
    weights,
    packed,
    done,
):
    probes, rows, cols = adj_in.shape
    groups = 2 * probes
    tiles = cols // LANES
    inside = pl.ds(TILE, rows)
    copies = []

    def copy(source, target):
        copies.append(pltpu.make_async_copy(source, target, done.at[len(copies)]))
        copies[-1].start()

    def copy_tile(c):
        for f, source in enumerate((adj_in, fwd_in)):
            copy(source.at[:, :, lanes(c)], x0.at[pl.ds(f * probes, probes), c, inside, :])

    def copy_lanes(start, count):
        part = pl.ds(start, count)
        for source, target in ((adj_next_in, adj_next), (fwd_next_in, fwd_next), (signs_in, signs)):
            copy(source.at[:, :, part], target.at[:, :, part])

    copy(weights_in, weights)
    for c in (0, tiles - 1):
        copy_tile(c)
        copy_lanes(c * LANES, LANES)
    copy(onsite_in, onsite)
    copy(hop_right_in, hop_right)
    copy(hop_down_in, hop_down)
    needed = len(copies)
    for c in range(1, tiles - 1):
        copy_tile(c)
    copy_lanes(LANES, cols - 2 * LANES)
    for at in range(needed):
        copies[at].wait()
    packed[...] = pack(
        packed.shape,
        [(x0[g, 0, inside, :], x0[g, tiles - 1, inside, :]) for g in range(groups)],
        [ends(ref, p) for ref in (adj_next, fwd_next) for p in range(probes)],
        [ends(signs, p) for p in range(probes)],
        [ends(ref) for ref in (onsite, hop_right, hop_down)],
        weights[0:1, 0:1],
    )
    for at in range(needed, len(copies)):
        copies[at].wait()


def edge_rows(block, weights, x0, adj_next, fwd_next, signs, lattice, lines, out):
    edge, second, third = lines
    groups, cols = block.groups, block.cols
    lane = lane_of((groups, cols))

    def next_rows(row):
        return jnp.concatenate([adj_next[:, row, :], fwd_next[:, row, :]], axis=0)

    def sign_rows(step, row):
        sign = weights[0:1, step : step + 1] * signs[:, row, :].astype(jnp.float32)
        return jnp.concatenate([sign, jnp.zeros_like(sign)], axis=0)

    def hop(kind, row):
        return lattice[kind][row : row + 1, :] * SCALE

    def across(x, row):
        right = jnp.broadcast_to(hop(1, row), x.shape)
        after = jnp.where(lane == cols - 1, 0.0, right * turned(x, -1))
        return hop(0, row) * x + after + jnp.where(lane == 0, 0.0, turned(right * x, 1))

    x_edge, x_second, x_third = (block.gathered(x0, row) for row in lines)
    down = hop(2, min(edge, second))
    one = (
        sign_rows(0, second)
        - next_rows(second)
        + across(x_second, second)
        + down * x_edge
        + hop(2, min(second, third)) * x_third
    )
    out[0:groups, :] = x_edge
    out[groups : 2 * groups, :] = (
        sign_rows(0, edge) - next_rows(edge) + across(x_edge, edge) + down * x_second
    )
    out[2 * groups : 3 * groups, :] = sign_rows(1, edge) - x_edge + down * one
    misc = 3 * groups
    for kind in range(3):
        out[misc + kind : misc + kind + 1, :] = hop(kind, edge)
    out[misc + 3 : misc + TILE, :] = jnp.zeros((TILE - 3, cols), jnp.float32)


def strips(own, left, right, span):
    lane = lane_of(own.shape)
    inner = lax.rem(lane, WIDE) < STEPS
    low = jnp.where(inner, left, own)
    high = jnp.where(inner, own, right)
    below = lane < span
    field = jnp.where(below, low, turned(high, span))
    base = jnp.where(below, turned(low, -span), high)
    coefficients = []
    for at in range(3):
        source = 2 * span + WIDE * at + lax.rem(lane, WIDE)
        coefficients.append(jnp.where(below, lanes_from(low, source), lanes_from(high, source)) * SCALE)
    return field, base, coefficients


def column_of(row, groups, at, cols=LANES):
    shape = (groups, LANES)
    source = WIDE * lax.broadcasted_iota(jnp.int32, shape, 0) + at
    value = lanes_from(jnp.broadcast_to(row, shape), source)
    return jnp.concatenate([value] * (cols // LANES), axis=1)


def sideways(x, hop, strip_row, hop_row, span):
    groups, cols = x.shape
    lane = lane_of(x.shape)
    before = jnp.where(lane == 0, column_of(strip_row, groups, STEPS - 1, cols), turned(x, 1))
    after = jnp.where(lane == cols - 1, column_of(strip_row, groups, span + STEPS, cols), turned(x, -1))
    hop = jnp.broadcast_to(hop, x.shape)
    hop_before = jnp.where(lane == 0, hop_row[:, STEPS - 1 : STEPS], turned(hop, 1))
    return hop * after + hop_before * before


class Block:
    def __init__(self, probes, rows, cols):
        self.probes, self.rows, self.cols = probes, rows, cols
        self.groups = 2 * probes
        self.span = WIDE * self.groups
        self.tiles = cols // LANES
        self.tall = rows + 2 * TILE
        self.field_shape = (self.groups * self.tiles * self.tall, LANES)

    def at(self, g, c, row, count=TILE):
        return (pl.ds((g * self.tiles + c) * self.tall + TILE + row, count), slice(None))

    def across(self, c, row):
        return (pl.ds(c * self.tall + TILE + row, self.groups, stride=self.tiles * self.tall), slice(None))

    def gathered(self, ref, row):
        return jnp.concatenate([ref[self.across(c, row)] for c in range(self.tiles)], axis=1)

    def scattered(self, ref, row, value):
        for c in range(self.tiles):
            ref[self.across(c, row)] = value[:, c * LANES : (c + 1) * LANES]

    def hop_row(self, hops, kind, row):
        at = TILE + row
        return jnp.concatenate([hops[kind, c, at : at + 1, :] for c in range(self.tiles)], axis=1)


def lanes(c):
    return pl.ds(c * LANES, LANES)


def beside(block, strip_tile):
    lane = lane_of(strip_tile.shape)
    picked = (lax.rem(lane, WIDE) == STEPS - 1) & (lane < block.span)
    both = jnp.where(picked, strip_tile, turned(strip_tile, -(block.span + 2)))
    return [turned(both, -(WIDE * g + STEPS - 1)) for g in range(block.groups)]


def tile_step(block, row, now, hops, sides, previous, sign, store, add, columns=None):
    lane = lane_of((TILE, LANES))
    tiles = block.tiles
    for c in range(tiles) if columns is None else columns:
        at = pl.ds(TILE + row, TILE)
        hop_site, hop_after, hop_before, hop_under = (hops[kind, c, at, :] for kind in range(4))
        hop_over = hops[3, c, pl.ds(TILE + row - 1, TILE), :]
        sums = None
        for p in range(block.probes):
            kept = []
            for f in range(2):
                g = f * block.probes + p
                side = 0.0 if sides is None else sides[g]
                centre = now[block.at(g, c, row)]
                if c > 0:
                    before = turned(jnp.where(lane == LANES - 1, now[block.at(g, c - 1, row)], centre), 1)
                else:
                    before = jnp.where(lane == 0, side, turned(centre, 1))
                if c < tiles - 1:
                    after = turned(jnp.where(lane == 0, now[block.at(g, c + 1, row)], centre), -1)
                else:
                    after = jnp.where(lane == LANES - 1, side, turned(centre, -1))
                under = now[block.at(g, c, row + 1)]
                over = now[block.at(g, c, row - 1)]
                total = hop_site * centre - previous(f, p, c)
                total = total + (hop_after * after + hop_before * before)
                total = total + (hop_under * under + hop_over * over)
                if f == 0:
                    total = total + sign(p, c)
                store(f, p, c, total)
                kept.append((centre, after, under))
            if add is not None:
                (a_centre, a_after, a_under), (q_centre, q_after, q_under) = kept
                terms = (
                    a_centre * q_after + a_after * q_centre,
                    a_centre * q_under + a_under * q_centre,
                    a_centre * q_centre,
                )
                sums = terms if p == 0 else tuple(x + y for x, y in zip(sums, terms))
        if add is not None:
            add(c, *sums)


def force_adder(forces, row, first):
    def add(c, *sums):
        for kind, term in enumerate(sums):
            spot = (kind, pl.ds(row, TILE), lanes(c))
            forces[spot] = term if first else forces[spot] + term

    return add


def sign_reader(signs, weights, step, row):
    weight = jnp.broadcast_to(weights[0:1, step : step + 1], (TILE, LANES))
    return lambda p, c: weight * signs[p, pl.ds(row, TILE), lanes(c)].astype(jnp.float32)


def field_storer(block, target, row):
    def store(f, p, c, tile):
        target[block.at(f * block.probes + p, c, row)] = tile

    return store


def field_reader(block, source, row):
    return lambda f, p, c: source[block.at(f * block.probes + p, c, row)]


def block_reader(adj, fwd, row):
    return lambda f, p, c: (fwd if f else adj)[p, pl.ds(row, TILE), lanes(c)]


def block_storer(adj, fwd, row):
    def store(f, p, c, tile):
        (fwd if f else adj)[p, pl.ds(row, TILE), lanes(c)] = tile

    return store


def first_kernel(
    weights, x0, adj_next, fwd_next, signs, onsite, hop_right, hop_down, x0_out, x1, x2, hops, forces, messages
):
    block = Block(*signs.shape)
    rows = block.rows
    nothing = jnp.zeros((block.groups, block.cols), jnp.float32)
    for row in (-1, rows):
        for x in (x0_out, x1, x2):
            block.scattered(x, row, nothing)
    for side, lines in enumerate(((0, 1, 2), (rows - 1, rows - 2, rows - 3))):
        edge_rows(
            block,
            weights,
            x0,
            adj_next,
            fwd_next,
            signs,
            (onsite, hop_right, hop_down),
            lines,
            messages.at[side],
        )
    wide_lane = lane_of((rows, LANES))
    inside = pl.ds(TILE, rows)
    hop_before = 0.0
    for c in range(block.tiles):
        hop = hop_right[:, lanes(c)] * SCALE
        hop_turned = turned(hop, 1)
        hops[0, c, inside, :] = onsite[:, lanes(c)] * SCALE
        hops[1, c, inside, :] = hop
        hops[2, c, inside, :] = jnp.where(wide_lane == 0, hop_before, hop_turned)
        hops[3, c, inside, :] = hop_down[:, lanes(c)] * SCALE
        hops[3, c, pl.ds(TILE - 1, 1), :] = jnp.zeros((1, LANES), jnp.float32)
        hop_before = hop_turned
    for row in range(0, rows, TILE):
        tile_step(
            block,
            row,
            x0_out,
            hops,
            None,
            block_reader(adj_next, fwd_next, row),
            sign_reader(signs, weights, 0, row),
            field_storer(block, x1, row),
            force_adder(forces, row, True),
        )
    for row in range(0, rows, TILE):
        tile_step(
            block,
            row,
            x1,
            hops,
            None,
            field_reader(block, x0_out, row),
            sign_reader(signs, weights, 1, row),
            field_storer(block, x2, row),
            force_adder(forces, row, False),
            range(1, block.tiles - 1),
        )


def at_ends(block, row):
    return (
        column_of(row, block.groups, STEPS - 1, block.cols),
        column_of(row, block.groups, block.span + STEPS, block.cols),
    )


def send_kernel(own, left, right, messages, to_above, to_below):
    rows, cols = own.shape[0], to_above.shape[1]
    groups = (to_above.shape[0] - TILE) // 3
    span = WIDE * groups
    misc = 3 * groups
    lane = lane_of((groups, LANES))
    left_part = lane_of((TILE, LANES)) < span
    for side, (edge, second) in enumerate(((0, 1), (TILE - 1, TILE - 2))):
        message = (to_above, to_below)[side]
        message[...] = messages[side]
        part = pl.ds(side * (rows - TILE), TILE)
        field, base, (s_on, s_right, s_down) = strips(own[part, :], left[part, :], right[part, :], span)
        before = turned(s_right, 1)
        level = base + s_on * field + s_right * turned(field, -1) + before * turned(field, 1)
        inward = jnp.where(left_part, s_right, before) * field
        down_inward = jnp.where(left_part, turned(s_down, -1), turned(s_down, 1))
        bond = min(edge, second)
        one = inward[edge : edge + 1, :]
        two = down_inward[bond : bond + 1, :] * inward[second : second + 1, :]
        for at, row in ((groups, one), (2 * groups, two)):
            for start, value, spot in (
                (0, column_of(row, groups, STEPS - 1), 0),
                (cols - LANES, column_of(row, groups, span + STEPS), LANES - 1),
            ):
                where = (pl.ds(at, groups), pl.ds(start, LANES))
                message[where] = message[where] + jnp.where(lane == spot, value, 0.0)
        message[misc + 3 : misc + 4, 0 : 4 * LANES] = jnp.concatenate(
            [
                field[edge : edge + 1, :],
                level[edge : edge + 1, :] + s_down[bond : bond + 1, :] * field[second : second + 1, :],
                s_down[edge : edge + 1, :],
                s_right[edge : edge + 1, :],
            ],
            axis=1,
        )


def strip_rows(block, strip, strip_base, strip_hops, step, row, count):
    here = pl.ds(TILE + row, count)
    now = strip[step, here, :]
    s_right = strip_hops[1, here, :]
    strip[step + 1, here, :] = (
        strip_base[step, pl.ds(row, count), :]
        + strip_hops[0, here, :] * now
        + s_right * turned(now, -1)
        + turned(s_right, 1) * turned(now, 1)
        + strip_hops[2, here, :] * strip[step, pl.ds(TILE + row + 1, count), :]
        + strip_hops[2, pl.ds(TILE + row - 1, count), :] * strip[step, pl.ds(TILE + row - 1, count), :]
    )


def inner_kernel(
    weights,
    x0,
    signs,
    own,
    left,
    right,
    sent,
    x1_in,
    x2_in,
    hops_in,
    forces_in,
    x1,
    x2,
    hops,
    forces,
    adj_out,
    fwd_out,
    strip,
    strip_base,
    strip_hops,
):
    del sent, x1_in, x2_in, hops_in, forces_in
    block = Block(*signs.shape)
    rows, tiles, probes = block.rows, block.tiles, block.probes
    inside = pl.ds(TILE, rows)
    lane = lane_of((TILE, LANES))
    for row in (TILE - 1, TILE + rows):
        strip_hops[2, row : row + 1, :] = jnp.zeros((1, LANES), jnp.float32)
        for step in range(2):
            strip[step, row : row + 1, :] = jnp.zeros((1, LANES), jnp.float32)
    field, base, (s_on, s_right, s_down) = strips(own[...], left[...], right[...], block.span)
    sign_strip = jnp.where(lane_of(base.shape) < block.span, turned(base, 2), turned(base, -2))
    strip[0, inside, :] = field
    strip_base[0] = base
    strip_base[1] = weights[0:1, 1:2] * sign_strip - field
    strip_hops[0, inside, :] = s_on
    strip_hops[1, inside, :] = s_right
    strip_hops[2, inside, :] = s_down

    last = tiles - 1
    for row in range(0, rows, TILE):
        at = pl.ds(TILE + row, TILE)
        sides = beside(block, strip[0, at, :])
        hop_first = turned(strip_hops[1, at, :], -(STEPS - 1))
        hops[2, 0, at, :] = jnp.where(lane == 0, hop_first, hops[2, 0, at, :])
        hop_last = hops[1, last, at, :]
        for g in range(block.groups):
            spot = block.at(g, 0, row)
            x1[spot] = x1[spot] + jnp.where(lane == 0, hop_first * sides[g], 0.0)
            spot = block.at(g, last, row)
            x1[spot] = x1[spot] + jnp.where(lane == LANES - 1, hop_last * sides[g], 0.0)
        total = None
        for p in range(probes):
            q = probes + p
            term = x0[block.at(p, last, row)] * sides[q] + sides[p] * x0[block.at(q, last, row)]
            total = term if total is None else total + term
        spot = (0, pl.ds(row, TILE), lanes(last))
        forces[spot] = forces[spot] + jnp.where(lane == LANES - 1, total, 0.0)

    for step in (1, 2):
        strip_rows(block, strip, strip_base, strip_hops, step - 1, 0, rows)
        now, before = (x1, x0) if step == 1 else (x2, x1)
        for row in range(0, rows, TILE):
            tile_step(
                block,
                row,
                now,
                hops,
                beside(block, strip[step, pl.ds(TILE + row, TILE), :]),
                field_reader(block, before, row),
                sign_reader(signs, weights, step, row),
                field_storer(block, x2, row) if step == 1 else block_storer(adj_out, fwd_out, row),
                force_adder(forces, row, False),
                sorted({0, last}) if step == 1 else None,
            )


def other_field(x):
    return pltpu.roll(x, x.shape[0] // 2, 0)


def outer_kernel(
    x0, x1, x2, hops, strip, strip_hops, above, below, forces_in, adj_in, fwd_in, *refs
):
    del forces_in, adj_in, fwd_in
    forces, adj_out, fwd_out = refs
    probes, rows, cols = adj_out.shape
    block = Block(probes, rows, cols)
    groups, span = block.groups, block.span
    misc = 3 * groups
    lane = lane_of((groups, cols))

    def s_line(ref, at, row):
        return ref[at, TILE + row : TILE + row + 1, :]

    def neighbours(x, strip_row):
        first, last = at_ends(block, strip_row)
        before = jnp.where(lane == 0, first, turned(x, 1))
        return before, jnp.where(lane == cols - 1, last, turned(x, -1))

    for side, source in enumerate((above, below)):
        edge, second, third = (0, 1, 2) if side == 0 else (rows - 1, rows - 2, rows - 3)
        bond, next_bond = (edge, second) if side == 0 else (second, third)
        corner = source[misc + 3 : misc + 4, 0 : 4 * LANES]
        c_field, c_one, c_down, c_right = (corner[:, k * LANES : (k + 1) * LANES] for k in range(4))
        hop_out = source[misc + 2 : misc + 3, :] if side == 0 else block.hop_row(hops, 3, edge)
        s_out = c_down if side == 0 else s_line(strip_hops, 2, edge)
        hop_in, hop_next = block.hop_row(hops, 3, bond), block.hop_row(hops, 3, next_bond)

        def across(x, pair, row):
            before, after = pair
            return (
                block.hop_row(hops, 0, row) * x
                + block.hop_row(hops, 1, row) * after
                + block.hop_row(hops, 2, row) * before
            )

        s_right = s_line(strip_hops, 1, edge)
        s_one_beyond = c_one + s_out * s_line(strip, 0, edge)
        s_one = s_out * c_field
        s_two = (
            s_line(strip_hops, 0, edge) * s_one
            + s_right * turned(s_one, -1)
            + turned(s_right, 1) * turned(s_one, 1)
            + s_out * s_one_beyond
        )
        s_two_second = s_line(strip_hops, 2, bond) * s_one

        x0_edge, x1_edge, x2_edge = (block.gathered(x, edge) for x in (x0, x1, x2))
        x1_second, x2_second = (block.gathered(x, second) for x in (x1, x2))
        x2_third = block.gathered(x2, third)
        x0_beyond = source[0:groups, :]
        one = hop_out * x0_beyond
        one_pair = neighbours(one, s_one)
        x1_beyond = source[groups : 2 * groups, :] + hop_out * x0_edge
        two = across(one, one_pair, edge) + hop_out * x1_beyond
        two_pair = neighbours(two, s_two)
        two_second = hop_in * one
        two_second_pair = neighbours(two_second, s_two_second)
        x1_new = x1_edge + one
        x2_beyond = (
            source[2 * groups : 3 * groups, :]
            + source[misc : misc + 1, :] * x1_beyond
            + sideways(x1_beyond, source[misc + 1 : misc + 2, :], s_one_beyond, c_right, span)
            + hop_out * x1_new
        )
        x2_new, x2_second_new = x2_edge + two, x2_second + two_second
        changes = (
            (edge, across(two, two_pair, edge) + hop_in * two_second + hop_out * x2_beyond - one),
            (second, across(two_second, two_second_pair, second) + hop_in * two),
            (third, hop_next * two_second),
        )
        for row, change in changes:
            adj_out[:, row, :] = adj_out[:, row, :] + change[:probes]
            fwd_out[:, row, :] = fwd_out[:, row, :] + change[probes:]

        def changed(x, change, new, other, other_change):
            return change * other_field(other) + x * other_field(other_change)

        def right_of(x, strip_row):
            return jnp.where(lane == cols - 1, column_of(strip_row, groups, span + STEPS, cols), turned(x, -1))

        one_right = right_of(x1_new, s_line(strip, 1, edge) + s_one)
        two_right = right_of(x2_new, s_line(strip, 2, edge) + s_two)
        second_right = right_of(x2_second_new, s_line(strip, 2, second) + s_two_second)
        terms = [
            (
                0,
                edge,
                changed(x1_edge, one, x1_new, one_right, one_pair[1])
                + changed(x2_edge, two, x2_new, two_right, two_pair[1]),
            ),
            (0, second, changed(x2_second, two_second, x2_second_new, second_right, two_second_pair[1])),
            (1, bond, changed(x2_edge, two, x2_new, x2_second_new, two_second) + one * other_field(x1_second)),
            (1, next_bond, two_second * other_field(x2_third)),
            (2, edge, 0.5 * (changed(x1_edge, one, x1_new, x1_new, one) + changed(x2_edge, two, x2_new, x2_new, two))),
            (2, second, 0.5 * changed(x2_second, two_second, x2_second_new, x2_second_new, two_second)),
        ]
        if side == 1:
            outward = (
                x0_edge * other_field(x0_beyond)
                + x1_new * other_field(x1_beyond)
                + x2_new * other_field(x2_beyond)
            )
            terms.append((1, edge, outward))
        for kind, row, term in terms:
            spot = (kind, pl.ds(row, 1), slice(None))
            forces[spot] = forces[spot] + jnp.sum(term, axis=0, keepdims=True)


def store_kernel(adj, fwd, adj_out, fwd_out, done):
    copies = []
    for source, target in ((adj, adj_out), (fwd, fwd_out)):
        for p in range(source.shape[0]):
            copies.append(pltpu.make_async_copy(source.at[p], target.at[p], done.at[len(copies)]))
            copies[-1].start()
    for each in copies:
        each.wait()


def sum_kernel(mine, other, right_out, down_out, site_out):
    for at, out in enumerate((right_out, down_out, site_out)):
        out[...] = (mine[at] + other[at]) * SCALE


def both_sides(x):
    left = shifted(x, "col", 1)
    return left, left if lax.axis_size("col") == 2 else shifted(x, "col", -1)


def in_vmem(*arrays):
    return tuple(pltpu.with_memory_space_constraint(v, pltpu.VMEM) for v in arrays)


def local(
    signs,
    onsite,
    hop_right,
    hop_down,
    moment_weights,
    forward_now,
    forward_next,
    adjoint_now,
    adjoint_next,
):
    probes, rows, cols = forward_now.shape
    block = Block(probes, rows, cols)
    groups, tiles, tall = block.groups, block.tiles, block.tall
    f32 = jnp.float32
    vmem = pl.BlockSpec(memory_space=pltpu.VMEM)
    hbm = pl.BlockSpec(memory_space=pltpu.HBM)
    params = pltpu.CompilerParams(vmem_limit_bytes=VMEM_LIMIT)

    def call(kernel, name, inputs, outs, scratch=(), aliases=None, flops=0, in_spec=vmem, out_spec=vmem):
        return pl.pallas_call(
            kernel,
            out_shape=outs,
            in_specs=[in_spec] * len(inputs),
            out_specs=(out_spec,) * len(outs),
            scratch_shapes=list(scratch),
            input_output_aliases=aliases or {},
            compiler_params=params,
            cost_estimate=pl.CostEstimate(flops=flops, bytes_accessed=flops, transcendentals=0),
            name=name,
        )(*inputs)

    def like(v, dtype=f32):
        return pltpu.VMEM(v.shape, dtype)

    sources = (
        moment_weights.reshape(1, STEPS),
        adjoint_now,
        forward_now,
        adjoint_next,
        forward_next,
        signs,
        onsite,
        hop_right,
        hop_down,
    )
    sources = tuple(pltpu.with_memory_space_constraint(v, pltpu.HBM) for v in sources)
    strip_tile = pltpu.VMEM((rows, LANES), f32)
    x0, adj_next, fwd_next, sign, on, hr, hd, weights, packed = call(
        load_kernel,
        "load",
        sources,
        (
            pltpu.VMEM((groups, tiles, tall, LANES), f32),
            like(adjoint_next),
            like(forward_next),
            like(signs, jnp.int32),
            like(onsite),
            like(hop_right),
            like(hop_down),
            pltpu.VMEM((1, STEPS), f32),
            strip_tile,
        ),
        [pltpu.SemaphoreType.DMA((13 + 2 * tiles,))],
        in_spec=hbm,
    )
    x0 = x0.reshape(block.field_shape)
    left, right = both_sides(packed)

    x0, adj_next, fwd_next, sign, on, hr, hd, weights, packed = in_vmem(
        x0, adj_next, fwd_next, sign, on, hr, hd, weights, packed
    )
    message = pltpu.VMEM((3 * groups + TILE, cols), f32)
    both_messages = pltpu.VMEM((2, 3 * groups + TILE, cols), f32)
    field = pltpu.VMEM(block.field_shape, f32)
    hops_shape = pltpu.VMEM((4, tiles, tall, LANES), f32)
    forces_shape = pltpu.VMEM((3, rows, cols), f32)
    x0, x1, x2, hops, forces, messages = call(
        first_kernel,
        "step_0",
        (weights, x0, adj_next, fwd_next, sign, on, hr, hd),
        (field, field, field, hops_shape, forces_shape, both_messages),
        aliases={1: 0},
        flops=COST,
    )

    x0, x1, x2, hops, forces = in_vmem(x0, x1, x2, hops, forces)
    messages, left, right = in_vmem(messages, left, right)
    to_above, to_below = call(
        send_kernel, "edge_rows", (packed, left, right, messages), (message, message)
    )
    above = shifted(to_below, "strip", 1)
    below = shifted(to_above, "strip", -1)

    (sent,) = in_vmem(to_above)
    x1, x2, hops, forces, adj_out, fwd_out, strip, strip_base, strip_hops = call(
        inner_kernel,
        "inner_steps",
        (weights, x0, sign, packed, left, right, sent, x1, x2, hops, forces),
        (
            field,
            field,
            hops_shape,
            forces_shape,
            like(adjoint_now),
            like(forward_now),
            pltpu.VMEM((STEPS, tall, LANES), f32),
            pltpu.VMEM((2, rows, LANES), f32),
            pltpu.VMEM((3, tall, LANES), f32),
        ),
        aliases={7: 0, 8: 1, 9: 2, 10: 3},
        flops=COST,
    )

    kept = in_vmem(forces, adj_out, fwd_out)
    read = (x0,) + in_vmem(x1, x2, hops, strip, strip_hops, above, below)
    forces, adjoint_out, forward_out = call(
        outer_kernel,
        "outer_rows",
        read + kept,
        tuple(like(v) for v in kept),
        aliases={len(read) + i: i for i in range(len(kept))},
        flops=COST,
    )

    other = shifted(forces, "probe", 1)
    whole = jax.ShapeDtypeStruct(adjoint_now.shape, f32)
    adjoint_out, forward_out = call(
        store_kernel,
        "store",
        in_vmem(adjoint_out, forward_out),
        (whole, whole),
        [pltpu.SemaphoreType.DMA((2 * probes,))],
        flops=COST,
        out_spec=hbm,
    )
    plain = jax.ShapeDtypeStruct((rows, cols), f32)
    right_force, down_force, site_force = call(
        sum_kernel, "force_sums", in_vmem(forces, other), (plain, plain, plain)
    )
    return right_force, down_force, site_force, forward_out, adjoint_out


def solution(mesh):
    placed = (
        P(("parts", "probe"), "strip", "col"),
        P(("parts", "strip"), "col"),
        P(("parts", "strip"), "col"),
        P(("parts", "strip"), "col"),
        P(),
        P(("parts", "probe"), "strip", "col"),
        P(("parts", "probe"), "strip", "col"),
        P(("parts", "probe"), "strip", "col"),
        P(("parts", "probe"), "strip", "col"),
    )
    return jax.shard_map(
        local,
        mesh=mesh,
        in_specs=placed,
        out_specs=(
            P(("parts", "strip"), "col"),
            P(("parts", "strip"), "col"),
            P(("parts", "strip"), "col"),
            P(("parts", "probe"), "strip", "col"),
            P(("parts", "probe"), "strip", "col"),
        ),
        check_vma=False,
    )
```

```python
import jax
import jax.numpy as jnp
from jax import lax
from jax.experimental import pallas as pl
from jax.experimental.pallas import tpu as pltpu
from jax.sharding import PartitionSpec as P

STEPS = 3
LANES = 128
TILE = 8
spectral_half = 7.5
SCALE = 2.0 / spectral_half

WIDE = 2 * STEPS
VMEM_LIMIT = 16 * 1024 * 1024
COST = 4_000_000


def shifted(x, axis, by):
    size = lax.axis_size(axis)
    return lax.ppermute(x, axis, [(i, (i + by) % size) for i in range(size)])


def lane_of(shape):
    return lax.broadcasted_iota(jnp.int32, shape, len(shape) - 1)


def lanes_from(x, source):
    return jnp.take_along_axis(x, source, axis=1, mode="promise_in_bounds")


def turned(x, by):
    return pltpu.roll(x, by % x.shape[1], 1)


def pack(shape, now, following, signs, lattice, weight):
    groups = len(now)
    span = WIDE * groups
    lane = lane_of(shape)

    def joined(pair):
        return jnp.where(lane < LANES // 2, pair[0], pair[1])

    packed = jnp.zeros(shape, jnp.float32)

    def put(packed, x, start):
        return jnp.where((lane >= start) & (lane < start + WIDE), turned(x, start + STEPS), packed)

    first, last = LANES - STEPS, STEPS - 1
    for g in range(groups):
        if g < len(signs):
            sign = joined(signs[g]).astype(jnp.float32)
            base = weight * sign - joined(following[g])
            base = jnp.where(lane == first, turned(sign, -2), jnp.where(lane == last, turned(sign, 2), base))
        else:
            base = jnp.where((lane == first) | (lane == last), 0.0, -joined(following[g]))
        packed = put(packed, joined(now[g]), WIDE * g)
        packed = put(packed, base, span + WIDE * g)
    for at, pair in enumerate(lattice):
        packed = put(packed, joined(pair), 2 * span + WIDE * at)
    return packed


def ends(ref, *at):
    cols = ref.shape[-1]
    return tuple(ref[(*at, slice(None), pl.ds(start, LANES))] for start in (0, cols - LANES))


def load_kernel(
    weights_in,
    adj_in,
    fwd_in,
    adj_next_in,
    fwd_next_in,
    signs_in,
    onsite_in,
    hop_right_in,
    hop_down_in,
    x0,
    adj_next,
    fwd_next,
    signs,
    onsite,
    hop_right,
    hop_down,
    weights,
    packed,
    done,
):
    probes, rows, cols = adj_in.shape
    groups = 2 * probes
    tiles = cols // LANES
    inside = pl.ds(TILE, rows)
    copies = []

    def copy(source, target):
        copies.append(pltpu.make_async_copy(source, target, done.at[len(copies)]))
        copies[-1].start()

    def copy_tile(c):
        for f, source in enumerate((adj_in, fwd_in)):
            copy(source.at[:, :, lanes(c)], x0.at[pl.ds(f * probes, probes), c, inside, :])

    def copy_lanes(start, count):
        part = pl.ds(start, count)
        for source, target in ((adj_next_in, adj_next), (fwd_next_in, fwd_next), (signs_in, signs)):
            copy(source.at[:, :, part], target.at[:, :, part])

    copy(weights_in, weights)
    for c in (0, tiles - 1):
        copy_tile(c)
        copy_lanes(c * LANES, LANES)
    copy(onsite_in, onsite)
    copy(hop_right_in, hop_right)
    copy(hop_down_in, hop_down)
    needed = len(copies)
    for c in range(1, tiles - 1):
        copy_tile(c)
    copy_lanes(LANES, cols - 2 * LANES)
    for at in range(needed):
        copies[at].wait()
    packed[...] = pack(
        packed.shape,
        [(x0[g, 0, inside, :], x0[g, tiles - 1, inside, :]) for g in range(groups)],
        [ends(ref, p) for ref in (adj_next, fwd_next) for p in range(probes)],
        [ends(signs, p) for p in range(probes)],
        [ends(ref) for ref in (onsite, hop_right, hop_down)],
        weights[0:1, 0:1],
    )
    for at in range(needed, len(copies)):
        copies[at].wait()


def edge_rows(block, weights, x0, adj_next, fwd_next, signs, lattice, lines, out):
    edge, second, third = lines
    groups, cols = block.groups, block.cols
    lane = lane_of((groups, cols))

    def next_rows(row):
        return jnp.concatenate([adj_next[:, row, :], fwd_next[:, row, :]], axis=0)

    def sign_rows(step, row):
        sign = weights[0:1, step : step + 1] * signs[:, row, :].astype(jnp.float32)
        return jnp.concatenate([sign, jnp.zeros_like(sign)], axis=0)

    def hop(kind, row):
        return lattice[kind][row : row + 1, :] * SCALE

    def across(x, row):
        right = jnp.broadcast_to(hop(1, row), x.shape)
        after = jnp.where(lane == cols - 1, 0.0, right * turned(x, -1))
        return hop(0, row) * x + after + jnp.where(lane == 0, 0.0, turned(right * x, 1))

    x_edge, x_second, x_third = (block.gathered(x0, row) for row in lines)
    down = hop(2, min(edge, second))
    one = (
        sign_rows(0, second)
        - next_rows(second)
        + across(x_second, second)
        + down * x_edge
        + hop(2, min(second, third)) * x_third
    )
    out[0:groups, :] = x_edge
    out[groups : 2 * groups, :] = (
        sign_rows(0, edge) - next_rows(edge) + across(x_edge, edge) + down * x_second
    )
    out[2 * groups : 3 * groups, :] = sign_rows(1, edge) - x_edge + down * one
    misc = 3 * groups
    for kind in range(3):
        out[misc + kind : misc + kind + 1, :] = hop(kind, edge)
    out[misc + 3 : misc + TILE, :] = jnp.zeros((TILE - 3, cols), jnp.float32)


def strips(own, left, right, span):
    lane = lane_of(own.shape)
    within = lane - WIDE * ((lane * (256 // WIDE + 1)) >> 8)
    inner = within < STEPS
    low = jnp.where(inner, left, own)
    high = jnp.where(inner, own, right)
    below = lane < span
    field = jnp.where(below, low, turned(high, span))
    base = jnp.where(below, turned(low, -span), high)
    coefficients = []
    for at in range(3):
        source = 2 * span + WIDE * at + within
        coefficients.append(jnp.where(below, lanes_from(low, source), lanes_from(high, source)) * SCALE)
    return field, base, coefficients


def column_of(row, groups, at, cols=LANES):
    shape = (groups, LANES)
    source = WIDE * lax.broadcasted_iota(jnp.int32, shape, 0) + at
    value = lanes_from(jnp.broadcast_to(row, shape), source)
    return jnp.concatenate([value] * (cols // LANES), axis=1)


def sideways(x, hop, strip_row, hop_row, span):
    groups, cols = x.shape
    lane = lane_of(x.shape)
    before = jnp.where(lane == 0, column_of(strip_row, groups, STEPS - 1, cols), turned(x, 1))
    after = jnp.where(lane == cols - 1, column_of(strip_row, groups, span + STEPS, cols), turned(x, -1))
    hop = jnp.broadcast_to(hop, x.shape)
    hop_before = jnp.where(lane == 0, hop_row[:, STEPS - 1 : STEPS], turned(hop, 1))
    return hop * after + hop_before * before


class Block:
    def __init__(self, probes, rows, cols):
        self.probes, self.rows, self.cols = probes, rows, cols
        self.groups = 2 * probes
        self.span = WIDE * self.groups
        self.tiles = cols // LANES
        self.tall = rows + 2 * TILE
        self.field_shape = (self.groups * self.tiles * self.tall, LANES)

    def at(self, g, c, row, count=TILE):
        return (pl.ds((g * self.tiles + c) * self.tall + TILE + row, count), slice(None))

    def across(self, c, row):
        return (pl.ds(c * self.tall + TILE + row, self.groups, stride=self.tiles * self.tall), slice(None))

    def gathered(self, ref, row):
        return jnp.concatenate([ref[self.across(c, row)] for c in range(self.tiles)], axis=1)

    def scattered(self, ref, row, value):
        for c in range(self.tiles):
            ref[self.across(c, row)] = value[:, c * LANES : (c + 1) * LANES]

    def hop_row(self, hops, kind, row):
        at = TILE + row
        return jnp.concatenate([hops[kind, c, at : at + 1, :] for c in range(self.tiles)], axis=1)


def lanes(c):
    return pl.ds(c * LANES, LANES)


def beside(block, strip_tile):
    first = lane_of(strip_tile.shape) < LANES // 2
    left, right = STEPS - 1, block.span + STEPS
    return [
        lanes_from(strip_tile, jnp.where(first, WIDE * g + left, WIDE * g + right)) for g in range(block.groups)
    ]


def tile_step(block, row, now, hops, sides, previous, sign, store, add, columns=None):
    lane = lane_of((TILE, LANES))
    tiles = block.tiles
    for c in range(tiles) if columns is None else columns:
        at = pl.ds(TILE + row, TILE)
        hop_site, hop_after, hop_before, hop_under = (hops[kind, c, at, :] for kind in range(4))
        hop_over = hops[3, c, pl.ds(TILE + row - 1, TILE), :]
        sums = None
        for p in range(block.probes):
            kept = []
            for f in range(2):
                g = f * block.probes + p
                side = 0.0 if sides is None else sides[g]
                centre = now[block.at(g, c, row)]
                if c > 0:
                    before = turned(jnp.where(lane == LANES - 1, now[block.at(g, c - 1, row)], centre), 1)
                else:
                    before = jnp.where(lane == 0, side, turned(centre, 1))
                if c < tiles - 1:
                    after = turned(jnp.where(lane == 0, now[block.at(g, c + 1, row)], centre), -1)
                else:
                    after = jnp.where(lane == LANES - 1, side, turned(centre, -1))
                under = now[block.at(g, c, row + 1)]
                over = now[block.at(g, c, row - 1)]
                total = hop_site * centre - previous(f, p, c)
                total = total + (hop_after * after + hop_before * before)
                total = total + (hop_under * under + hop_over * over)
                if f == 0:
                    total = total + sign(p, c)
                store(f, p, c, total)
                kept.append((centre, after, under))
            if add is not None:
                (a_centre, a_after, a_under), (q_centre, q_after, q_under) = kept
                terms = (
                    a_centre * q_after + a_after * q_centre,
                    a_centre * q_under + a_under * q_centre,
                    a_centre * q_centre,
                )
                sums = terms if p == 0 else tuple(x + y for x, y in zip(sums, terms))
        if add is not None:
            add(c, *sums)


def force_adder(forces, row, first):
    def add(c, *sums):
        for kind, term in enumerate(sums):
            spot = (kind, pl.ds(row, TILE), lanes(c))
            forces[spot] = term if first else forces[spot] + term

    return add


def sign_reader(signs, weights, step, row):
    weight = jnp.broadcast_to(weights[0:1, step : step + 1], (TILE, LANES))
    return lambda p, c: weight * signs[p, pl.ds(row, TILE), lanes(c)].astype(jnp.float32)


def field_storer(block, target, row):
    def store(f, p, c, tile):
        target[block.at(f * block.probes + p, c, row)] = tile

    return store


def field_reader(block, source, row):
    return lambda f, p, c: source[block.at(f * block.probes + p, c, row)]


def block_reader(adj, fwd, row):
    return lambda f, p, c: (fwd if f else adj)[p, pl.ds(row, TILE), lanes(c)]


def block_storer(adj, fwd, row):
    def store(f, p, c, tile):
        (fwd if f else adj)[p, pl.ds(row, TILE), lanes(c)] = tile

    return store


def first_kernel(
    weights, x0, adj_next, fwd_next, signs, onsite, hop_right, hop_down, x0_out, x1, x2, hops, forces, messages
):
    block = Block(*signs.shape)
    rows = block.rows
    nothing = jnp.zeros((block.groups, block.cols), jnp.float32)
    for row in (-1, rows):
        for x in (x0_out, x1, x2):
            block.scattered(x, row, nothing)
    for side, lines in enumerate(((0, 1, 2), (rows - 1, rows - 2, rows - 3))):
        edge_rows(
            block,
            weights,
            x0,
            adj_next,
            fwd_next,
            signs,
            (onsite, hop_right, hop_down),
            lines,
            messages.at[side],
        )
    wide_lane = lane_of((rows, LANES))
    inside = pl.ds(TILE, rows)
    hop_before = 0.0
    for c in range(block.tiles):
        hop = hop_right[:, lanes(c)] * SCALE
        hop_turned = turned(hop, 1)
        hops[0, c, inside, :] = onsite[:, lanes(c)] * SCALE
        hops[1, c, inside, :] = hop
        hops[2, c, inside, :] = jnp.where(wide_lane == 0, hop_before, hop_turned)
        hops[3, c, inside, :] = hop_down[:, lanes(c)] * SCALE
        hops[3, c, pl.ds(TILE - 1, 1), :] = jnp.zeros((1, LANES), jnp.float32)
        hop_before = hop_turned
    for row in range(0, rows, TILE):
        tile_step(
            block,
            row,
            x0_out,
            hops,
            None,
            block_reader(adj_next, fwd_next, row),
            sign_reader(signs, weights, 0, row),
            field_storer(block, x1, row),
            force_adder(forces, row, True),
        )
    for row in range(0, rows, TILE):
        tile_step(
            block,
            row,
            x1,
            hops,
            None,
            field_reader(block, x0_out, row),
            sign_reader(signs, weights, 1, row),
            field_storer(block, x2, row),
            force_adder(forces, row, False),
            range(1, block.tiles - 1),
        )


def at_ends(block, row):
    return (
        column_of(row, block.groups, STEPS - 1, block.cols),
        column_of(row, block.groups, block.span + STEPS, block.cols),
    )


def send_kernel(own, left, right, messages, to_above, to_below):
    rows, cols = own.shape[0], to_above.shape[1]
    groups = (to_above.shape[0] - TILE) // 3
    span = WIDE * groups
    misc = 3 * groups
    lane = lane_of((groups, LANES))
    left_part = lane_of((TILE, LANES)) < span
    for side, (edge, second) in enumerate(((0, 1), (TILE - 1, TILE - 2))):
        message = (to_above, to_below)[side]
        message[...] = messages[side]
        part = pl.ds(side * (rows - TILE), TILE)
        field, base, (s_on, s_right, s_down) = strips(own[part, :], left[part, :], right[part, :], span)
        before = turned(s_right, 1)
        level = base + s_on * field + s_right * turned(field, -1) + before * turned(field, 1)
        inward = jnp.where(left_part, s_right, before) * field
        down_inward = jnp.where(left_part, turned(s_down, -1), turned(s_down, 1))
        bond = min(edge, second)
        one = inward[edge : edge + 1, :]
        two = down_inward[bond : bond + 1, :] * inward[second : second + 1, :]
        for at, row in ((groups, one), (2 * groups, two)):
            for start, value, spot in (
                (0, column_of(row, groups, STEPS - 1), 0),
                (cols - LANES, column_of(row, groups, span + STEPS), LANES - 1),
            ):
                where = (pl.ds(at, groups), pl.ds(start, LANES))
                message[where] = message[where] + jnp.where(lane == spot, value, 0.0)
        message[misc + 3 : misc + 4, 0 : 4 * LANES] = jnp.concatenate(
            [
                field[edge : edge + 1, :],
                level[edge : edge + 1, :] + s_down[bond : bond + 1, :] * field[second : second + 1, :],
                s_down[edge : edge + 1, :],
                s_right[edge : edge + 1, :],
            ],
            axis=1,
        )


def strip_rows(block, strip, strip_base, strip_hops, step, row, count):
    here = pl.ds(TILE + row, count)
    now = strip[step, here, :]
    s_right = strip_hops[1, here, :]
    strip[step + 1, here, :] = (
        strip_base[step, pl.ds(row, count), :]
        + strip_hops[0, here, :] * now
        + s_right * turned(now, -1)
        + turned(s_right, 1) * turned(now, 1)
        + strip_hops[2, here, :] * strip[step, pl.ds(TILE + row + 1, count), :]
        + strip_hops[2, pl.ds(TILE + row - 1, count), :] * strip[step, pl.ds(TILE + row - 1, count), :]
    )


def inner_kernel(
    weights,
    x0,
    signs,
    own,
    left,
    right,
    sent,
    x1_in,
    x2_in,
    hops_in,
    forces_in,
    x1,
    x2,
    hops,
    forces,
    adj_out,
    fwd_out,
    strip,
    strip_base,
    strip_hops,
):
    del sent, x1_in, x2_in, hops_in, forces_in
    block = Block(*signs.shape)
    rows, tiles, probes = block.rows, block.tiles, block.probes
    inside = pl.ds(TILE, rows)
    lane = lane_of((TILE, LANES))
    for row in (TILE - 1, TILE + rows):
        strip_hops[2, row : row + 1, :] = jnp.zeros((1, LANES), jnp.float32)
        for step in range(2):
            strip[step, row : row + 1, :] = jnp.zeros((1, LANES), jnp.float32)
    field, base, (s_on, s_right, s_down) = strips(own[...], left[...], right[...], block.span)
    sign_strip = jnp.where(lane_of(base.shape) < block.span, turned(base, 2), turned(base, -2))
    strip[0, inside, :] = field
    strip_base[0] = base
    strip_base[1] = weights[0:1, 1:2] * sign_strip - field
    strip_hops[0, inside, :] = s_on
    strip_hops[1, inside, :] = s_right
    strip_hops[2, inside, :] = s_down

    last = tiles - 1
    for row in range(0, rows, TILE):
        at = pl.ds(TILE + row, TILE)
        sides = beside(block, strip[0, at, :])
        hop_first = turned(strip_hops[1, at, :], -(STEPS - 1))
        hops[2, 0, at, :] = jnp.where(lane == 0, hop_first, hops[2, 0, at, :])
        hop_last = hops[1, last, at, :]
        for g in range(block.groups):
            spot = block.at(g, 0, row)
            x1[spot] = x1[spot] + jnp.where(lane == 0, hop_first * sides[g], 0.0)
            spot = block.at(g, last, row)
            x1[spot] = x1[spot] + jnp.where(lane == LANES - 1, hop_last * sides[g], 0.0)
        total = None
        for p in range(probes):
            q = probes + p
            term = x0[block.at(p, last, row)] * sides[q] + sides[p] * x0[block.at(q, last, row)]
            total = term if total is None else total + term
        spot = (0, pl.ds(row, TILE), lanes(last))
        forces[spot] = forces[spot] + jnp.where(lane == LANES - 1, total, 0.0)

    for step in (1, 2):
        strip_rows(block, strip, strip_base, strip_hops, step - 1, 0, rows)
        now, before = (x1, x0) if step == 1 else (x2, x1)
        for row in range(0, rows, TILE):
            tile_step(
                block,
                row,
                now,
                hops,
                beside(block, strip[step, pl.ds(TILE + row, TILE), :]),
                field_reader(block, before, row),
                sign_reader(signs, weights, step, row),
                field_storer(block, x2, row) if step == 1 else block_storer(adj_out, fwd_out, row),
                force_adder(forces, row, False),
                sorted({0, last}) if step == 1 else None,
            )


def other_field(x):
    return pltpu.roll(x, x.shape[0] // 2, 0)


def outer_kernel(
    x0, x1, x2, hops, strip, strip_hops, above, below, forces_in, adj_in, fwd_in, *refs
):
    del forces_in, adj_in, fwd_in
    forces, adj_out, fwd_out = refs
    probes, rows, cols = adj_out.shape
    block = Block(probes, rows, cols)
    groups, span = block.groups, block.span
    misc = 3 * groups
    lane = lane_of((groups, cols))

    def s_line(ref, at, row):
        return ref[at, TILE + row : TILE + row + 1, :]

    def neighbours(x, strip_row):
        first, last = at_ends(block, strip_row)
        before = jnp.where(lane == 0, first, turned(x, 1))
        return before, jnp.where(lane == cols - 1, last, turned(x, -1))

    for side, source in enumerate((above, below)):
        edge, second, third = (0, 1, 2) if side == 0 else (rows - 1, rows - 2, rows - 3)
        bond, next_bond = (edge, second) if side == 0 else (second, third)
        corner = source[misc + 3 : misc + 4, 0 : 4 * LANES]
        c_field, c_one, c_down, c_right = (corner[:, k * LANES : (k + 1) * LANES] for k in range(4))
        hop_out = source[misc + 2 : misc + 3, :] if side == 0 else block.hop_row(hops, 3, edge)
        s_out = c_down if side == 0 else s_line(strip_hops, 2, edge)
        hop_in, hop_next = block.hop_row(hops, 3, bond), block.hop_row(hops, 3, next_bond)

        def across(x, pair, row):
            before, after = pair
            return (
                block.hop_row(hops, 0, row) * x
                + block.hop_row(hops, 1, row) * after
                + block.hop_row(hops, 2, row) * before
            )

        s_right = s_line(strip_hops, 1, edge)
        s_one_beyond = c_one + s_out * s_line(strip, 0, edge)
        s_one = s_out * c_field
        s_two = (
            s_line(strip_hops, 0, edge) * s_one
            + s_right * turned(s_one, -1)
            + turned(s_right, 1) * turned(s_one, 1)
            + s_out * s_one_beyond
        )
        s_two_second = s_line(strip_hops, 2, bond) * s_one

        x0_edge, x1_edge, x2_edge = (block.gathered(x, edge) for x in (x0, x1, x2))
        x1_second, x2_second = (block.gathered(x, second) for x in (x1, x2))
        x2_third = block.gathered(x2, third)
        x0_beyond = source[0:groups, :]
        one = hop_out * x0_beyond
        one_pair = neighbours(one, s_one)
        x1_beyond = source[groups : 2 * groups, :] + hop_out * x0_edge
        two = across(one, one_pair, edge) + hop_out * x1_beyond
        two_pair = neighbours(two, s_two)
        two_second = hop_in * one
        two_second_pair = neighbours(two_second, s_two_second)
        x1_new = x1_edge + one
        x2_beyond = (
            source[2 * groups : 3 * groups, :]
            + source[misc : misc + 1, :] * x1_beyond
            + sideways(x1_beyond, source[misc + 1 : misc + 2, :], s_one_beyond, c_right, span)
            + hop_out * x1_new
        )
        x2_new, x2_second_new = x2_edge + two, x2_second + two_second
        changes = (
            (edge, across(two, two_pair, edge) + hop_in * two_second + hop_out * x2_beyond - one),
            (second, across(two_second, two_second_pair, second) + hop_in * two),
            (third, hop_next * two_second),
        )
        for row, change in changes:
            adj_out[:, row, :] = adj_out[:, row, :] + change[:probes]
            fwd_out[:, row, :] = fwd_out[:, row, :] + change[probes:]

        def changed(x, change, new, other, other_change):
            return change * other_field(other) + x * other_field(other_change)

        def right_of(x, strip_row):
            return jnp.where(lane == cols - 1, column_of(strip_row, groups, span + STEPS, cols), turned(x, -1))

        one_right = right_of(x1_new, s_line(strip, 1, edge) + s_one)
        two_right = right_of(x2_new, s_line(strip, 2, edge) + s_two)
        second_right = right_of(x2_second_new, s_line(strip, 2, second) + s_two_second)
        terms = [
            (
                0,
                edge,
                changed(x1_edge, one, x1_new, one_right, one_pair[1])
                + changed(x2_edge, two, x2_new, two_right, two_pair[1]),
            ),
            (0, second, changed(x2_second, two_second, x2_second_new, second_right, two_second_pair[1])),
            (1, bond, changed(x2_edge, two, x2_new, x2_second_new, two_second) + one * other_field(x1_second)),
            (1, next_bond, two_second * other_field(x2_third)),
            (2, edge, 0.5 * (changed(x1_edge, one, x1_new, x1_new, one) + changed(x2_edge, two, x2_new, x2_new, two))),
            (2, second, 0.5 * changed(x2_second, two_second, x2_second_new, x2_second_new, two_second)),
        ]
        if side == 1:
            outward = (
                x0_edge * other_field(x0_beyond)
                + x1_new * other_field(x1_beyond)
                + x2_new * other_field(x2_beyond)
            )
            terms.append((1, edge, outward))
        for kind, row, term in terms:
            spot = (kind, pl.ds(row, 1), slice(None))
            forces[spot] = forces[spot] + jnp.sum(term, axis=0, keepdims=True)


def store_kernel(adj, fwd, adj_out, fwd_out, done):
    copies = []
    for source, target in ((adj, adj_out), (fwd, fwd_out)):
        for p in range(source.shape[0]):
            copies.append(pltpu.make_async_copy(source.at[p], target.at[p], done.at[len(copies)]))
            copies[-1].start()
    for each in copies:
        each.wait()


def sum_kernel(mine, other, right_out, down_out, site_out):
    for at, out in enumerate((right_out, down_out, site_out)):
        out[...] = (mine[at] + other[at]) * SCALE


def both_sides(x):
    left = shifted(x, "col", 1)
    return left, left if lax.axis_size("col") == 2 else shifted(x, "col", -1)


def in_vmem(*arrays):
    return tuple(pltpu.with_memory_space_constraint(v, pltpu.VMEM) for v in arrays)


def local(
    signs,
    onsite,
    hop_right,
    hop_down,
    moment_weights,
    forward_now,
    forward_next,
    adjoint_now,
    adjoint_next,
):
    probes, rows, cols = forward_now.shape
    block = Block(probes, rows, cols)
    groups, tiles, tall = block.groups, block.tiles, block.tall
    f32 = jnp.float32
    vmem = pl.BlockSpec(memory_space=pltpu.VMEM)
    hbm = pl.BlockSpec(memory_space=pltpu.HBM)
    params = pltpu.CompilerParams(vmem_limit_bytes=VMEM_LIMIT)

    def call(kernel, name, inputs, outs, scratch=(), aliases=None, flops=0, in_spec=vmem, out_spec=vmem):
        return pl.pallas_call(
            kernel,
            out_shape=outs,
            in_specs=[in_spec] * len(inputs),
            out_specs=(out_spec,) * len(outs),
            scratch_shapes=list(scratch),
            input_output_aliases=aliases or {},
            compiler_params=params,
            cost_estimate=pl.CostEstimate(flops=flops, bytes_accessed=flops, transcendentals=0),
            name=name,
        )(*inputs)

    def like(v, dtype=f32):
        return pltpu.VMEM(v.shape, dtype)

    sources = (
        moment_weights.reshape(1, STEPS),
        adjoint_now,
        forward_now,
        adjoint_next,
        forward_next,
        signs,
        onsite,
        hop_right,
        hop_down,
    )
    sources = tuple(pltpu.with_memory_space_constraint(v, pltpu.HBM) for v in sources)
    strip_tile = pltpu.VMEM((rows, LANES), f32)
    x0, adj_next, fwd_next, sign, on, hr, hd, weights, packed = call(
        load_kernel,
        "load",
        sources,
        (
            pltpu.VMEM((groups, tiles, tall, LANES), f32),
            like(adjoint_next),
            like(forward_next),
            like(signs, jnp.int32),
            like(onsite),
            like(hop_right),
            like(hop_down),
            pltpu.VMEM((1, STEPS), f32),
            strip_tile,
        ),
        [pltpu.SemaphoreType.DMA((13 + 2 * tiles,))],
        in_spec=hbm,
    )
    x0 = x0.reshape(block.field_shape)
    left, right = both_sides(packed)

    x0, adj_next, fwd_next, sign, on, hr, hd, weights, packed = in_vmem(
        x0, adj_next, fwd_next, sign, on, hr, hd, weights, packed
    )
    message = pltpu.VMEM((3 * groups + TILE, cols), f32)
    both_messages = pltpu.VMEM((2, 3 * groups + TILE, cols), f32)
    field = pltpu.VMEM(block.field_shape, f32)
    hops_shape = pltpu.VMEM((4, tiles, tall, LANES), f32)
    forces_shape = pltpu.VMEM((3, rows, cols), f32)
    x0, x1, x2, hops, forces, messages = call(
        first_kernel,
        "step_0",
        (weights, x0, adj_next, fwd_next, sign, on, hr, hd),
        (field, field, field, hops_shape, forces_shape, both_messages),
        aliases={1: 0},
        flops=COST,
    )

    x0, x1, x2, hops, forces = in_vmem(x0, x1, x2, hops, forces)
    messages, left, right = in_vmem(messages, left, right)
    to_above, to_below = call(
        send_kernel, "edge_rows", (packed, left, right, messages), (message, message)
    )
    above = shifted(to_below, "strip", 1)
    below = shifted(to_above, "strip", -1)

    (sent,) = in_vmem(to_above)
    x1, x2, hops, forces, adj_out, fwd_out, strip, strip_base, strip_hops = call(
        inner_kernel,
        "inner_steps",
        (weights, x0, sign, packed, left, right, sent, x1, x2, hops, forces),
        (
            field,
            field,
            hops_shape,
            forces_shape,
            like(adjoint_now),
            like(forward_now),
            pltpu.VMEM((STEPS, tall, LANES), f32),
            pltpu.VMEM((2, rows, LANES), f32),
            pltpu.VMEM((3, tall, LANES), f32),
        ),
        aliases={7: 0, 8: 1, 9: 2, 10: 3},
        flops=COST,
    )

    kept = in_vmem(forces, adj_out, fwd_out)
    read = (x0,) + in_vmem(x1, x2, hops, strip, strip_hops, above, below)
    forces, adjoint_out, forward_out = call(
        outer_kernel,
        "outer_rows",
        read + kept,
        tuple(like(v) for v in kept),
        aliases={len(read) + i: i for i in range(len(kept))},
        flops=COST,
    )

    other = shifted(forces, "probe", 1)
    whole = jax.ShapeDtypeStruct(adjoint_now.shape, f32)
    adjoint_out, forward_out = call(
        store_kernel,
        "store",
        in_vmem(adjoint_out, forward_out),
        (whole, whole),
        [pltpu.SemaphoreType.DMA((2 * probes,))],
        flops=COST,
        out_spec=hbm,
    )
    plain = jax.ShapeDtypeStruct((rows, cols), f32)
    right_force, down_force, site_force = call(
        sum_kernel, "force_sums", in_vmem(forces, other), (plain, plain, plain)
    )
    return right_force, down_force, site_force, forward_out, adjoint_out


def solution(mesh):
    placed = (
        P(("parts", "probe"), "strip", "col"),
        P(("parts", "strip"), "col"),
        P(("parts", "strip"), "col"),
        P(("parts", "strip"), "col"),
        P(),
        P(("parts", "probe"), "strip", "col"),
        P(("parts", "probe"), "strip", "col"),
        P(("parts", "probe"), "strip", "col"),
        P(("parts", "probe"), "strip", "col"),
    )
    return jax.shard_map(
        local,
        mesh=mesh,
        in_specs=placed,
        out_specs=(
            P(("parts", "strip"), "col"),
            P(("parts", "strip"), "col"),
            P(("parts", "strip"), "col"),
            P(("parts", "probe"), "strip", "col"),
            P(("parts", "probe"), "strip", "col"),
        ),
        check_vma=False,
    )
```

```python
import jax
import jax.numpy as jnp
from jax import lax
from jax.experimental import pallas as pl
from jax.experimental.pallas import tpu as pltpu
from jax.sharding import PartitionSpec as P

STEPS = 3
LANES = 128
TILE = 8
spectral_half = 7.5
SCALE = 2.0 / spectral_half

WIDE = 2 * STEPS
VMEM_LIMIT = 16 * 1024 * 1024
COST = 4_000_000


def shifted(x, axis, by):
    size = lax.axis_size(axis)
    return lax.ppermute(x, axis, [(i, (i + by) % size) for i in range(size)])


def lane_of(shape):
    return lax.broadcasted_iota(jnp.int32, shape, len(shape) - 1)


def lanes_from(x, source):
    return jnp.take_along_axis(x, source, axis=1, mode="promise_in_bounds")


def turned(x, by):
    return pltpu.roll(x, by % x.shape[1], 1)


def pack(shape, probes, now, following, sign, lattice, weight):
    groups = 2 * probes
    span = WIDE * groups
    lane = lane_of(shape)

    def joined(pair):
        return jnp.where(lane < LANES // 2, pair[0], pair[1])

    packed = jnp.zeros(shape, jnp.float32)

    def put(packed, x, start):
        return jnp.where((lane >= start) & (lane < start + WIDE), turned(x, start + STEPS), packed)

    first, last = LANES - STEPS, STEPS - 1
    for at in range(3):
        packed = put(packed, joined(lattice(at)), 2 * span + WIDE * at)
    for g in range(groups):
        packed = put(packed, joined(now(g)), WIDE * g)
    for g in reversed(range(groups)):
        if g < probes:
            own_sign = joined(sign(g)).astype(jnp.float32)
            base = weight() * own_sign - joined(following(g))
            base = jnp.where(lane == first, turned(own_sign, -2), jnp.where(lane == last, turned(own_sign, 2), base))
        else:
            base = jnp.where((lane == first) | (lane == last), 0.0, -joined(following(g)))
        packed = put(packed, base, span + WIDE * g)
    return packed


def ends(ref, *at):
    cols = ref.shape[-1]
    return tuple(ref[(*at, slice(None), pl.ds(start, LANES))] for start in (0, cols - LANES))


def load_kernel(
    weights_in,
    adj_in,
    fwd_in,
    adj_next_in,
    fwd_next_in,
    signs_in,
    onsite_in,
    hop_right_in,
    hop_down_in,
    x0,
    adj_next,
    fwd_next,
    signs,
    onsite,
    hop_right,
    hop_down,
    weights,
    packed,
    done,
):
    probes, rows, cols = adj_in.shape
    tiles = cols // LANES
    inside = pl.ds(TILE, rows)
    copies = []
    started = {}

    def copy(name, source, target):
        copies.append(pltpu.make_async_copy(source, target, done.at[len(copies)]))
        copies[-1].start()
        started.setdefault(name, []).append(copies[-1])

    def here(name):
        for each in started.pop(name, ()):
            each.wait()

    def copy_tile(name, f, c):
        source = (adj_in, fwd_in)[f]
        copy(name, source.at[:, :, lanes(c)], x0.at[pl.ds(f * probes, probes), c, inside, :])

    rest = ((adj_next_in, adj_next), (fwd_next_in, fwd_next), (signs_in, signs))
    copy("lattice", onsite_in, onsite)
    copy("lattice", hop_right_in, hop_right)
    copy("lattice", hop_down_in, hop_down)
    copy("weights", weights_in, weights)
    ends_at = (0, tiles - 1)
    for f in range(2):
        for c in ends_at:
            copy_tile(("now", f), f, c)
    for at in (1, 2, 0):
        source, target = rest[at]
        for c in ends_at:
            copy(("rest", at), source.at[:, :, lanes(c)], target.at[:, :, lanes(c)])
    for c in range(1, tiles - 1):
        for f in range(2):
            copy_tile("others", f, c)

    def now(g):
        here(("now", g // probes))
        return x0[g, 0, inside, :], x0[g, tiles - 1, inside, :]

    def following(g):
        here(("rest", g // probes))
        return ends(rest[g // probes][1], g % probes)

    def sign(p):
        here(("rest", 2))
        return ends(signs, p)

    def lattice(kind):
        here("lattice")
        return ends((onsite, hop_right, hop_down)[kind])

    def weight():
        here("weights")
        return weights[0:1, 0:1]

    packed[...] = pack(packed.shape, probes, now, following, sign, lattice, weight)
    for name in list(started):
        here(name)


def edge_rows(block, weights, x0, adj_next, fwd_next, signs, lattice, lines, out):
    edge, second, third = lines
    groups, cols = block.groups, block.cols
    lane = lane_of((groups, cols))

    def next_rows(row):
        return jnp.concatenate([adj_next[:, row, :], fwd_next[:, row, :]], axis=0)

    def sign_rows(step, row):
        sign = weights[0:1, step : step + 1] * signs[:, row, :].astype(jnp.float32)
        return jnp.concatenate([sign, jnp.zeros_like(sign)], axis=0)

    def hop(kind, row):
        return lattice[kind][row : row + 1, :] * SCALE

    def across(x, row):
        right = jnp.broadcast_to(hop(1, row), x.shape)
        after = jnp.where(lane == cols - 1, 0.0, right * turned(x, -1))
        return hop(0, row) * x + after + jnp.where(lane == 0, 0.0, turned(right * x, 1))

    x_edge, x_second, x_third = (block.gathered(x0, row) for row in lines)
    down = hop(2, min(edge, second))
    one = (
        sign_rows(0, second)
        - next_rows(second)
        + across(x_second, second)
        + down * x_edge
        + hop(2, min(second, third)) * x_third
    )
    out[0:groups, :] = x_edge
    out[groups : 2 * groups, :] = (
        sign_rows(0, edge) - next_rows(edge) + across(x_edge, edge) + down * x_second
    )
    out[2 * groups : 3 * groups, :] = sign_rows(1, edge) - x_edge + down * one
    misc = 3 * groups
    for kind in range(3):
        out[misc + kind : misc + kind + 1, :] = hop(kind, edge)
    out[misc + 3 : misc + TILE, :] = jnp.zeros((TILE - 3, cols), jnp.float32)


def strips(own, left, right, span):
    lane = lane_of(own.shape)
    within = lane - WIDE * ((lane * (256 // WIDE + 1)) >> 8)
    inner = within < STEPS
    low = jnp.where(inner, left, own)
    high = jnp.where(inner, own, right)
    below = lane < span
    field = jnp.where(below, low, turned(high, span))
    base = jnp.where(below, turned(low, -span), high)
    coefficients = []
    for at in range(3):
        source = 2 * span + WIDE * at + within
        coefficients.append(jnp.where(below, lanes_from(low, source), lanes_from(high, source)) * SCALE)
    return field, base, coefficients


def column_of(row, groups, at, cols=LANES):
    shape = (groups, LANES)
    source = WIDE * lax.broadcasted_iota(jnp.int32, shape, 0) + at
    value = lanes_from(jnp.broadcast_to(row, shape), source)
    return jnp.concatenate([value] * (cols // LANES), axis=1)


def sideways(x, hop, strip_row, hop_row, span):
    groups, cols = x.shape
    lane = lane_of(x.shape)
    before = jnp.where(lane == 0, column_of(strip_row, groups, STEPS - 1, cols), turned(x, 1))
    after = jnp.where(lane == cols - 1, column_of(strip_row, groups, span + STEPS, cols), turned(x, -1))
    hop = jnp.broadcast_to(hop, x.shape)
    hop_before = jnp.where(lane == 0, hop_row[:, STEPS - 1 : STEPS], turned(hop, 1))
    return hop * after + hop_before * before


class Block:
    def __init__(self, probes, rows, cols):
        self.probes, self.rows, self.cols = probes, rows, cols
        self.groups = 2 * probes
        self.span = WIDE * self.groups
        self.tiles = cols // LANES
        self.tall = rows + 2 * TILE
        self.field_shape = (self.groups * self.tiles * self.tall, LANES)

    def at(self, g, c, row, count=TILE):
        return (pl.ds((g * self.tiles + c) * self.tall + TILE + row, count), slice(None))

    def across(self, c, row):
        return (pl.ds(c * self.tall + TILE + row, self.groups, stride=self.tiles * self.tall), slice(None))

    def gathered(self, ref, row):
        return jnp.concatenate([ref[self.across(c, row)] for c in range(self.tiles)], axis=1)

    def scattered(self, ref, row, value):
        for c in range(self.tiles):
            ref[self.across(c, row)] = value[:, c * LANES : (c + 1) * LANES]

    def hop_row(self, hops, kind, row):
        at = TILE + row
        return jnp.concatenate([hops[kind, c, at : at + 1, :] for c in range(self.tiles)], axis=1)


def lanes(c):
    return pl.ds(c * LANES, LANES)


def beside(block, strip_tile):
    first = lane_of(strip_tile.shape) < LANES // 2
    left, right = STEPS - 1, block.span + STEPS
    return [
        lanes_from(strip_tile, jnp.where(first, WIDE * g + left, WIDE * g + right)) for g in range(block.groups)
    ]


def tile_step(block, row, now, hops, sides, previous, sign, store, add, columns=None):
    lane = lane_of((TILE, LANES))
    tiles = block.tiles
    for c in range(tiles) if columns is None else columns:
        at = pl.ds(TILE + row, TILE)
        hop_site, hop_after, hop_before, hop_under = (hops[kind, c, at, :] for kind in range(4))
        hop_over = hops[3, c, pl.ds(TILE + row - 1, TILE), :]
        sums = None
        for p in range(block.probes):
            kept = []
            for f in range(2):
                g = f * block.probes + p
                side = 0.0 if sides is None else sides[g]
                centre = now[block.at(g, c, row)]
                if c > 0:
                    before = turned(jnp.where(lane == LANES - 1, now[block.at(g, c - 1, row)], centre), 1)
                else:
                    before = jnp.where(lane == 0, side, turned(centre, 1))
                if c < tiles - 1:
                    after = turned(jnp.where(lane == 0, now[block.at(g, c + 1, row)], centre), -1)
                else:
                    after = jnp.where(lane == LANES - 1, side, turned(centre, -1))
                under = now[block.at(g, c, row + 1)]
                over = now[block.at(g, c, row - 1)]
                total = hop_site * centre - previous(f, p, c)
                total = total + (hop_after * after + hop_before * before)
                total = total + (hop_under * under + hop_over * over)
                if f == 0:
                    total = total + sign(p, c)
                store(f, p, c, total)
                kept.append((centre, after, under))
            if add is not None:
                (a_centre, a_after, a_under), (q_centre, q_after, q_under) = kept
                terms = (
                    a_centre * q_after + a_after * q_centre,
                    a_centre * q_under + a_under * q_centre,
                    a_centre * q_centre,
                )
                sums = terms if p == 0 else tuple(x + y for x, y in zip(sums, terms))
        if add is not None:
            add(c, *sums)


def force_adder(forces, row, first):
    def add(c, *sums):
        for kind, term in enumerate(sums):
            spot = (kind, pl.ds(row, TILE), lanes(c))
            forces[spot] = term if first else forces[spot] + term

    return add


def sign_reader(signs, weights, step, row):
    weight = jnp.broadcast_to(weights[0:1, step : step + 1], (TILE, LANES))
    return lambda p, c: weight * signs[p, pl.ds(row, TILE), lanes(c)].astype(jnp.float32)


def field_storer(block, target, row):
    def store(f, p, c, tile):
        target[block.at(f * block.probes + p, c, row)] = tile

    return store


def field_reader(block, source, row):
    return lambda f, p, c: source[block.at(f * block.probes + p, c, row)]


def block_reader(adj, fwd, row):
    return lambda f, p, c: (fwd if f else adj)[p, pl.ds(row, TILE), lanes(c)]


def block_storer(adj, fwd, row):
    def store(f, p, c, tile):
        (fwd if f else adj)[p, pl.ds(row, TILE), lanes(c)] = tile

    return store


def first_kernel(
    adj_next_in,
    fwd_next_in,
    signs_in,
    weights,
    x0_in,
    adj_next_start,
    fwd_next_start,
    signs_start,
    onsite,
    hop_right,
    hop_down,
    x0,
    adj_next,
    fwd_next,
    signs,
    x1,
    x2,
    hops,
    forces,
    messages,
    done,
):
    del x0_in, adj_next_start, fwd_next_start, signs_start
    block = Block(*signs.shape)
    rows = block.rows
    part = pl.ds(LANES, block.cols - 2 * LANES)
    copies = []
    for source, target in ((adj_next_in, adj_next), (fwd_next_in, fwd_next), (signs_in, signs)):
        copies.append(
            pltpu.make_async_copy(source.at[:, :, part], target.at[:, :, part], done.at[len(copies)])
        )
        copies[-1].start()
    nothing = jnp.zeros((block.groups, block.cols), jnp.float32)
    for row in (-1, rows):
        for x in (x0, x1, x2):
            block.scattered(x, row, nothing)
    wide_lane = lane_of((rows, LANES))
    inside = pl.ds(TILE, rows)
    hop_before = 0.0
    for c in range(block.tiles):
        hop = hop_right[:, lanes(c)] * SCALE
        hop_turned = turned(hop, 1)
        hops[0, c, inside, :] = onsite[:, lanes(c)] * SCALE
        hops[1, c, inside, :] = hop
        hops[2, c, inside, :] = jnp.where(wide_lane == 0, hop_before, hop_turned)
        hops[3, c, inside, :] = hop_down[:, lanes(c)] * SCALE
        hops[3, c, pl.ds(TILE - 1, 1), :] = jnp.zeros((1, LANES), jnp.float32)
        hop_before = hop_turned
    for each in copies:
        each.wait()
    for side, lines in enumerate(((0, 1, 2), (rows - 1, rows - 2, rows - 3))):
        edge_rows(
            block,
            weights,
            x0,
            adj_next,
            fwd_next,
            signs,
            (onsite, hop_right, hop_down),
            lines,
            messages.at[side],
        )
    for row in range(0, rows, TILE):
        tile_step(
            block,
            row,
            x0,
            hops,
            None,
            block_reader(adj_next, fwd_next, row),
            sign_reader(signs, weights, 0, row),
            field_storer(block, x1, row),
            force_adder(forces, row, True),
        )

def at_ends(block, row):
    return (
        column_of(row, block.groups, STEPS - 1, block.cols),
        column_of(row, block.groups, block.span + STEPS, block.cols),
    )


def send_kernel(own, left, right, messages, to_above, to_below):
    rows, cols = own.shape[0], to_above.shape[1]
    groups = (to_above.shape[0] - TILE) // 3
    span = WIDE * groups
    misc = 3 * groups
    lane = lane_of((groups, LANES))
    left_part = lane_of((TILE, LANES)) < span
    for side, (edge, second) in enumerate(((0, 1), (TILE - 1, TILE - 2))):
        message = (to_above, to_below)[side]
        message[...] = messages[side]
        part = pl.ds(side * (rows - TILE), TILE)
        field, base, (s_on, s_right, s_down) = strips(own[part, :], left[part, :], right[part, :], span)
        before = turned(s_right, 1)
        level = base + s_on * field + s_right * turned(field, -1) + before * turned(field, 1)
        inward = jnp.where(left_part, s_right, before) * field
        down_inward = jnp.where(left_part, turned(s_down, -1), turned(s_down, 1))
        bond = min(edge, second)
        one = inward[edge : edge + 1, :]
        two = down_inward[bond : bond + 1, :] * inward[second : second + 1, :]
        for at, row in ((groups, one), (2 * groups, two)):
            for start, value, spot in (
                (0, column_of(row, groups, STEPS - 1), 0),
                (cols - LANES, column_of(row, groups, span + STEPS), LANES - 1),
            ):
                where = (pl.ds(at, groups), pl.ds(start, LANES))
                message[where] = message[where] + jnp.where(lane == spot, value, 0.0)
        message[misc + 3 : misc + 4, 0 : 4 * LANES] = jnp.concatenate(
            [
                field[edge : edge + 1, :],
                level[edge : edge + 1, :] + s_down[bond : bond + 1, :] * field[second : second + 1, :],
                s_down[edge : edge + 1, :],
                s_right[edge : edge + 1, :],
            ],
            axis=1,
        )


def strip_rows(block, strip, strip_base, strip_hops, step, row, count):
    here = pl.ds(TILE + row, count)
    now = strip[step, here, :]
    s_right = strip_hops[1, here, :]
    strip[step + 1, here, :] = (
        strip_base[step, pl.ds(row, count), :]
        + strip_hops[0, here, :] * now
        + s_right * turned(now, -1)
        + turned(s_right, 1) * turned(now, 1)
        + strip_hops[2, here, :] * strip[step, pl.ds(TILE + row + 1, count), :]
        + strip_hops[2, pl.ds(TILE + row - 1, count), :] * strip[step, pl.ds(TILE + row - 1, count), :]
    )


def inner_kernel(
    weights,
    x0,
    signs,
    own,
    left,
    right,
    sent,
    x1_in,
    x2_in,
    hops_in,
    forces_in,
    x1,
    x2,
    hops,
    forces,
    adj_out,
    fwd_out,
    strip,
    strip_base,
    strip_hops,
):
    del sent, x1_in, x2_in, hops_in, forces_in
    block = Block(*signs.shape)
    rows, tiles, probes = block.rows, block.tiles, block.probes
    inside = pl.ds(TILE, rows)
    lane = lane_of((TILE, LANES))
    for row in (TILE - 1, TILE + rows):
        strip_hops[2, row : row + 1, :] = jnp.zeros((1, LANES), jnp.float32)
        for step in range(2):
            strip[step, row : row + 1, :] = jnp.zeros((1, LANES), jnp.float32)
    field, base, (s_on, s_right, s_down) = strips(own[...], left[...], right[...], block.span)
    sign_strip = jnp.where(lane_of(base.shape) < block.span, turned(base, 2), turned(base, -2))
    strip[0, inside, :] = field
    strip_base[0] = base
    strip_base[1] = weights[0:1, 1:2] * sign_strip - field
    strip_hops[0, inside, :] = s_on
    strip_hops[1, inside, :] = s_right
    strip_hops[2, inside, :] = s_down

    last = tiles - 1
    for row in range(0, rows, TILE):
        at = pl.ds(TILE + row, TILE)
        sides = beside(block, strip[0, at, :])
        hop_first = turned(strip_hops[1, at, :], -(STEPS - 1))
        hops[2, 0, at, :] = jnp.where(lane == 0, hop_first, hops[2, 0, at, :])
        hop_last = hops[1, last, at, :]
        for g in range(block.groups):
            spot = block.at(g, 0, row)
            x1[spot] = x1[spot] + jnp.where(lane == 0, hop_first * sides[g], 0.0)
            spot = block.at(g, last, row)
            x1[spot] = x1[spot] + jnp.where(lane == LANES - 1, hop_last * sides[g], 0.0)
        total = None
        for p in range(probes):
            q = probes + p
            term = x0[block.at(p, last, row)] * sides[q] + sides[p] * x0[block.at(q, last, row)]
            total = term if total is None else total + term
        spot = (0, pl.ds(row, TILE), lanes(last))
        forces[spot] = forces[spot] + jnp.where(lane == LANES - 1, total, 0.0)

    for step in (1, 2):
        strip_rows(block, strip, strip_base, strip_hops, step - 1, 0, rows)
        now, before = (x1, x0) if step == 1 else (x2, x1)
        for row in range(0, rows, TILE):
            tile_step(
                block,
                row,
                now,
                hops,
                beside(block, strip[step, pl.ds(TILE + row, TILE), :]),
                field_reader(block, before, row),
                sign_reader(signs, weights, step, row),
                field_storer(block, x2, row) if step == 1 else block_storer(adj_out, fwd_out, row),
                force_adder(forces, row, False),
            )


def other_field(x):
    return pltpu.roll(x, x.shape[0] // 2, 0)


def outer_kernel(
    x0, x1, x2, hops, strip, strip_hops, above, below, forces_in, adj_in, fwd_in, *refs
):
    del forces_in, adj_in, fwd_in
    forces, adj_out, fwd_out = refs
    probes, rows, cols = adj_out.shape
    block = Block(probes, rows, cols)
    groups, span = block.groups, block.span
    misc = 3 * groups
    lane = lane_of((groups, cols))

    def s_line(ref, at, row):
        return ref[at, TILE + row : TILE + row + 1, :]

    def neighbours(x, strip_row):
        first, last = at_ends(block, strip_row)
        before = jnp.where(lane == 0, first, turned(x, 1))
        return before, jnp.where(lane == cols - 1, last, turned(x, -1))

    for side, source in enumerate((above, below)):
        edge, second, third = (0, 1, 2) if side == 0 else (rows - 1, rows - 2, rows - 3)
        bond, next_bond = (edge, second) if side == 0 else (second, third)
        corner = source[misc + 3 : misc + 4, 0 : 4 * LANES]
        c_field, c_one, c_down, c_right = (corner[:, k * LANES : (k + 1) * LANES] for k in range(4))
        hop_out = source[misc + 2 : misc + 3, :] if side == 0 else block.hop_row(hops, 3, edge)
        s_out = c_down if side == 0 else s_line(strip_hops, 2, edge)
        hop_in, hop_next = block.hop_row(hops, 3, bond), block.hop_row(hops, 3, next_bond)

        def across(x, pair, row):
            before, after = pair
            return (
                block.hop_row(hops, 0, row) * x
                + block.hop_row(hops, 1, row) * after
                + block.hop_row(hops, 2, row) * before
            )

        s_right = s_line(strip_hops, 1, edge)
        s_one_beyond = c_one + s_out * s_line(strip, 0, edge)
        s_one = s_out * c_field
        s_two = (
            s_line(strip_hops, 0, edge) * s_one
            + s_right * turned(s_one, -1)
            + turned(s_right, 1) * turned(s_one, 1)
            + s_out * s_one_beyond
        )
        s_two_second = s_line(strip_hops, 2, bond) * s_one

        x0_edge, x1_edge, x2_edge = (block.gathered(x, edge) for x in (x0, x1, x2))
        x1_second, x2_second = (block.gathered(x, second) for x in (x1, x2))
        x2_third = block.gathered(x2, third)
        x0_beyond = source[0:groups, :]
        one = hop_out * x0_beyond
        one_pair = neighbours(one, s_one)
        x1_beyond = source[groups : 2 * groups, :] + hop_out * x0_edge
        two = across(one, one_pair, edge) + hop_out * x1_beyond
        two_pair = neighbours(two, s_two)
        two_second = hop_in * one
        two_second_pair = neighbours(two_second, s_two_second)
        x1_new = x1_edge + one
        x2_beyond = (
            source[2 * groups : 3 * groups, :]
            + source[misc : misc + 1, :] * x1_beyond
            + sideways(x1_beyond, source[misc + 1 : misc + 2, :], s_one_beyond, c_right, span)
            + hop_out * x1_new
        )
        x2_new, x2_second_new = x2_edge + two, x2_second + two_second
        changes = (
            (edge, across(two, two_pair, edge) + hop_in * two_second + hop_out * x2_beyond - one),
            (second, across(two_second, two_second_pair, second) + hop_in * two),
            (third, hop_next * two_second),
        )
        for row, change in changes:
            adj_out[:, row, :] = adj_out[:, row, :] + change[:probes]
            fwd_out[:, row, :] = fwd_out[:, row, :] + change[probes:]

        def changed(x, change, new, other, other_change):
            return change * other_field(other) + x * other_field(other_change)

        def right_of(x, strip_row):
            return jnp.where(lane == cols - 1, column_of(strip_row, groups, span + STEPS, cols), turned(x, -1))

        one_right = right_of(x1_new, s_line(strip, 1, edge) + s_one)
        two_right = right_of(x2_new, s_line(strip, 2, edge) + s_two)
        second_right = right_of(x2_second_new, s_line(strip, 2, second) + s_two_second)
        terms = [
            (
                0,
                edge,
                changed(x1_edge, one, x1_new, one_right, one_pair[1])
                + changed(x2_edge, two, x2_new, two_right, two_pair[1]),
            ),
            (0, second, changed(x2_second, two_second, x2_second_new, second_right, two_second_pair[1])),
            (1, bond, changed(x2_edge, two, x2_new, x2_second_new, two_second) + one * other_field(x1_second)),
            (1, next_bond, two_second * other_field(x2_third)),
            (2, edge, 0.5 * (changed(x1_edge, one, x1_new, x1_new, one) + changed(x2_edge, two, x2_new, x2_new, two))),
            (2, second, 0.5 * changed(x2_second, two_second, x2_second_new, x2_second_new, two_second)),
        ]
        if side == 1:
            outward = (
                x0_edge * other_field(x0_beyond)
                + x1_new * other_field(x1_beyond)
                + x2_new * other_field(x2_beyond)
            )
            terms.append((1, edge, outward))
        for kind, row, term in terms:
            spot = (kind, pl.ds(row, 1), slice(None))
            forces[spot] = forces[spot] + jnp.sum(term, axis=0, keepdims=True)


def store_kernel(adj, fwd, adj_out, fwd_out, done):
    copies = []
    for source, target in ((adj, adj_out), (fwd, fwd_out)):
        for p in range(source.shape[0]):
            copies.append(pltpu.make_async_copy(source.at[p], target.at[p], done.at[len(copies)]))
            copies[-1].start()
    for each in copies:
        each.wait()


def sum_kernel(mine, other, right_out, down_out, site_out):
    for at, out in enumerate((right_out, down_out, site_out)):
        out[...] = (mine[at] + other[at]) * SCALE


def both_sides(x):
    left = shifted(x, "col", 1)
    return left, left if lax.axis_size("col") == 2 else shifted(x, "col", -1)


def in_vmem(*arrays):
    return tuple(pltpu.with_memory_space_constraint(v, pltpu.VMEM) for v in arrays)


def local(
    signs,
    onsite,
    hop_right,
    hop_down,
    moment_weights,
    forward_now,
    forward_next,
    adjoint_now,
    adjoint_next,
):
    probes, rows, cols = forward_now.shape
    block = Block(probes, rows, cols)
    groups, tiles, tall = block.groups, block.tiles, block.tall
    f32 = jnp.float32
    vmem = pl.BlockSpec(memory_space=pltpu.VMEM)
    hbm = pl.BlockSpec(memory_space=pltpu.HBM)
    params = pltpu.CompilerParams(vmem_limit_bytes=VMEM_LIMIT)

    def call(kernel, name, inputs, outs, scratch=(), aliases=None, flops=0, in_spec=vmem, out_spec=vmem):
        return pl.pallas_call(
            kernel,
            out_shape=outs,
            in_specs=in_spec if isinstance(in_spec, list) else [in_spec] * len(inputs),
            out_specs=(out_spec,) * len(outs),
            scratch_shapes=list(scratch),
            input_output_aliases=aliases or {},
            compiler_params=params,
            cost_estimate=pl.CostEstimate(flops=flops, bytes_accessed=flops, transcendentals=0),
            name=name,
        )(*inputs)

    def like(v, dtype=f32):
        return pltpu.VMEM(v.shape, dtype)

    sources = (
        moment_weights.reshape(1, STEPS),
        adjoint_now,
        forward_now,
        adjoint_next,
        forward_next,
        signs,
        onsite,
        hop_right,
        hop_down,
    )
    sources = tuple(pltpu.with_memory_space_constraint(v, pltpu.HBM) for v in sources)
    strip_tile = pltpu.VMEM((rows, LANES), f32)
    x0, adj_next, fwd_next, sign, on, hr, hd, weights, packed = call(
        load_kernel,
        "load",
        sources,
        (
            pltpu.VMEM((groups, tiles, tall, LANES), f32),
            like(adjoint_next),
            like(forward_next),
            like(signs, jnp.int32),
            like(onsite),
            like(hop_right),
            like(hop_down),
            pltpu.VMEM((1, STEPS), f32),
            strip_tile,
        ),
        [pltpu.SemaphoreType.DMA((10 + 2 * tiles,))],
        in_spec=hbm,
    )
    x0 = x0.reshape(block.field_shape)
    left, right = both_sides(packed)

    x0, adj_next, fwd_next, sign, on, hr, hd, weights, packed = in_vmem(
        x0, adj_next, fwd_next, sign, on, hr, hd, weights, packed
    )
    message = pltpu.VMEM((3 * groups + TILE, cols), f32)
    both_messages = pltpu.VMEM((2, 3 * groups + TILE, cols), f32)
    field = pltpu.VMEM(block.field_shape, f32)
    hops_shape = pltpu.VMEM((4, tiles, tall, LANES), f32)
    forces_shape = pltpu.VMEM((3, rows, cols), f32)
    inputs = sources[3:6] + (weights, x0, adj_next, fwd_next, sign, on, hr, hd)
    next_shape = like(adjoint_next)
    x0, adj_next, fwd_next, sign, x1, x2, hops, forces, messages = call(
        first_kernel,
        "step_0",
        inputs,
        (field, next_shape, next_shape, like(sign, jnp.int32), field, field, hops_shape, forces_shape, both_messages),
        [pltpu.SemaphoreType.DMA((3,))],
        aliases={4 + i: i for i in range(4)},
        flops=COST,
        in_spec=[hbm] * 3 + [vmem] * 8,
    )
    (sign,) = in_vmem(sign)

    x0, x1, x2, hops, forces = in_vmem(x0, x1, x2, hops, forces)
    messages, left, right = in_vmem(messages, left, right)
    to_above, to_below = call(
        send_kernel, "edge_rows", (packed, left, right, messages), (message, message)
    )
    above = shifted(to_below, "strip", 1)
    below = shifted(to_above, "strip", -1)

    (sent,) = in_vmem(to_above)
    x1, x2, hops, forces, adj_out, fwd_out, strip, strip_base, strip_hops = call(
        inner_kernel,
        "inner_steps",
        (weights, x0, sign, packed, left, right, sent, x1, x2, hops, forces),
        (
            field,
            field,
            hops_shape,
            forces_shape,
            like(adjoint_now),
            like(forward_now),
            pltpu.VMEM((STEPS, tall, LANES), f32),
            pltpu.VMEM((2, rows, LANES), f32),
            pltpu.VMEM((3, tall, LANES), f32),
        ),
        aliases={7: 0, 8: 1, 9: 2, 10: 3},
        flops=COST,
    )

    kept = in_vmem(forces, adj_out, fwd_out)
    read = (x0,) + in_vmem(x1, x2, hops, strip, strip_hops, above, below)
    forces, adjoint_out, forward_out = call(
        outer_kernel,
        "outer_rows",
        read + kept,
        tuple(like(v) for v in kept),
        aliases={len(read) + i: i for i in range(len(kept))},
        flops=COST,
    )

    other = shifted(forces, "probe", 1)
    whole = jax.ShapeDtypeStruct(adjoint_now.shape, f32)
    adjoint_out, forward_out = call(
        store_kernel,
        "store",
        in_vmem(adjoint_out, forward_out),
        (whole, whole),
        [pltpu.SemaphoreType.DMA((2 * probes,))],
        flops=COST,
        out_spec=hbm,
    )
    plain = jax.ShapeDtypeStruct((rows, cols), f32)
    right_force, down_force, site_force = call(
        sum_kernel, "force_sums", in_vmem(forces, other), (plain, plain, plain)
    )
    return right_force, down_force, site_force, forward_out, adjoint_out


def solution(mesh):
    placed = (
        P(("parts", "probe"), "strip", "col"),
        P(("parts", "strip"), "col"),
        P(("parts", "strip"), "col"),
        P(("parts", "strip"), "col"),
        P(),
        P(("parts", "probe"), "strip", "col"),
        P(("parts", "probe"), "strip", "col"),
        P(("parts", "probe"), "strip", "col"),
        P(("parts", "probe"), "strip", "col"),
    )
    return jax.shard_map(
        local,
        mesh=mesh,
        in_specs=placed,
        out_specs=(
            P(("parts", "strip"), "col"),
            P(("parts", "strip"), "col"),
            P(("parts", "strip"), "col"),
            P(("parts", "probe"), "strip", "col"),
            P(("parts", "probe"), "strip", "col"),
        ),
        check_vma=False,
    )
```
